512 devices in a mesh: dp: 64 (over y, z), mp: 8 (over x, core).
Axes of the slice: x: 4, y: 8, z: 8, core: 2. Of those that a mesh axis runs over, the one named last changes fastest.
Arguments:
- features: bfloat16 [128, 1024, 512], P('mp', 'dp'), may hold values from -6 to 6
- conv_weight: bfloat16 [2, 512, 512], replicated, may hold values from -0.1875 to 0.1875
- proj_weight: bfloat16 [512, 1280], replicated, may hold values from -0.25 to 0.25
- pos_weight: bfloat16 [128, 16, 80, 80], P('dp', 'mp'), may hold values from -0.0625 to 0.0625
- utt_len: int32 [128], replicated, may hold values from 5120 to 158720, as said below
- pack_order: int32 [128], replicated, may hold values from 0 to 127, as said below
Outputs:
- hidden: bfloat16 [32768, 1280], P('dp', 'mp')
The draws below stay inside these ranges and needn't reach their ends.
Inputs may be any that keep to these rules, and one draw needn't show every extreme that they name: `utt_len`: each a multiple of 320. The two utterances pack_order[2 o] and pack_order[2 o + 1] together span at most 512 frames. `pack_order`: A permutation of the utterances.
All inputs are finite; a program needn't handle non-finite values.
Results may differ from the reference program's by a relative error of at most 0.0066.
Values may be sent and summed in bfloat16 or wider, within the bound.
No kernel may reach another device: no remote copies, remote signals or barrier semaphores. Data moves between devices by JAX's collectives and lax.ppermute only.
A program may use at most 128 MiB of HBM per device.

```python
import jax
import jax.numpy as jnp
from jax import lax

C_EXT = 512
D = 1280
KPOS = 128
GROUPS = 16
HOP = 320
GW = 80
TMAX = 512
B = 128


def pair_lengths(key):
    owners = B // 2
    utt_order = jax.random.permutation(jax.random.fold_in(key, 11), B).astype(jnp.int32)
    first_frames = jax.random.randint(jax.random.fold_in(key, 12), (owners,), TMAX // 2, TMAX - 15)
    chosen = jax.random.randint(jax.random.fold_in(key, 14), (), 0, owners)
    marker = jnp.arange(owners) == chosen
    first_frames = jnp.where(marker, TMAX - 16, first_frames)
    second_frames = jax.random.randint(jax.random.fold_in(key, 13), (owners,), 16, TMAX - first_frames + 1)
    lengths = jnp.zeros((B,), jnp.int32)
    lengths = lengths.at[utt_order[0::2]].set(first_frames * HOP)
    lengths = lengths.at[utt_order[1::2]].set(second_frames * HOP)
    return (utt_order, lengths.astype(jnp.int32))


def draw_utt_len(key, part):
    utt_order, lengths = pair_lengths(key)
    return lengths


def draw_pack_order(key, part):
    utt_order, lengths = pair_lengths(key)
    return utt_order


def steps_of(own_key, shape, shards, smallest, high):
    level, own = 1.0, jax.random.fold_in(own_key, 6)
    for dim, parts in shards:
        steps = jnp.exp(jax.random.uniform(jax.random.fold_in(own, dim), (parts,), jnp.float32, smallest / len(shards), high / len(shards)))
        level = level * jnp.repeat(steps, shape[dim] // parts).reshape([-1 if axis == dim else 1 for axis in range(len(shape))])
    return level


def scatter_about(stream_key, dims, width, bound, shards=(), kind=jnp.bfloat16):
    result = width * jax.random.normal(stream_key, dims, jnp.float32)
    if shards:
        result = result * steps_of(stream_key, dims, shards, -0.22, 0.18)
    return jnp.clip(result, -bound, bound).astype(kind)


def setup_inputs(seed: int = 0) -> dict:
    key_of = jax.random.split(jax.random.key(seed), 7)
    return {
        "features": scatter_about(key_of[0], (B, 2 * TMAX, C_EXT), 1.0, 6.0, ((0, 8), (1, 64))),
        "conv_weight": scatter_about(key_of[1], (2, C_EXT, C_EXT), (2 * C_EXT) ** -0.5, 0.1875),
        "proj_weight": scatter_about(key_of[2], (C_EXT, D), C_EXT ** -0.5, 0.25),
        "pos_weight": scatter_about(key_of[3], (KPOS, GROUPS, GW, GW), (KPOS * GW) ** -0.5, 0.0625, ((0, 64), (1, 8))),
        "utt_len": draw_utt_len(jax.random.fold_in(key_of[6], 71), 0),
        "pack_order": draw_pack_order(jax.random.fold_in(key_of[6], 71), 0),
    }


EPS = 1e-05

def layer_norm(values):
    average = lax.optimization_barrier(jnp.mean(values, axis=-1, keepdims=True))
    centred = values - average
    variance = lax.optimization_barrier(jnp.mean(centred * centred, axis=-1, keepdims=True))
    return centred * lax.rsqrt(variance + EPS)

def pack_pair(first_rows, second_rows, first_len, second_len):
    total = first_rows.shape[0]
    position = jnp.arange(total, dtype=jnp.int32)
    doubled = jnp.concatenate([jnp.zeros_like(second_rows), second_rows], axis=0)
    moved = lax.dynamic_slice_in_dim(doubled, (total - first_len).astype(jnp.int32), total, 0)
    in_first = position < first_len
    in_second = jnp.logical_and(position >= first_len, position < first_len + second_len)
    blank = jnp.zeros_like(first_rows)
    packed = jnp.where(in_first[:, None], first_rows, jnp.where(in_second[:, None], moved, blank))
    segments = jnp.where(in_first, 0, jnp.where(in_second, 1, 2)).astype(jnp.int32)
    return (packed, segments)

def positional(packed, segments, weights):
    total = packed.shape[0]
    kernel = weights.shape[0]
    half = kernel // 2
    groups = weights.shape[1]
    group_width = weights.shape[2]
    rows = packed.astype(jnp.float32).reshape(total, groups, group_width)
    padded_rows = jnp.pad(rows, ((half, half), (0, 0), (0, 0)))
    padded_segments = jnp.pad(segments, (half, half), constant_values=-1)
    weights_wide = weights.astype(jnp.float32)

    def add_tap(tap, running):
        tap_index = jnp.asarray(tap).astype(jnp.int32)
        shifted = lax.dynamic_slice_in_dim(padded_rows, tap_index, total, 0)
        same = (lax.dynamic_slice_in_dim(padded_segments, tap_index, total, 0) == segments).astype(jnp.float32)
        tap_matrix = lax.dynamic_index_in_dim(weights_wide, tap_index, 0, keepdims=False)
        return running + jnp.einsum('tgc,gcd->tgd', shifted * same[:, None, None], tap_matrix)
    conv_sum = lax.fori_loop(0, kernel, add_tap, jnp.zeros((total, groups, group_width), jnp.float32))
    hidden = rows + jax.nn.gelu(conv_sum, approximate=False)
    return hidden.astype(jnp.bfloat16).reshape(total, groups * group_width)

def reference(features, conv_weight, proj_weight, pos_weight, utt_len, pack_order):
    conv_matrix = conv_weight.reshape(2 * C_EXT, C_EXT)

    def extract(single):
        pairs = single.reshape(TMAX, 2 * C_EXT)
        conv_out = jnp.dot(pairs, conv_matrix, preferred_element_type=jnp.float32)
        frames = jax.nn.gelu(layer_norm(conv_out), approximate=False).astype(jnp.bfloat16)
        frames = lax.optimization_barrier(frames)
        normed = layer_norm(frames.astype(jnp.float32)).astype(jnp.bfloat16)
        return jnp.dot(normed, proj_weight, preferred_element_type=jnp.float32).astype(jnp.bfloat16)
    projected = lax.map(extract, features)

    def one_owner(position):
        first_utt = pack_order[2 * position]
        second_utt = pack_order[2 * position + 1]
        packed, segments = pack_pair(projected[first_utt], projected[second_utt], utt_len[first_utt] // HOP, utt_len[second_utt] // HOP)
        return positional(packed, segments, pos_weight)
    hidden = lax.map(one_owner, jnp.arange(B // 2, dtype=jnp.int32))
    return hidden.reshape(B // 2 * TMAX, D)
```

```python
import functools

import jax
import jax.numpy as jnp
from jax import lax
from jax.experimental import pallas as pl
from jax.experimental.pallas import tpu as pltpu
from jax.sharding import PartitionSpec as P

HOP = 320
EPS = 1e-05
LANES = 128
TAP_ROWS = 208
GAP = 64
STEP = 16


def iota(shape, dim):
    return lax.broadcasted_iota(jnp.int32, shape, dim)


def one_hot(condition):
    return jnp.where(condition, 1.0, 0.0).astype(jnp.bfloat16)


def dot(a, b, contract=((1,), (0,))):
    return lax.dot_general(a, b, (contract, ((), ())), preferred_element_type=jnp.float32)


def layer_norm(values):
    average = jnp.mean(values, axis=-1, keepdims=True)
    centred = values - average
    variance = jnp.mean(centred * centred, axis=-1, keepdims=True)
    return centred * lax.rsqrt(variance + EPS)


def gelu(values):
    return 0.5 * values * (1.0 + lax.erf(values * (0.5**0.5)))


def pack_taps_kernel(taps_ref, out_ref):
    wide = jnp.concatenate([taps_ref[0, 0], taps_ref[1, 0], taps_ref[0, 1], taps_ref[1, 1]], axis=1)
    out_ref[0:80, :] = wide[:, 0:128]
    out_ref[80:160, :] = wide[:, 128:256]
    rest = wide[:, 256:320]
    lower = jnp.concatenate([rest[48:80], rest[0:16]], axis=0)
    out_ref[160:208, :] = jnp.concatenate([rest[0:48], lower], axis=1)


def front_kernel(utts, frames, parts, features_ref, conv_ref, proj_ref, out_ref):
    rows = utts * frames
    features = features_ref[...]
    row = iota((rows, 2 * rows), 0)
    column = iota((rows, 2 * rows), 1)
    source = (row % utts) * (2 * frames) + 2 * (row // utts)
    first = dot(one_hot(column == source), features).astype(jnp.bfloat16)
    second = dot(one_hot(column == source + 1), features).astype(jnp.bfloat16)
    conv_out = dot(first, conv_ref[0]) + dot(second, conv_ref[1])
    hidden = gelu(layer_norm(conv_out)).astype(jnp.bfloat16)
    normed = layer_norm(hidden.astype(jnp.float32)).astype(jnp.bfloat16)
    projected = dot(normed, proj_ref[...]).astype(jnp.bfloat16)
    width = projected.shape[1] // parts
    for part in range(parts):
        pieces = [
            projected[f * utts : (f + 1) * utts, part * width : (part + 1) * width] for f in range(frames)
        ]
        out_ref[part] = jnp.concatenate(pieces, axis=1)


def order_kernel(order_ref, spread_ref, out_ref):
    utts, lanes = spread_ref.shape
    rows, width = out_ref.shape
    quarters = lanes // width
    chosen = one_hot(iota((utts, utts), 0) == order_ref[...])
    ordered = dot(chosen, spread_ref[...], ((0,), (0,))).astype(jnp.bfloat16)
    slot = iota((rows, utts), 0) // quarters
    quarter = iota((rows, utts), 0) % quarters
    same = slot == iota((rows, utts), 1)
    total = None
    for q in range(quarters):
        term = dot(one_hot(same & (quarter == q)), ordered[:, q * width : (q + 1) * width])
        total = term if total is None else total + term
    out_ref[...] = total.astype(out_ref.dtype)


def positional_kernel(total, half, blocks, owner_ref, order_ref, len_ref, rows_ref, taps_hbm, out_ref, taps, placed, shifted, sums, sem):
    copy = pltpu.make_async_copy(taps_hbm, taps, sem)
    copy.start()
    owner = owner_ref[0]
    first_len = len_ref[order_ref[2 * owner]] // HOP
    second_len = len_ref[order_ref[2 * owner + 1]] // HOP

    width = out_ref.shape[0]
    group = width // 2
    spots = placed.shape[0]
    columns = rows_ref.shape[0]
    column = iota((1, columns), 1)
    slot = (column // 4) % 2
    spot = iota((spots, columns), 0)
    acc = None
    for parity in range(2):
        frame = (column // 8) * 8 + (column % 4) * 2 + parity
        target = jnp.where(slot == 0, frame, frame + first_len + GAP) + half
        valid = frame < jnp.where(slot == 0, first_len, second_len)
        target = jnp.where(valid, target, -1)
        term = dot(one_hot(spot == target), rows_ref[:, parity * width : (parity + 1) * width])
        acc = term if acc is None else acc + term
    placed[...] = acc

    length = shifted.shape[1]
    for g in range(2):
        lanes = slice(g * group, (g + 1) * group)
        for third in range(3):
            pairs = [k for k in range(3 * third, 3 * third + 3) if k < 8]
            pieces = [placed[2 * k : 2 * k + length, lanes].astype(jnp.bfloat16) for k in pairs]
            pieces.append(jnp.zeros((length, 256 - group * len(pairs)), jnp.bfloat16))
            shifted[g, :, third * 256 : (third + 1) * 256] = jnp.concatenate(pieces, axis=1)
    sums[...] = jnp.zeros_like(sums)
    copy.wait()

    reach = sums.shape[1]

    def add_block(block, carry):
        start = pl.multiple_of(block * STEP, STEP)

        def piece(pair, tile, size):
            base = pl.multiple_of((block * 8 + pair) * TAP_ROWS, 16)
            if tile < 2:
                return taps[pl.ds(base + 80 * tile, size), :]
            tail = taps[pl.ds(base + 160, 48), :]
            low = jnp.concatenate([tail, jnp.roll(tail, 64, axis=1)], axis=0)
            return low[:size]

        matrices = []
        for tile in range(3):
            parts = []
            for third in range(3):
                pairs = [min(k, 7) for k in range(3 * third, 3 * third + 3)]
                parts += [piece(pairs[0], tile, 80), piece(pairs[1], tile, 80), piece(pairs[2], tile, 96)]
            matrices.append(jnp.concatenate(parts, axis=0))
        for g in range(2):
            right = jnp.concatenate([matrices[g], matrices[g + 1]], axis=1)
            sums[g] += dot(shifted[g, pl.ds(start, reach), :], right)
        return carry

    lax.fori_loop(0, blocks, add_block, 0)

    spot = iota((total, 1), 0)
    in_first = spot < first_len
    inside = spot < first_len + second_len
    result = []
    for g in range(2):
        offset = 32 * g
        even = slice(offset, offset + group)
        odd = slice(offset + group, offset + 2 * group)
        near = sums[g, 0:total, even] + sums[g, 1 : total + 1, odd]
        far = sums[g, GAP : GAP + total, even] + sums[g, GAP + 1 : GAP + total + 1, odd]
        result.append(jnp.where(inside, jnp.where(in_first, near, far), 0.0))
    conv_sum = jnp.concatenate(result, axis=1)
    packed = jnp.where(in_first, placed[half : half + total, :], placed[half + GAP : half + GAP + total, :])
    hidden = packed + gelu(conv_sum)
    hidden = jnp.concatenate([hidden, jnp.zeros((total, -width % LANES), jnp.float32)], axis=1)
    out_ref[...] = hidden.T[:width].astype(out_ref.dtype)


VMEM = pl.BlockSpec(memory_space=pltpu.VMEM)
SMEM = pl.BlockSpec(memory_space=pltpu.SMEM)


def shards(features, conv_weight, proj_weight, pos_weight, utt_len, pack_order):
    owner = lax.axis_index("dp").reshape(1)
    owners = lax.axis_size("dp")
    parts = lax.axis_size("mp")
    utts, slice_rows, channels = features.shape
    frames = slice_rows // 2
    model_width = proj_weight.shape[1]
    width = model_width // parts
    total = frames * owners
    half = pos_weight.shape[0] * owners // 2
    params = pltpu.CompilerParams(vmem_limit_bytes=48 * 1024 * 1024)

    packed_taps = pl.pallas_call(
        pack_taps_kernel,
        out_shape=jax.ShapeDtypeStruct((TAP_ROWS, LANES), jnp.bfloat16),
        in_specs=[VMEM],
        out_specs=VMEM,
        compiler_params=params,
    )(pos_weight)
    taps = lax.all_gather(packed_taps, "dp", axis=0, tiled=True)

    sent = pl.pallas_call(
        functools.partial(front_kernel, utts, frames, parts),
        out_shape=jax.ShapeDtypeStruct((parts, utts, frames * width), jnp.bfloat16),
        in_specs=[VMEM] * 3,
        out_specs=VMEM,
        compiler_params=params,
    )(features.reshape(utts * slice_rows, channels), conv_weight, proj_weight)
    spread = lax.all_to_all(sent, "mp", split_axis=0, concat_axis=0, tiled=True)

    ordered = pl.pallas_call(
        order_kernel,
        out_shape=jax.ShapeDtypeStruct((owners * 8, 2 * width), jnp.bfloat16),
        in_specs=[VMEM] * 2,
        out_specs=VMEM,
        compiler_params=params,
    )(pack_order.reshape(1, -1), spread.reshape(parts * utts, frames * width))
    pair_rows = lax.all_to_all(
        ordered.reshape(owners, 8, 2 * width), "dp", split_axis=0, concat_axis=0, tiled=True
    )

    blocks = 2 * half // STEP
    reach = total + GAP + 16
    length = reach + 2 * half - STEP
    hidden = pl.pallas_call(
        functools.partial(positional_kernel, total, half, blocks),
        out_shape=jax.ShapeDtypeStruct((width, total), jnp.bfloat16),
        in_specs=[SMEM, SMEM, SMEM, VMEM, pl.BlockSpec(memory_space=pl.ANY)],
        out_specs=VMEM,
        scratch_shapes=[
            pltpu.VMEM((owners * TAP_ROWS, LANES), jnp.bfloat16),
            pltpu.VMEM((length + STEP, width), jnp.float32),
            pltpu.VMEM((2, length, 768), jnp.bfloat16),
            pltpu.VMEM((2, reach, 256), jnp.float32),
            pltpu.SemaphoreType.DMA,
        ],
        compiler_params=pltpu.CompilerParams(vmem_limit_bytes=62 * 1024 * 1024),
    )(owner, pack_order, utt_len, pair_rows.reshape(owners * 8, 2 * width), taps)
    return hidden.T


def solution(mesh):
    in_specs = (P("mp", "dp", None), P(), P(), P("dp", "mp", None, None), P(), P())
    out_specs = P("dp", "mp")
    return jax.shard_map(shards, mesh=mesh, in_specs=in_specs, out_specs=out_specs, check_vma=False)
```

```python
import functools

import jax
import jax.numpy as jnp
from jax import lax
from jax.experimental import pallas as pl
from jax.experimental.pallas import tpu as pltpu
from jax.sharding import PartitionSpec as P

HOP = 320
EPS = 1e-05
LANES = 128
TAP_ROWS = 112
GAP = 64
STEP = 16


def iota(shape, dim):
    return lax.broadcasted_iota(jnp.int32, shape, dim)


def one_hot(condition):
    return jnp.where(condition, 1.0, 0.0).astype(jnp.bfloat16)


def dot(a, b, contract=((1,), (0,))):
    return lax.dot_general(a, b, (contract, ((), ())), preferred_element_type=jnp.float32)


def layer_norm(values):
    average = jnp.mean(values, axis=-1, keepdims=True)
    centred = values - average
    variance = jnp.mean(centred * centred, axis=-1, keepdims=True)
    return centred * lax.rsqrt(variance + EPS)


def gelu(values):
    return 0.5 * values * (1.0 + lax.erf(values * (0.5**0.5)))


def pack_taps_kernel(taps_ref, *out_refs):
    for g, out_ref in enumerate(out_refs):
        out_ref[0:80, :] = jnp.concatenate([taps_ref[0, g], taps_ref[1, g, :, 0:48]], axis=1)
        rest = taps_ref[1, g, :, 48:80]
        out_ref[80:96, :] = jnp.concatenate([rest[16 * r : 16 * r + 16] for r in range(4)], axis=1)
        out_ref[96:112, :] = jnp.concatenate([rest[64:80], jnp.zeros((16, 96), rest.dtype)], axis=1)


def stack_kernel(*refs):
    pieces, outs = refs[:-2], refs[-2:]
    per_group = len(pieces) // 2
    for n, piece in enumerate(pieces):
        outs[n // per_group][TAP_ROWS * (n % per_group) : TAP_ROWS * (n % per_group + 1), :] = piece[...]


def front_kernel(utts, frames, parts, features_hbm, conv_hbm, proj_hbm, out_ref, features_ref, conv_ref, proj_ref, sems):
    copies = [
        pltpu.make_async_copy(source, target, sems.at[n])
        for n, (source, target) in enumerate(
            [(features_hbm, features_ref), (conv_hbm, conv_ref), (proj_hbm, proj_ref)]
        )
    ]
    for copy in copies:
        copy.start()
    rows = utts * frames
    copies[0].wait()
    features = features_ref[...]
    row = iota((rows, 2 * rows), 0)
    column = iota((rows, 2 * rows), 1)
    source = (row % utts) * (2 * frames) + 2 * (row // utts)
    first = dot(one_hot(column == source), features).astype(jnp.bfloat16)
    second = dot(one_hot(column == source + 1), features).astype(jnp.bfloat16)
    copies[1].wait()
    conv_out = dot(first, conv_ref[0]) + dot(second, conv_ref[1])
    hidden = gelu(layer_norm(conv_out)).astype(jnp.bfloat16)
    normed = layer_norm(hidden.astype(jnp.float32)).astype(jnp.bfloat16)
    copies[2].wait()
    projected = dot(normed, proj_ref[...]).astype(jnp.bfloat16)
    width = projected.shape[1] // parts
    for part in range(parts):
        pieces = [
            projected[f * utts : (f + 1) * utts, part * width : (part + 1) * width] for f in range(frames)
        ]
        out_ref[part] = jnp.concatenate(pieces, axis=1)


def order_kernel(order_ref, spread_ref, out_ref):
    utts, lanes = spread_ref.shape
    rows, width = out_ref.shape
    quarters = lanes // width
    chosen = one_hot(iota((utts, utts), 0) == order_ref[...])
    ordered = dot(chosen, spread_ref[...], ((0,), (0,))).astype(jnp.bfloat16)
    slot = iota((rows, utts), 0) // quarters
    quarter = iota((rows, utts), 0) % quarters
    same = slot == iota((rows, utts), 1)
    total = None
    for q in range(quarters):
        term = dot(one_hot(same & (quarter == q)), ordered[:, q * width : (q + 1) * width])
        total = term if total is None else total + term
    out_ref[...] = total.astype(out_ref.dtype)


def positional_kernel(
    total, half, ring, where_ref, order_ref, len_ref, rows_ref, *refs
):
    pieces_hbm, (out_ref, taps, placed, shifted, sums, sems) = refs[:-6], refs[-6:]
    per_group = len(pieces_hbm) // 2
    copies = []
    for g in range(2):
        offset = 0
        for n in range(per_group):
            source = pieces_hbm[g * per_group + n]
            target = taps.at[g, pl.ds(offset, source.shape[0]), :]
            copies.append(pltpu.make_async_copy(source, target, sems.at[len(copies)]))
            copies[-1].start()
            offset += source.shape[0]
    here_y, here_z = where_ref[0], where_ref[1]
    owner = here_y * ring + here_z
    first_len = len_ref[order_ref[2 * owner]] // HOP
    second_len = len_ref[order_ref[2 * owner + 1]] // HOP

    width = out_ref.shape[0]
    group = width // 2
    spots = placed.shape[0]
    columns = rows_ref.shape[0]
    column = iota((1, columns), 1)
    slot = (column // 4) % 2
    spot = iota((spots, columns), 0)
    acc = None
    for parity in range(2):
        frame = (column // 8) * 8 + (column % 4) * 2 + parity
        target = jnp.where(slot == 0, frame, frame + first_len + GAP) + half
        valid = frame < jnp.where(slot == 0, first_len, second_len)
        target = jnp.where(valid, target, -1)
        term = dot(one_hot(spot == target), rows_ref[:, parity * width : (parity + 1) * width])
        acc = term if acc is None else acc + term
    placed[...] = acc

    length = shifted.shape[1]
    for g in range(2):
        lanes = slice(g * group, (g + 1) * group)
        for third in range(3):
            pairs = [k for k in range(3 * third, 3 * third + 3) if k < 8]
            pieces = [placed[2 * k : 2 * k + length, lanes].astype(jnp.bfloat16) for k in pairs]
            pieces.append(jnp.zeros((length, 256 - group * len(pairs)), jnp.bfloat16))
            shifted[g, :, third * 256 : (third + 1) * 256] = jnp.concatenate(pieces, axis=1)
    sums[...] = jnp.zeros_like(sums)
    for copy in copies:
        copy.wait()

    reach = sums.shape[1]

    def add_block(block, carry):
        start = pl.multiple_of(block * STEP, STEP)
        away_y = lax.rem(here_y + ring - block, ring)
        for g in range(2):
            left, right = [], []
            for slot in range(9):
                pair = min(slot, 7)
                away_z = lax.rem(here_z + ring - pair, ring)
                first, second = (away_y, away_z) if g == 0 else (away_z, away_y)
                base = pl.multiple_of((first * ring + second) * TAP_ROWS, 16)
                size = 96 if slot % 3 == 2 else 80
                left.append(taps[g, pl.ds(base, size), :])
                fold = taps[g, pl.ds(base + 80, 16), :]
                right += [fold] + [jnp.roll(fold, -32 * r, axis=1) for r in range(1, 4)]
                right.append(taps[g, pl.ds(base + 96, 16), :])
                if size == 96:
                    right.append(fold)
            matrix = jnp.concatenate([jnp.concatenate(left, axis=0), jnp.concatenate(right, axis=0)], axis=1)
            sums[g] += dot(shifted[g, pl.ds(start, reach), :], matrix)
        return carry

    lax.fori_loop(0, 2 * half // STEP, add_block, 0)

    spot = iota((total, 1), 0)
    in_first = spot < first_len
    inside = spot < first_len + second_len
    result = []
    for g in range(2):
        even, odd = slice(0, group), slice(group, 2 * group)
        near = sums[g, 0:total, even] + sums[g, 1 : total + 1, odd]
        far = sums[g, GAP : GAP + total, even] + sums[g, GAP + 1 : GAP + total + 1, odd]
        result.append(jnp.where(inside, jnp.where(in_first, near, far), 0.0))
    conv_sum = jnp.concatenate(result, axis=1)
    packed = jnp.where(in_first, placed[half : half + total, :], placed[half + GAP : half + GAP + total, :])
    hidden = packed + gelu(conv_sum)
    hidden = jnp.concatenate([hidden, jnp.zeros((total, -width % LANES), jnp.float32)], axis=1)
    out_ref[...] = hidden.T[:width].astype(out_ref.dtype)


VMEM = pl.BlockSpec(memory_space=pltpu.VMEM)
SMEM = pl.BlockSpec(memory_space=pltpu.SMEM)
ANY = pl.BlockSpec(memory_space=pl.ANY)


def send(values, ring, axis, step):
    pairs = []
    for y in range(ring):
        for z in range(ring):
            to = ((y + step) % ring, z) if axis == 0 else (y, (z + step) % ring)
            pairs.append((y * ring + z, to[0] * ring + to[1]))
    return lax.ppermute(values, "dp", pairs)


def near_taps(own, ring, axis):
    return [own] + [send(own, ring, axis, step) for step in range(1, ring)]


def first_round(block, ring, axis):
    return [send(block, ring, axis, step) for step in (1, 2, -2, -1)]


def second_round(received, ring, axis):
    one, two, minus_two, minus_one = received
    middle = two.shape[0] // 2
    three = send(two, ring, axis, 1)
    low = send(two[:middle], ring, axis, 2)
    high = send(minus_two[middle:], ring, axis, -2)
    minus_three = send(minus_two, ring, axis, -1)
    return [one, two, three, low, high, minus_three, minus_two, minus_one]


def shards(features, conv_weight, proj_weight, pos_weight, utt_len, pack_order):
    owners = lax.axis_size("dp")
    parts = lax.axis_size("mp")
    utts, slice_rows, channels = features.shape
    frames = slice_rows // 2
    model_width = proj_weight.shape[1]
    width = model_width // parts
    total = frames * owners
    half = pos_weight.shape[0] * owners // 2
    params = pltpu.CompilerParams(vmem_limit_bytes=48 * 1024 * 1024)
    large = pltpu.CompilerParams(vmem_limit_bytes=62 * 1024 * 1024)

    ring = round(owners**0.5)
    where = jnp.stack([lax.axis_index("dp") // ring, lax.axis_index("dp") % ring]).astype(jnp.int32)
    packed_taps = pl.pallas_call(
        pack_taps_kernel,
        out_shape=[jax.ShapeDtypeStruct((TAP_ROWS, LANES), jnp.bfloat16)] * 2,
        in_specs=[VMEM],
        out_specs=[VMEM] * 2,
        compiler_params=params,
    )(pos_weight)
    near = near_taps(packed_taps[0], ring, 1) + near_taps(packed_taps[1], ring, 0)

    sent = pl.pallas_call(
        functools.partial(front_kernel, utts, frames, parts),
        out_shape=jax.ShapeDtypeStruct((parts, utts, frames * width), jnp.bfloat16),
        in_specs=[ANY] * 3,
        out_specs=VMEM,
        scratch_shapes=[
            pltpu.VMEM((utts * slice_rows, channels), jnp.bfloat16),
            pltpu.VMEM(conv_weight.shape, jnp.bfloat16),
            pltpu.VMEM(proj_weight.shape, jnp.bfloat16),
            pltpu.SemaphoreType.DMA((3,)),
        ],
        compiler_params=large,
    )(features.reshape(utts * slice_rows, channels), conv_weight, proj_weight)
    *near, sent = lax.optimization_barrier((*near, sent))
    blocks = pl.pallas_call(
        stack_kernel,
        out_shape=[jax.ShapeDtypeStruct((ring * TAP_ROWS, LANES), jnp.bfloat16)] * 2,
        in_specs=[VMEM] * len(near),
        out_specs=[VMEM] * 2,
        compiler_params=params,
    )(*near)
    *blocks, sent = lax.optimization_barrier((*blocks, sent))
    received = [first_round(blocks[g], ring, g) for g in range(2)]
    spread = lax.all_to_all(sent, "mp", split_axis=0, concat_axis=0, tiled=True)

    ordered = pl.pallas_call(
        order_kernel,
        out_shape=jax.ShapeDtypeStruct((owners * 8, 2 * width), jnp.bfloat16),
        in_specs=[VMEM] * 2,
        out_specs=VMEM,
        compiler_params=params,
    )(pack_order.reshape(1, -1), spread.reshape(parts * utts, frames * width))
    received, ordered = lax.optimization_barrier((received, ordered))
    taps = []
    for g in range(2):
        taps += [blocks[g]] + second_round(received[g], ring, g)
    pair_rows = lax.all_to_all(
        ordered.reshape(owners, 8, 2 * width), "dp", split_axis=0, concat_axis=0, tiled=True
    )

    reach = total + GAP + 16
    length = reach + 2 * half - STEP
    hidden = pl.pallas_call(
        functools.partial(positional_kernel, total, half, ring),
        out_shape=jax.ShapeDtypeStruct((width, total), jnp.bfloat16),
        in_specs=[SMEM, SMEM, SMEM, VMEM] + [ANY] * len(taps),
        out_specs=VMEM,
        scratch_shapes=[
            pltpu.VMEM((2, owners * TAP_ROWS, LANES), jnp.bfloat16),
            pltpu.VMEM((length + STEP, width), jnp.float32),
            pltpu.VMEM((2, length, 768), jnp.bfloat16),
            pltpu.VMEM((2, reach, 256), jnp.float32),
            pltpu.SemaphoreType.DMA((len(taps),)),
        ],
        compiler_params=large,
    )(where, pack_order, utt_len, pair_rows.reshape(owners * 8, 2 * width), *taps)
    return hidden.T


def solution(mesh):
    in_specs = (P("mp", "dp", None), P(), P(), P("dp", "mp", None, None), P(), P())
    out_specs = P("dp", "mp")
    return jax.shard_map(shards, mesh=mesh, in_specs=in_specs, out_specs=out_specs, check_vma=False)
```

```python
import functools

import jax
import jax.numpy as jnp
from jax import lax
from jax.experimental import pallas as pl
from jax.experimental.pallas import tpu as pltpu
from jax.sharding import PartitionSpec as P

HOP = 320
EPS = 1e-05
LANES = 128
TAP_ROWS = 112
GAP = 64
STEP = 16


def iota(shape, dim):
    return lax.broadcasted_iota(jnp.int32, shape, dim)


def one_hot(condition):
    return jnp.where(condition, 1.0, 0.0).astype(jnp.bfloat16)


def dot(a, b, contract=((1,), (0,))):
    return lax.dot_general(a, b, (contract, ((), ())), preferred_element_type=jnp.float32)


def layer_norm(values):
    average = jnp.mean(values, axis=-1, keepdims=True)
    centred = values - average
    variance = jnp.mean(centred * centred, axis=-1, keepdims=True)
    return centred * lax.rsqrt(variance + EPS)


def gelu(values):
    return 0.5 * values * (1.0 + lax.erf(values * (0.5**0.5)))


def pack_taps_kernel(taps_ref, out_ref):
    packed = []
    for g in range(2):
        rest = taps_ref[1, g, :, 48:80]
        packed.append(
            jnp.concatenate(
                [
                    jnp.concatenate([taps_ref[0, g], taps_ref[1, g, :, 0:48]], axis=1),
                    jnp.concatenate([rest[16 * r : 16 * r + 16] for r in range(4)], axis=1),
                    jnp.concatenate([rest[64:80], jnp.zeros((16, 96), rest.dtype)], axis=1),
                ],
                axis=0,
            )
        )
    for device in range(out_ref.shape[0]):
        out_ref[device] = packed[device % 2]


def front_kernel(utts, frames, parts, features_hbm, conv_hbm, proj_hbm, out_ref, features_ref, conv_ref, proj_ref, sems):
    copies = [
        pltpu.make_async_copy(source, target, sems.at[n])
        for n, (source, target) in enumerate(
            [(features_hbm, features_ref), (conv_hbm, conv_ref), (proj_hbm, proj_ref)]
        )
    ]
    for copy in copies:
        copy.start()
    rows = utts * frames
    copies[0].wait()
    features = features_ref[...]
    row = iota((rows, 2 * rows), 0)
    column = iota((rows, 2 * rows), 1)
    source = (row % utts) * (2 * frames) + 2 * (row // utts)
    first = dot(one_hot(column == source), features).astype(jnp.bfloat16)
    second = dot(one_hot(column == source + 1), features).astype(jnp.bfloat16)
    copies[1].wait()
    conv_out = dot(first, conv_ref[0]) + dot(second, conv_ref[1])
    hidden = gelu(layer_norm(conv_out)).astype(jnp.bfloat16)
    normed = layer_norm(hidden.astype(jnp.float32)).astype(jnp.bfloat16)
    copies[2].wait()
    projected = dot(normed, proj_ref[...]).astype(jnp.bfloat16)
    group = projected.shape[1] // (2 * parts)
    for part in range(parts):
        pieces = [
            projected[f * utts : (f + 1) * utts, (2 * part + g) * group : (2 * part + g + 1) * group]
            for g in range(2)
            for f in range(frames)
        ]
        out_ref[part] = jnp.concatenate(pieces, axis=1)


def order_kernel(order_ref, spread_ref, out_ref):
    utts, lanes = spread_ref.shape
    rows, width = out_ref.shape
    width //= 2
    chosen = one_hot(iota((utts, utts), 0) == order_ref[...])
    ordered = dot(chosen, spread_ref[...], ((0,), (0,))).astype(jnp.bfloat16)
    row = iota((rows, utts), 0)
    eighth = (row // 8) % 2 * 4 + row % 4
    slot = row // 16 * 4 + row // 4 % 2
    for which in range(2):
        same = slot + 2 * which == iota((rows, utts), 1)
        total = None
        for e in range(0, lanes // width, 2):
            left = jnp.concatenate([one_hot(same & (eighth == e + n)) for n in range(2)], axis=1)
            right = [ordered[:, (e + n) * width : (e + n + 1) * width] for n in range(2)]
            term = dot(left, jnp.concatenate(right, axis=0))
            total = term if total is None else total + term
        out_ref[:, which * width : (which + 1) * width] = total.astype(out_ref.dtype)


def positional_kernel(
    total, half, owner_ref, order_ref, len_ref, rows_ref, taps_hbm, own_ref, other_ref, taps, placed, shifted, sums, both, sem
):
    copy = pltpu.make_async_copy(taps_hbm, taps, sem)
    copy.start()
    parity = owner_ref[0] % 2
    pair = owner_ref[0] - parity
    lengths = []
    for which in range(2):
        slot = 2 * (pair + which)
        lengths.append([len_ref[order_ref[slot + n]] // HOP for n in range(2)])

    group = own_ref.shape[0]
    spots = placed.shape[1]
    columns = rows_ref.shape[0]
    column = iota((1, columns), 1)
    is_first = (column // 4) % 2 == 0
    spot = iota((spots, columns), 0)
    for which in range(2):
        first_len, second_len = lengths[which]
        acc = None
        for odd in range(2):
            frame = (column // 8) * 8 + (column % 4) * 2 + odd
            target = jnp.where(is_first, frame, frame + first_len + GAP) + half
            valid = frame < jnp.where(is_first, first_len, second_len)
            target = jnp.where(valid, target, -1)
            lane = (2 * which + odd) * group
            term = dot(one_hot(spot == target), rows_ref[:, lane : lane + group])
            acc = term if acc is None else acc + term
        placed[which] = acc

    length = shifted.shape[1]
    for which in range(2):
        for third in range(3):
            pairs = [k for k in range(3 * third, 3 * third + 3) if k < 8]
            pieces = [placed[which, 2 * k : 2 * k + length, :].astype(jnp.bfloat16) for k in pairs]
            pieces.append(jnp.zeros((length, 256 - group * len(pairs)), jnp.bfloat16))
            shifted[which, :, third * 256 : (third + 1) * 256] = jnp.concatenate(pieces, axis=1)
    sums[...] = jnp.zeros_like(sums)
    copy.wait()

    reach = sums.shape[0] // 2

    def add_block(block, carry):
        start = pl.multiple_of(block * STEP, STEP)
        left, right = [], []
        for slot in range(9):
            piece = block * 8 + min(slot, 7)
            size = 96 if slot % 3 == 2 else 80
            left.append(taps[piece, 0:size, :])
            fold = taps[piece, 80:96, :]
            right += [fold] + [jnp.roll(fold, -32 * r, axis=1) for r in range(1, 4)]
            right.append(taps[piece, 96:112, :])
            if size == 96:
                right.append(fold)
        matrix = jnp.concatenate([jnp.concatenate(left, axis=0), jnp.concatenate(right, axis=0)], axis=1)
        both_rows = jnp.concatenate([shifted[which, pl.ds(start, reach), :] for which in range(2)], axis=0)
        sums[...] += dot(both_rows, matrix)
        return carry

    lax.fori_loop(0, 2 * half // STEP, add_block, 0)

    spot = iota((total, 1), 0)
    for which in range(2):
        first_len, second_len = lengths[which]
        in_first = spot < first_len
        inside = spot < first_len + second_len
        base = which * reach
        near = sums[base : base + total, 0:group] + sums[base + 1 : base + total + 1, group : 2 * group]
        base += GAP
        far = sums[base : base + total, 0:group] + sums[base + 1 : base + total + 1, group : 2 * group]
        conv_sum = jnp.where(inside, jnp.where(in_first, near, far), 0.0)
        packed = jnp.where(
            in_first, placed[which, half : half + total, :], placed[which, half + GAP : half + GAP + total, :]
        )
        hidden = packed + gelu(conv_sum)
        hidden = jnp.concatenate([hidden, jnp.zeros((total, -group % LANES), jnp.float32)], axis=1)
        both[which] = hidden.T[:group].astype(both.dtype)
    own_ref[...] = both[parity]
    other_ref[...] = both[1 - parity]


def join_kernel(owner_ref, own_ref, received_ref, out_ref):
    group = own_ref.shape[0]
    parity = owner_ref[0] % 2
    out_ref[pl.ds(pl.multiple_of(parity * group, 16), group), :] = own_ref[...]
    out_ref[pl.ds(pl.multiple_of((1 - parity) * group, 16), group), :] = received_ref[...]


VMEM = pl.BlockSpec(memory_space=pltpu.VMEM)
SMEM = pl.BlockSpec(memory_space=pltpu.SMEM)
ANY = pl.BlockSpec(memory_space=pl.ANY)


def shards(features, conv_weight, proj_weight, pos_weight, utt_len, pack_order):
    owners = lax.axis_size("dp")
    parts = lax.axis_size("mp")
    utts, slice_rows, channels = features.shape
    frames = slice_rows // 2
    model_width = proj_weight.shape[1]
    width = model_width // parts
    total = frames * owners
    half = pos_weight.shape[0] * owners // 2
    params = pltpu.CompilerParams(vmem_limit_bytes=48 * 1024 * 1024)
    large = pltpu.CompilerParams(vmem_limit_bytes=62 * 1024 * 1024)

    owner = lax.axis_index("dp").reshape(1)
    tap_copies = pl.pallas_call(
        pack_taps_kernel,
        out_shape=jax.ShapeDtypeStruct((owners, TAP_ROWS, LANES), jnp.bfloat16),
        in_specs=[VMEM],
        out_specs=VMEM,
        compiler_params=params,
    )(pos_weight)
    taps = lax.all_to_all(tap_copies, "dp", split_axis=0, concat_axis=0, tiled=True)

    sent = pl.pallas_call(
        functools.partial(front_kernel, utts, frames, parts),
        out_shape=jax.ShapeDtypeStruct((parts, utts, frames * width), jnp.bfloat16),
        in_specs=[ANY] * 3,
        out_specs=VMEM,
        scratch_shapes=[
            pltpu.VMEM((utts * slice_rows, channels), jnp.bfloat16),
            pltpu.VMEM(conv_weight.shape, jnp.bfloat16),
            pltpu.VMEM(proj_weight.shape, jnp.bfloat16),
            pltpu.SemaphoreType.DMA((3,)),
        ],
        compiler_params=large,
    )(features.reshape(utts * slice_rows, channels), conv_weight, proj_weight)
    spread = lax.all_to_all(sent, "mp", split_axis=0, concat_axis=0, tiled=True)

    ordered = pl.pallas_call(
        order_kernel,
        out_shape=jax.ShapeDtypeStruct((owners * 8, 2 * width), jnp.bfloat16),
        in_specs=[VMEM] * 2,
        out_specs=VMEM,
        compiler_params=params,
    )(pack_order.reshape(1, -1), spread.reshape(parts * utts, frames * width))
    pair_rows = lax.all_to_all(
        ordered.reshape(owners, 8, 2 * width), "dp", split_axis=0, concat_axis=0, tiled=True
    )

    reach = total + GAP + 16
    length = reach + 2 * half - STEP
    group = width // 2
    own, other = pl.pallas_call(
        functools.partial(positional_kernel, total, half),
        out_shape=[jax.ShapeDtypeStruct((group, total), jnp.bfloat16)] * 2,
        in_specs=[SMEM, SMEM, SMEM, VMEM, ANY],
        out_specs=[VMEM] * 2,
        scratch_shapes=[
            pltpu.VMEM((owners, TAP_ROWS, LANES), jnp.bfloat16),
            pltpu.VMEM((2, length + STEP, group), jnp.float32),
            pltpu.VMEM((2, length, 768), jnp.bfloat16),
            pltpu.VMEM((2 * reach, 256), jnp.float32),
            pltpu.VMEM((2, group, total), jnp.bfloat16),
            pltpu.SemaphoreType.DMA,
        ],
        compiler_params=large,
    )(owner, pack_order, utt_len, pair_rows.reshape(owners * 8, 2 * width), taps)
    received = lax.ppermute(other, "dp", [(o, o ^ 1) for o in range(owners)])
    hidden = pl.pallas_call(
        join_kernel,
        out_shape=jax.ShapeDtypeStruct((width, total), jnp.bfloat16),
        in_specs=[SMEM, VMEM, VMEM],
        out_specs=VMEM,
        compiler_params=params,
    )(owner, own, received)
    return hidden.T


def solution(mesh):
    in_specs = (P("mp", "dp", None), P(), P(), P("dp", "mp", None, None), P(), P())
    out_specs = P("dp", "mp")
    return jax.shard_map(shards, mesh=mesh, in_specs=in_specs, out_specs=out_specs, check_vma=False)
```

```python
import functools

import jax
import jax.numpy as jnp
from jax import lax
from jax.experimental import pallas as pl
from jax.experimental.pallas import tpu as pltpu
from jax.sharding import PartitionSpec as P

HOP = 320
EPS = 1e-05
LANES = 128
TAP_ROWS = 208
GAP = 64
STEP = 16


def iota(shape, dim):
    return lax.broadcasted_iota(jnp.int32, shape, dim)


def one_hot(condition):
    return jnp.where(condition, 1.0, 0.0).astype(jnp.bfloat16)


def dot(a, b, contract=((1,), (0,))):
    return lax.dot_general(a, b, (contract, ((), ())), preferred_element_type=jnp.float32)


def layer_norm(values):
    average = jnp.mean(values, axis=-1, keepdims=True)
    centred = values - average
    variance = jnp.mean(centred * centred, axis=-1, keepdims=True)
    return centred * lax.rsqrt(variance + EPS)


def gelu(values):
    return 0.5 * values * (1.0 + lax.erf(values * (0.5**0.5)))


def pack_taps_kernel(taps_ref, out_ref):
    wide = jnp.concatenate([taps_ref[0, 0], taps_ref[1, 0], taps_ref[0, 1], taps_ref[1, 1]], axis=1)
    out_ref[0:80, :] = wide[:, 0:128]
    out_ref[80:160, :] = wide[:, 128:256]
    rest = wide[:, 256:320]
    lower = jnp.concatenate([rest[48:80], rest[0:16]], axis=0)
    out_ref[160:208, :] = jnp.concatenate([rest[0:48], lower], axis=1)


def front_kernel(utts, frames, parts, features_hbm, conv_hbm, proj_hbm, out_ref, features_ref, conv_ref, proj_ref, sems):
    copies = [
        pltpu.make_async_copy(source, target, sems.at[n])
        for n, (source, target) in enumerate(
            [(features_hbm, features_ref), (conv_hbm, conv_ref), (proj_hbm, proj_ref)]
        )
    ]
    for copy in copies:
        copy.start()
    rows = utts * frames
    copies[0].wait()
    features = features_ref[...]
    row = iota((rows, 2 * rows), 0)
    column = iota((rows, 2 * rows), 1)
    source = (row % utts) * (2 * frames) + 2 * (row // utts)
    first = dot(one_hot(column == source), features).astype(jnp.bfloat16)
    second = dot(one_hot(column == source + 1), features).astype(jnp.bfloat16)
    copies[1].wait()
    conv_out = dot(first, conv_ref[0]) + dot(second, conv_ref[1])
    hidden = gelu(layer_norm(conv_out)).astype(jnp.bfloat16)
    normed = layer_norm(hidden.astype(jnp.float32)).astype(jnp.bfloat16)
    copies[2].wait()
    projected = dot(normed, proj_ref[...]).astype(jnp.bfloat16)
    width = projected.shape[1] // parts
    for part in range(parts):
        pieces = [
            projected[f * utts : (f + 1) * utts, part * width : (part + 1) * width] for f in range(frames)
        ]
        out_ref[part] = jnp.concatenate(pieces, axis=1)


def order_kernel(order_ref, spread_ref, out_ref):
    utts, lanes = spread_ref.shape
    rows, width = out_ref.shape
    quarters = lanes // width
    chosen = one_hot(iota((utts, utts), 0) == order_ref[...])
    ordered = dot(chosen, spread_ref[...], ((0,), (0,))).astype(jnp.bfloat16)
    slot = iota((rows, utts), 0) // quarters
    quarter = iota((rows, utts), 0) % quarters
    same = slot == iota((rows, utts), 1)
    total = None
    for q in range(quarters):
        term = dot(one_hot(same & (quarter == q)), ordered[:, q * width : (q + 1) * width])
        total = term if total is None else total + term
    out_ref[...] = total.astype(out_ref.dtype)


def positional_kernel(total, half, blocks, owner_ref, order_ref, len_ref, rows_ref, taps_hbm, out_ref, taps, placed, shifted, sums, sem):
    copy = pltpu.make_async_copy(taps_hbm, taps, sem)
    copy.start()
    owner = owner_ref[0]
    first_len = len_ref[order_ref[2 * owner]] // HOP
    second_len = len_ref[order_ref[2 * owner + 1]] // HOP

    width = out_ref.shape[0]
    group = width // 2
    spots = placed.shape[0]
    columns = rows_ref.shape[0]
    column = iota((1, columns), 1)
    slot = (column // 4) % 2
    spot = iota((spots, columns), 0)
    acc = None
    for parity in range(2):
        frame = (column // 8) * 8 + (column % 4) * 2 + parity
        target = jnp.where(slot == 0, frame, frame + first_len + GAP) + half
        valid = frame < jnp.where(slot == 0, first_len, second_len)
        target = jnp.where(valid, target, -1)
        term = dot(one_hot(spot == target), rows_ref[:, parity * width : (parity + 1) * width])
        acc = term if acc is None else acc + term
    placed[...] = acc

    length = shifted.shape[1]
    for g in range(2):
        lanes = slice(g * group, (g + 1) * group)
        for third in range(3):
            pairs = [k for k in range(3 * third, 3 * third + 3) if k < 8]
            pieces = [placed[2 * k : 2 * k + length, lanes].astype(jnp.bfloat16) for k in pairs]
            pieces.append(jnp.zeros((length, 256 - group * len(pairs)), jnp.bfloat16))
            shifted[g, :, third * 256 : (third + 1) * 256] = jnp.concatenate(pieces, axis=1)
    sums[...] = jnp.zeros_like(sums)
    copy.wait()

    reach = sums.shape[1]

    def add_block(block, carry):
        start = pl.multiple_of(block * STEP, STEP)

        def piece(pair, tile, size):
            base = pl.multiple_of((block * 8 + pair) * TAP_ROWS, 16)
            if tile < 2:
                return taps[pl.ds(base + 80 * tile, size), :]
            tail = taps[pl.ds(base + 160, 48), :]
            low = jnp.concatenate([tail, jnp.roll(tail, 64, axis=1)], axis=0)
            return low[:size]

        matrices = []
        for tile in range(3):
            parts = []
            for third in range(3):
                pairs = [min(k, 7) for k in range(3 * third, 3 * third + 3)]
                parts += [piece(pairs[0], tile, 80), piece(pairs[1], tile, 80), piece(pairs[2], tile, 96)]
            matrices.append(jnp.concatenate(parts, axis=0))
        for g in range(2):
            right = jnp.concatenate([matrices[g], matrices[g + 1]], axis=1)
            sums[g] += dot(shifted[g, pl.ds(start, reach), :], right)
        return carry

    lax.fori_loop(0, blocks, add_block, 0)

    spot = iota((total, 1), 0)
    in_first = spot < first_len
    inside = spot < first_len + second_len
    result = []
    for g in range(2):
        offset = 32 * g
        even = slice(offset, offset + group)
        odd = slice(offset + group, offset + 2 * group)
        near = sums[g, 0:total, even] + sums[g, 1 : total + 1, odd]
        far = sums[g, GAP : GAP + total, even] + sums[g, GAP + 1 : GAP + total + 1, odd]
        result.append(jnp.where(inside, jnp.where(in_first, near, far), 0.0))
    conv_sum = jnp.concatenate(result, axis=1)
    packed = jnp.where(in_first, placed[half : half + total, :], placed[half + GAP : half + GAP + total, :])
    hidden = packed + gelu(conv_sum)
    hidden = jnp.concatenate([hidden, jnp.zeros((total, -width % LANES), jnp.float32)], axis=1)
    out_ref[...] = hidden.T[:width].astype(out_ref.dtype)


VMEM = pl.BlockSpec(memory_space=pltpu.VMEM)
SMEM = pl.BlockSpec(memory_space=pltpu.SMEM)
ANY = pl.BlockSpec(memory_space=pl.ANY)


def shards(features, conv_weight, proj_weight, pos_weight, utt_len, pack_order):
    owner = lax.axis_index("dp").reshape(1)
    owners = lax.axis_size("dp")
    parts = lax.axis_size("mp")
    utts, slice_rows, channels = features.shape
    frames = slice_rows // 2
    model_width = proj_weight.shape[1]
    width = model_width // parts
    total = frames * owners
    half = pos_weight.shape[0] * owners // 2
    params = pltpu.CompilerParams(vmem_limit_bytes=48 * 1024 * 1024)
    large = pltpu.CompilerParams(vmem_limit_bytes=62 * 1024 * 1024)

    packed_taps = pl.pallas_call(
        pack_taps_kernel,
        out_shape=jax.ShapeDtypeStruct((TAP_ROWS, LANES), jnp.bfloat16),
        in_specs=[VMEM],
        out_specs=VMEM,
        compiler_params=params,
    )(pos_weight)
    ring = round(owners**0.5)
    along_z = [[y * ring + z for z in range(ring)] for y in range(ring)]
    along_y = [[y * ring + z for y in range(ring)] for z in range(ring)]
    taps = lax.all_gather(packed_taps, "dp", axis=0, tiled=True, axis_index_groups=along_z)

    sent = pl.pallas_call(
        functools.partial(front_kernel, utts, frames, parts),
        out_shape=jax.ShapeDtypeStruct((parts, utts, frames * width), jnp.bfloat16),
        in_specs=[ANY] * 3,
        out_specs=VMEM,
        scratch_shapes=[
            pltpu.VMEM((utts * slice_rows, channels), jnp.bfloat16),
            pltpu.VMEM(conv_weight.shape, jnp.bfloat16),
            pltpu.VMEM(proj_weight.shape, jnp.bfloat16),
            pltpu.SemaphoreType.DMA((3,)),
        ],
        compiler_params=large,
    )(features.reshape(utts * slice_rows, channels), conv_weight, proj_weight)
    spread = lax.all_to_all(sent, "mp", split_axis=0, concat_axis=0, tiled=True)

    taps, spread = lax.optimization_barrier((taps, spread))
    taps = lax.all_gather(taps, "dp", axis=0, tiled=True, axis_index_groups=along_y)

    ordered = pl.pallas_call(
        order_kernel,
        out_shape=jax.ShapeDtypeStruct((owners * 8, 2 * width), jnp.bfloat16),
        in_specs=[VMEM] * 2,
        out_specs=VMEM,
        compiler_params=params,
    )(pack_order.reshape(1, -1), spread.reshape(parts * utts, frames * width))
    pair_rows = lax.all_to_all(
        ordered.reshape(owners, 8, 2 * width), "dp", split_axis=0, concat_axis=0, tiled=True
    )

    blocks = 2 * half // STEP
    reach = total + GAP + 16
    length = reach + 2 * half - STEP
    hidden = pl.pallas_call(
        functools.partial(positional_kernel, total, half, blocks),
        out_shape=jax.ShapeDtypeStruct((width, total), jnp.bfloat16),
        in_specs=[SMEM, SMEM, SMEM, VMEM, pl.BlockSpec(memory_space=pl.ANY)],
        out_specs=VMEM,
        scratch_shapes=[
            pltpu.VMEM((owners * TAP_ROWS, LANES), jnp.bfloat16),
            pltpu.VMEM((length + STEP, width), jnp.float32),
            pltpu.VMEM((2, length, 768), jnp.bfloat16),
            pltpu.VMEM((2, reach, 256), jnp.float32),
            pltpu.SemaphoreType.DMA,
        ],
        compiler_params=large,
    )(owner, pack_order, utt_len, pair_rows.reshape(owners * 8, 2 * width), taps)
    return hidden.T


def solution(mesh):
    in_specs = (P("mp", "dp", None), P(), P(), P("dp", "mp", None, None), P(), P())
    out_specs = P("dp", "mp")
    return jax.shard_map(shards, mesh=mesh, in_specs=in_specs, out_specs=out_specs, check_vma=False)
```

```python
import functools

import jax
import jax.numpy as jnp
from jax import lax
from jax.experimental import pallas as pl
from jax.experimental.pallas import tpu as pltpu
from jax.sharding import PartitionSpec as P

HOP = 320
EPS = 1e-05
LANES = 128
TAP_ROWS = 112
GAP = 64
STEP = 16


def iota(shape, dim):
    return lax.broadcasted_iota(jnp.int32, shape, dim)


def one_hot(condition):
    return jnp.where(condition, 1.0, 0.0).astype(jnp.bfloat16)


def dot(a, b, contract=((1,), (0,))):
    return lax.dot_general(a, b, (contract, ((), ())), preferred_element_type=jnp.float32)


def layer_norm(values):
    average = jnp.mean(values, axis=-1, keepdims=True)
    centred = values - average
    variance = jnp.mean(centred * centred, axis=-1, keepdims=True)
    return centred * lax.rsqrt(variance + EPS)


def gelu(values):
    return 0.5 * values * (1.0 + lax.erf(values * (0.5**0.5)))


def pack_taps_kernel(taps_ref, out_ref):
    packed = []
    for g in range(2):
        rest = taps_ref[1, g, :, 48:80]
        packed.append(
            jnp.concatenate(
                [
                    jnp.concatenate([taps_ref[0, g], taps_ref[1, g, :, 0:48]], axis=1),
                    jnp.concatenate([rest[16 * r : 16 * r + 16] for r in range(4)], axis=1),
                    jnp.concatenate([rest[64:80], jnp.zeros((16, 96), rest.dtype)], axis=1),
                ],
                axis=0,
            )
        )
    for device in range(out_ref.shape[0]):
        out_ref[device] = packed[device % 2]


def front_kernel(utts, frames, parts, features_hbm, conv_hbm, proj_hbm, out_ref, features_ref, conv_ref, proj_ref, sems):
    copies = [
        pltpu.make_async_copy(source, target, sems.at[n])
        for n, (source, target) in enumerate(
            [(features_hbm, features_ref), (conv_hbm, conv_ref), (proj_hbm, proj_ref)]
        )
    ]
    for copy in copies:
        copy.start()
    rows = utts * frames
    copies[0].wait()
    features = features_ref[...]
    row = iota((rows, 2 * rows), 0)
    column = iota((rows, 2 * rows), 1)
    source = (row % utts) * (2 * frames) + 2 * (row // utts)
    first = dot(one_hot(column == source), features).astype(jnp.bfloat16)
    second = dot(one_hot(column == source + 1), features).astype(jnp.bfloat16)
    copies[1].wait()
    conv_out = dot(first, conv_ref[0]) + dot(second, conv_ref[1])
    hidden = gelu(layer_norm(conv_out)).astype(jnp.bfloat16)
    normed = layer_norm(hidden.astype(jnp.float32)).astype(jnp.bfloat16)
    copies[2].wait()
    projected = dot(normed, proj_ref[...]).astype(jnp.bfloat16)
    group = projected.shape[1] // (2 * parts)
    for part in range(parts):
        pieces = [
            projected[f * utts : (f + 1) * utts, (2 * part + g) * group : (2 * part + g + 1) * group]
            for g in range(2)
            for f in range(frames)
        ]
        out_ref[part] = jnp.concatenate(pieces, axis=1)


def order_kernel(order_ref, spread_ref, out_ref):
    utts, lanes = spread_ref.shape
    rows, width = out_ref.shape
    width //= 2
    chosen = one_hot(iota((utts, utts), 0) == order_ref[...])
    ordered = dot(chosen, spread_ref[...], ((0,), (0,))).astype(jnp.bfloat16)
    row = iota((rows, utts), 0)
    eighth = (row // 8) % 2 * 4 + row % 4
    slot = row // 16 * 4 + row // 4 % 2
    for which in range(2):
        same = slot + 2 * which == iota((rows, utts), 1)
        total = None
        for e in range(0, lanes // width, 2):
            left = jnp.concatenate([one_hot(same & (eighth == e + n)) for n in range(2)], axis=1)
            right = [ordered[:, (e + n) * width : (e + n + 1) * width] for n in range(2)]
            term = dot(left, jnp.concatenate(right, axis=0))
            total = term if total is None else total + term
        out_ref[:, which * width : (which + 1) * width] = total.astype(out_ref.dtype)


def pair_lengths(owner_ref, order_ref, len_ref):
    slot = owner_ref[0] // 2 * 4
    return [[len_ref[order_ref[slot + 2 * which + n]] // HOP for n in range(2)] for which in range(2)]


def place_kernel(total, half, owner_ref, order_ref, len_ref, rows_ref, shifted_ref, packed_ref, placed):
    lengths = pair_lengths(owner_ref, order_ref, len_ref)
    _, spots, group = placed.shape
    columns = rows_ref.shape[0]
    column = iota((1, columns), 1)
    is_first = (column // 4) % 2 == 0
    spot = iota((spots, columns), 0)
    for which in range(2):
        first_len, second_len = lengths[which]
        acc = None
        for odd in range(2):
            frame = (column // 8) * 8 + (column % 4) * 2 + odd
            target = jnp.where(is_first, frame, frame + first_len + GAP) + half
            valid = frame < jnp.where(is_first, first_len, second_len)
            target = jnp.where(valid, target, -1)
            lane = (2 * which + odd) * group
            term = dot(one_hot(spot == target), rows_ref[:, lane : lane + group])
            acc = term if acc is None else acc + term
        placed[which] = acc

    length = shifted_ref.shape[1]
    for which in range(2):
        for third in range(3):
            pairs = [k for k in range(3 * third, 3 * third + 3) if k < 8]
            pieces = [placed[which, 2 * k : 2 * k + length, :].astype(jnp.bfloat16) for k in pairs]
            pieces.append(jnp.zeros((length, 256 - group * len(pairs)), jnp.bfloat16))
            shifted_ref[which, :, third * 256 : (third + 1) * 256] = jnp.concatenate(pieces, axis=1)
        packed_ref[which] = jnp.where(
            iota((total, 1), 0) < lengths[which][0],
            placed[which, half : half + total, :],
            placed[which, half + GAP : half + GAP + total, :],
        )


def positional_kernel(
    owner_ref, order_ref, len_ref, shifted_ref, packed_ref, taps_ref, own_ref, other_ref, sums, both
):
    blocks = taps_ref.shape[0] // 8
    lengths = pair_lengths(owner_ref, order_ref, len_ref)
    parity = owner_ref[0] % 2
    group, total = own_ref.shape
    reach = sums.shape[0] // 2

    for block in range(blocks):
        start = block * STEP
        left, right = [], []
        for slot in range(9):
            piece = block * 8 + min(slot, 7)
            size = 96 if slot % 3 == 2 else 80
            left.append(taps_ref[piece, 0:size, :])
            fold = taps_ref[piece, 80:96, :]
            right += [fold] + [jnp.roll(fold, -32 * r, axis=1) for r in range(1, 4)]
            right.append(taps_ref[piece, 96:112, :])
            if size == 96:
                right.append(fold)
        matrix = jnp.concatenate([jnp.concatenate(left, axis=0), jnp.concatenate(right, axis=0)], axis=1)
        for which in range(2):
            rows = slice(which * reach, (which + 1) * reach)
            term = dot(shifted_ref[which, start : start + reach, :], matrix)
            sums[rows, :] = term if block == 0 else sums[rows, :] + term

    spot = iota((total, 1), 0)
    for which in range(2):
        first_len, second_len = lengths[which]
        base = which * reach
        near = sums[base : base + total, 0:group] + sums[base + 1 : base + total + 1, group : 2 * group]
        base += GAP
        far = sums[base : base + total, 0:group] + sums[base + 1 : base + total + 1, group : 2 * group]
        conv_sum = jnp.where(spot < first_len + second_len, jnp.where(spot < first_len, near, far), 0.0)
        hidden = packed_ref[which] + gelu(conv_sum)
        hidden = jnp.concatenate([hidden, jnp.zeros((total, -group % LANES), jnp.float32)], axis=1)
        both[which] = hidden.T[:group].astype(both.dtype)
    own_ref[...] = both[parity]
    other_ref[...] = both[1 - parity]


def join_kernel(owner_ref, own_ref, received_ref, out_ref):
    group = own_ref.shape[0]
    parity = owner_ref[0] % 2
    out_ref[pl.ds(pl.multiple_of(parity * group, 16), group), :] = own_ref[...]
    out_ref[pl.ds(pl.multiple_of((1 - parity) * group, 16), group), :] = received_ref[...]


VMEM = pl.BlockSpec(memory_space=pltpu.VMEM)
SMEM = pl.BlockSpec(memory_space=pltpu.SMEM)
ANY = pl.BlockSpec(memory_space=pl.ANY)


def shards(features, conv_weight, proj_weight, pos_weight, utt_len, pack_order):
    owners = lax.axis_size("dp")
    parts = lax.axis_size("mp")
    utts, slice_rows, channels = features.shape
    frames = slice_rows // 2
    model_width = proj_weight.shape[1]
    width = model_width // parts
    total = frames * owners
    half = pos_weight.shape[0] * owners // 2
    params = pltpu.CompilerParams(vmem_limit_bytes=48 * 1024 * 1024)
    large = pltpu.CompilerParams(vmem_limit_bytes=62 * 1024 * 1024)

    owner = lax.axis_index("dp").reshape(1)
    ring = round(owners**0.5)
    along_z = [[y * ring + z for z in range(ring)] for y in range(ring)]
    along_y = [[y * ring + z for y in range(ring)] for z in range(ring)]
    tap_copies = pl.pallas_call(
        pack_taps_kernel,
        out_shape=jax.ShapeDtypeStruct((ring, TAP_ROWS, LANES), jnp.bfloat16),
        in_specs=[VMEM],
        out_specs=VMEM,
        compiler_params=params,
    )(pos_weight)
    taps = lax.all_to_all(tap_copies, "dp", 0, 0, axis_index_groups=along_z, tiled=True)

    sent = pl.pallas_call(
        functools.partial(front_kernel, utts, frames, parts),
        out_shape=jax.ShapeDtypeStruct((parts, utts, frames * width), jnp.bfloat16),
        in_specs=[ANY] * 3,
        out_specs=VMEM,
        scratch_shapes=[
            pltpu.VMEM((utts * slice_rows, channels), jnp.bfloat16),
            pltpu.VMEM(conv_weight.shape, jnp.bfloat16),
            pltpu.VMEM(proj_weight.shape, jnp.bfloat16),
            pltpu.SemaphoreType.DMA((3,)),
        ],
        compiler_params=large,
    )(features.reshape(utts * slice_rows, channels), conv_weight, proj_weight)
    taps, sent = lax.optimization_barrier((taps, sent))
    taps = lax.all_gather(taps, "dp", axis=0, tiled=True, axis_index_groups=along_y)
    spread = lax.all_to_all(sent, "mp", split_axis=0, concat_axis=0, tiled=True)

    ordered = pl.pallas_call(
        order_kernel,
        out_shape=jax.ShapeDtypeStruct((owners * 8, 2 * width), jnp.bfloat16),
        in_specs=[VMEM] * 2,
        out_specs=VMEM,
        compiler_params=params,
    )(pack_order.reshape(1, -1), spread.reshape(parts * utts, frames * width))
    pair_rows = lax.all_to_all(
        ordered.reshape(owners, 8, 2 * width), "dp", split_axis=0, concat_axis=0, tiled=True
    )

    reach = total + GAP + 16
    length = reach + 2 * half - STEP
    group = width // 2
    scalars = (owner, pack_order, utt_len)
    shifted, packed = pl.pallas_call(
        functools.partial(place_kernel, total, half),
        out_shape=[
            jax.ShapeDtypeStruct((2, length, 768), jnp.bfloat16),
            jax.ShapeDtypeStruct((2, total, group), jnp.float32),
        ],
        in_specs=[SMEM, SMEM, SMEM, VMEM],
        out_specs=[VMEM] * 2,
        scratch_shapes=[pltpu.VMEM((2, length + STEP, group), jnp.float32)],
        compiler_params=params,
    )(*scalars, pair_rows.reshape(owners * 8, 2 * width))
    own, other = pl.pallas_call(
        positional_kernel,
        out_shape=[jax.ShapeDtypeStruct((group, total), jnp.bfloat16)] * 2,
        in_specs=[SMEM, SMEM, SMEM, VMEM, VMEM, VMEM],
        out_specs=[VMEM] * 2,
        scratch_shapes=[
            pltpu.VMEM((2 * reach, 256), jnp.float32),
            pltpu.VMEM((2, group, total), jnp.bfloat16),
        ],
        compiler_params=params,
    )(*scalars, shifted, packed, taps)
    received = lax.ppermute(other, "dp", [(o, o ^ 1) for o in range(owners)])
    hidden = pl.pallas_call(
        join_kernel,
        out_shape=jax.ShapeDtypeStruct((width, total), jnp.bfloat16),
        in_specs=[SMEM, VMEM, VMEM],
        out_specs=VMEM,
        compiler_params=params,
    )(owner, own, received)
    return hidden.T


def solution(mesh):
    in_specs = (P("mp", "dp", None), P(), P(), P("dp", "mp", None, None), P(), P())
    out_specs = P("dp", "mp")
    return jax.shard_map(shards, mesh=mesh, in_specs=in_specs, out_specs=out_specs, check_vma=False)
```

```python
import functools

import jax
import jax.numpy as jnp
from jax import lax
from jax.experimental import pallas as pl
from jax.experimental.pallas import tpu as pltpu
from jax.sharding import PartitionSpec as P

HOP = 320
EPS = 1e-05
LANES = 128
TAP_ROWS = 208
GAP = 64
STEP = 16


def iota(shape, dim):
    return lax.broadcasted_iota(jnp.int32, shape, dim)


def one_hot(condition):
    return jnp.where(condition, 1.0, 0.0).astype(jnp.bfloat16)


def dot(a, b, contract=((1,), (0,))):
    return lax.dot_general(a, b, (contract, ((), ())), preferred_element_type=jnp.float32)


def layer_norm(values):
    average = jnp.mean(values, axis=-1, keepdims=True)
    centred = values - average
    variance = jnp.mean(centred * centred, axis=-1, keepdims=True)
    return centred * lax.rsqrt(variance + EPS)


def gelu(values):
    return 0.5 * values * (1.0 + lax.erf(values * (0.5**0.5)))


def pack_taps_kernel(taps_hbm, out_ref, taps_ref, sem):
    copy = pltpu.make_async_copy(taps_hbm, taps_ref, sem)
    copy.start()
    copy.wait()
    wide = jnp.concatenate([taps_ref[0, 0], taps_ref[1, 0], taps_ref[0, 1], taps_ref[1, 1]], axis=1)
    rest = wide[:, 256:320]
    lower = jnp.concatenate([rest[48:80], rest[0:16]], axis=0)
    folded = jnp.concatenate([rest[0:48], lower], axis=1)
    packed = jnp.concatenate([wide[:, 0:128], wide[:, 128:256], folded], axis=0)
    for receiver in range(out_ref.shape[0]):
        out_ref[receiver] = packed


def front_kernel(utts, frames, parts, features_hbm, conv_hbm, proj_hbm, out_ref, features_ref, conv_ref, proj_ref, sems):
    copies = [
        pltpu.make_async_copy(source, target, sems.at[n])
        for n, (source, target) in enumerate(
            [(features_hbm, features_ref), (conv_hbm, conv_ref), (proj_hbm, proj_ref)]
        )
    ]
    for copy in copies:
        copy.start()
    rows = utts * frames
    copies[0].wait()
    features = features_ref[...]
    row = iota((rows, 2 * rows), 0)
    column = iota((rows, 2 * rows), 1)
    source = (row % utts) * (2 * frames) + 2 * (row // utts)
    first = dot(one_hot(column == source), features).astype(jnp.bfloat16)
    second = dot(one_hot(column == source + 1), features).astype(jnp.bfloat16)
    copies[1].wait()
    conv_out = dot(first, conv_ref[0]) + dot(second, conv_ref[1])
    hidden = gelu(layer_norm(conv_out)).astype(jnp.bfloat16)
    normed = layer_norm(hidden.astype(jnp.float32)).astype(jnp.bfloat16)
    copies[2].wait()
    projected = dot(normed, proj_ref[...]).astype(jnp.bfloat16)
    width = projected.shape[1] // parts
    for part in range(parts):
        pieces = [
            projected[f * utts : (f + 1) * utts, part * width : (part + 1) * width] for f in range(frames)
        ]
        out_ref[part] = jnp.concatenate(pieces, axis=1)


def order_kernel(order_ref, spread_ref, out_ref):
    utts, lanes = spread_ref.shape
    rows, width = out_ref.shape
    quarters = lanes // width
    chosen = one_hot(iota((utts, utts), 0) == order_ref[...])
    ordered = dot(chosen, spread_ref[...], ((0,), (0,))).astype(jnp.bfloat16)
    slot = iota((rows, utts), 0) // quarters
    quarter = iota((rows, utts), 0) % quarters
    same = slot == iota((rows, utts), 1)
    total = None
    for q in range(quarters):
        term = dot(one_hot(same & (quarter == q)), ordered[:, q * width : (q + 1) * width])
        total = term if total is None else total + term
    out_ref[...] = total.astype(out_ref.dtype)


def own_lengths(owner_ref, order_ref, len_ref):
    return [len_ref[order_ref[2 * owner_ref[0] + n]] // HOP for n in range(2)]


def place_kernel(total, half, owner_ref, order_ref, len_ref, rows_ref, shifted_ref, packed_ref, placed):
    first_len, second_len = own_lengths(owner_ref, order_ref, len_ref)
    spots, width = placed.shape
    group = width // 2
    columns = rows_ref.shape[0]
    column = iota((1, columns), 1)
    is_first = (column // 4) % 2 == 0
    spot = iota((spots, columns), 0)
    acc = None
    for odd in range(2):
        frame = (column // 8) * 8 + (column % 4) * 2 + odd
        target = jnp.where(is_first, frame, frame + first_len + GAP) + half
        valid = frame < jnp.where(is_first, first_len, second_len)
        target = jnp.where(valid, target, -1)
        term = dot(one_hot(spot == target), rows_ref[:, odd * width : (odd + 1) * width])
        acc = term if acc is None else acc + term
    placed[...] = acc

    length = shifted_ref.shape[1]
    for g in range(2):
        lanes = slice(g * group, (g + 1) * group)
        for third in range(3):
            pairs = [k for k in range(3 * third, 3 * third + 3) if k < 8]
            pieces = [placed[2 * k : 2 * k + length, lanes].astype(jnp.bfloat16) for k in pairs]
            pieces.append(jnp.zeros((length, 256 - group * len(pairs)), jnp.bfloat16))
            shifted_ref[g, :, third * 256 : (third + 1) * 256] = jnp.concatenate(pieces, axis=1)
    packed_ref[...] = jnp.where(
        iota((total, 1), 0) < first_len, placed[half : half + total, :], placed[half + GAP : half + GAP + total, :]
    )


def positional_kernel(
    owner_ref, order_ref, len_ref, shifted_hbm, packed_hbm, taps_hbm, out_ref, shifted, packed, taps, sums, sems
):
    blocks = sems.shape[0] - 3
    size = taps.shape[0] // blocks
    tap_copies = []
    for block in range(blocks):
        rows = pl.ds(size * block, size)
        tap_copies.append(pltpu.make_async_copy(taps_hbm.at[rows, :], taps.at[rows, :], sems.at[block]))
    row_copies = [pltpu.make_async_copy(shifted_hbm.at[g], shifted.at[g], sems.at[blocks + g]) for g in range(2)]
    packed_copy = pltpu.make_async_copy(packed_hbm, packed, sems.at[blocks + 2])
    for copy in tap_copies[:1] + row_copies + tap_copies[1:] + [packed_copy]:
        copy.start()
    first_len, second_len = own_lengths(owner_ref, order_ref, len_ref)
    width, total = out_ref.shape
    group = width // 2
    reach = sums.shape[1]

    for block in range(blocks):
        tap_copies[block].wait()
        pairs = [min(slot, 7) for slot in range(9)]
        matrices = []
        for tile in range(3):
            parts = []
            for slot, pair in enumerate(pairs):
                base = (block * 8 + pair) * TAP_ROWS
                rows = 96 if slot % 3 == 2 else 80
                if tile < 2:
                    parts.append(taps[base + 80 * tile : base + 80 * tile + rows, :])
                else:
                    tail = taps[base + 160 : base + 208, :]
                    parts += [tail, jnp.roll(tail, 64, axis=1)[: rows - 48]]
            matrices.append(jnp.concatenate(parts, axis=0))
        for g in range(2):
            if block == 0:
                row_copies[g].wait()
            matrix = jnp.concatenate([matrices[g], matrices[g + 1]], axis=1)
            term = dot(shifted[g, block * STEP : block * STEP + reach, :], matrix)
            sums[g] = term if block == 0 else sums[g] + term

    packed_copy.wait()
    spot = iota((total, 1), 0)
    result = []
    for g in range(2):
        offset = 32 * g
        even = slice(offset, offset + group)
        odd = slice(offset + group, offset + 2 * group)
        near = sums[g, 0:total, even] + sums[g, 1 : total + 1, odd]
        far = sums[g, GAP : GAP + total, even] + sums[g, GAP + 1 : GAP + total + 1, odd]
        result.append(jnp.where(spot < first_len + second_len, jnp.where(spot < first_len, near, far), 0.0))
    hidden = packed[...] + gelu(jnp.concatenate(result, axis=1))
    hidden = jnp.concatenate([hidden, jnp.zeros((total, -width % LANES), jnp.float32)], axis=1)
    out_ref[...] = hidden.T[:width].astype(out_ref.dtype)


VMEM = pl.BlockSpec(memory_space=pltpu.VMEM)
SMEM = pl.BlockSpec(memory_space=pltpu.SMEM)
ANY = pl.BlockSpec(memory_space=pl.ANY)


def shards(features, conv_weight, proj_weight, pos_weight, utt_len, pack_order):
    owner = lax.axis_index("dp").reshape(1)
    owners = lax.axis_size("dp")
    parts = lax.axis_size("mp")
    utts, slice_rows, channels = features.shape
    frames = slice_rows // 2
    model_width = proj_weight.shape[1]
    width = model_width // parts
    total = frames * owners
    half = pos_weight.shape[0] * owners // 2
    params = pltpu.CompilerParams(vmem_limit_bytes=48 * 1024 * 1024)
    large = pltpu.CompilerParams(vmem_limit_bytes=62 * 1024 * 1024)

    ring = round(owners**0.5)
    along_z = [[y * ring + z for z in range(ring)] for y in range(ring)]
    along_y = [[y * ring + z for y in range(ring)] for z in range(ring)]
    tap_copies = pl.pallas_call(
        pack_taps_kernel,
        out_shape=jax.ShapeDtypeStruct((ring, TAP_ROWS, LANES), jnp.bfloat16),
        in_specs=[ANY],
        out_specs=VMEM,
        scratch_shapes=[pltpu.VMEM(pos_weight.shape, jnp.bfloat16), pltpu.SemaphoreType.DMA],
        compiler_params=large,
    )(pos_weight)
    taps = lax.all_to_all(tap_copies, "dp", 0, 0, axis_index_groups=along_z, tiled=True)

    sent = pl.pallas_call(
        functools.partial(front_kernel, utts, frames, parts),
        out_shape=jax.ShapeDtypeStruct((parts, utts, frames * width), jnp.bfloat16),
        in_specs=[ANY] * 3,
        out_specs=VMEM,
        scratch_shapes=[
            pltpu.VMEM((utts * slice_rows, channels), jnp.bfloat16),
            pltpu.VMEM(conv_weight.shape, jnp.bfloat16),
            pltpu.VMEM(proj_weight.shape, jnp.bfloat16),
            pltpu.SemaphoreType.DMA((3,)),
        ],
        compiler_params=large,
    )(features.reshape(utts * slice_rows, channels), conv_weight, proj_weight)
    taps, sent = lax.optimization_barrier((taps, sent))
    taps = lax.all_gather(taps.reshape(ring * TAP_ROWS, LANES), "dp", axis=0, tiled=True, axis_index_groups=along_y)
    spread = lax.all_to_all(sent, "mp", split_axis=0, concat_axis=0, tiled=True)

    ordered = pl.pallas_call(
        order_kernel,
        out_shape=jax.ShapeDtypeStruct((owners * 8, 2 * width), jnp.bfloat16),
        in_specs=[VMEM] * 2,
        out_specs=VMEM,
        compiler_params=params,
    )(pack_order.reshape(1, -1), spread.reshape(parts * utts, frames * width))
    pair_rows = lax.all_to_all(
        ordered.reshape(owners, 8, 2 * width), "dp", split_axis=0, concat_axis=0, tiled=True
    )

    blocks = 2 * half // STEP
    reach = total + GAP + 16
    length = reach + 2 * half - STEP
    scalars = (owner, pack_order, utt_len)
    shifted, packed = pl.pallas_call(
        functools.partial(place_kernel, total, half),
        out_shape=[
            jax.ShapeDtypeStruct((2, length, 768), jnp.bfloat16),
            jax.ShapeDtypeStruct((total, width), jnp.float32),
        ],
        in_specs=[SMEM, SMEM, SMEM, VMEM],
        out_specs=[VMEM] * 2,
        scratch_shapes=[pltpu.VMEM((length + STEP, width), jnp.float32)],
        compiler_params=params,
    )(*scalars, pair_rows.reshape(owners * 8, 2 * width))
    hidden = pl.pallas_call(
        positional_kernel,
        out_shape=jax.ShapeDtypeStruct((width, total), jnp.bfloat16),
        in_specs=[SMEM, SMEM, SMEM, ANY, ANY, ANY],
        out_specs=VMEM,
        scratch_shapes=[
            pltpu.VMEM(shifted.shape, jnp.bfloat16),
            pltpu.VMEM(packed.shape, jnp.float32),
            pltpu.VMEM((owners * TAP_ROWS, LANES), jnp.bfloat16),
            pltpu.VMEM((2, reach, 256), jnp.float32),
            pltpu.SemaphoreType.DMA((blocks + 3,)),
        ],
        compiler_params=large,
    )(*scalars, shifted, packed, taps)
    return hidden.T


def solution(mesh):
    in_specs = (P("mp", "dp", None), P(), P(), P("dp", "mp", None, None), P(), P())
    out_specs = P("dp", "mp")
    return jax.shard_map(shards, mesh=mesh, in_specs=in_specs, out_specs=out_specs, check_vma=False)
```

```python
import functools

import jax
import jax.numpy as jnp
from jax import lax
from jax.experimental import pallas as pl
from jax.experimental.pallas import tpu as pltpu
from jax.sharding import PartitionSpec as P

HOP = 320
EPS = 1e-05
LANES = 128
TAP_ROWS = 112
GAP = 64
STEP = 16


def iota(shape, dim):
    return lax.broadcasted_iota(jnp.int32, shape, dim)


def one_hot(condition):
    return jnp.where(condition, 1.0, 0.0).astype(jnp.bfloat16)


def dot(a, b, contract=((1,), (0,))):
    return lax.dot_general(a, b, (contract, ((), ())), preferred_element_type=jnp.float32)


def layer_norm(values):
    average = jnp.mean(values, axis=-1, keepdims=True)
    centred = values - average
    variance = jnp.mean(centred * centred, axis=-1, keepdims=True)
    return centred * lax.rsqrt(variance + EPS)


def gelu(values):
    return 0.5 * values * (1.0 + lax.erf(values * (0.5**0.5)))


def pack_taps_kernel(taps_ref, out_ref):
    packed = []
    for g in range(2):
        rest = taps_ref[1, g, :, 48:80]
        packed.append(
            jnp.concatenate(
                [
                    jnp.concatenate([taps_ref[0, g], taps_ref[1, g, :, 0:48]], axis=1),
                    jnp.concatenate([rest[16 * r : 16 * r + 16] for r in range(4)], axis=1),
                    jnp.concatenate([rest[64:80], jnp.zeros((16, 96), rest.dtype)], axis=1),
                ],
                axis=0,
            )
        )
    for device in range(out_ref.shape[0]):
        out_ref[device] = packed[device % 2]


def front_kernel(utts, frames, parts, features_hbm, conv_hbm, proj_hbm, out_ref, features_ref, conv_ref, proj_ref, sems):
    copies = [
        pltpu.make_async_copy(source, target, sems.at[n])
        for n, (source, target) in enumerate(
            [(features_hbm, features_ref), (conv_hbm, conv_ref), (proj_hbm, proj_ref)]
        )
    ]
    for copy in copies:
        copy.start()
    rows = utts * frames
    copies[0].wait()
    features = features_ref[...]
    row = iota((rows, 2 * rows), 0)
    column = iota((rows, 2 * rows), 1)
    source = (row % utts) * (2 * frames) + 2 * (row // utts)
    first = dot(one_hot(column == source), features).astype(jnp.bfloat16)
    second = dot(one_hot(column == source + 1), features).astype(jnp.bfloat16)
    copies[1].wait()
    conv_out = dot(first, conv_ref[0]) + dot(second, conv_ref[1])
    hidden = gelu(layer_norm(conv_out)).astype(jnp.bfloat16)
    normed = layer_norm(hidden.astype(jnp.float32)).astype(jnp.bfloat16)
    copies[2].wait()
    projected = dot(normed, proj_ref[...]).astype(jnp.bfloat16)
    group = projected.shape[1] // (2 * parts)
    for part in range(parts):
        pieces = [
            projected[f * utts : (f + 1) * utts, (2 * part + g) * group : (2 * part + g + 1) * group]
            for g in range(2)
            for f in range(frames)
        ]
        out_ref[part] = jnp.concatenate(pieces, axis=1)


def order_kernel(order_ref, spread_ref, out_ref):
    utts, lanes = spread_ref.shape
    rows, width = out_ref.shape
    width //= 2
    chosen = one_hot(iota((utts, utts), 0) == order_ref[...])
    ordered = dot(chosen, spread_ref[...], ((0,), (0,))).astype(jnp.bfloat16)
    row = iota((rows, utts), 0)
    eighth = (row // 8) % 2 * 4 + row % 4
    slot = row // 16 * 4 + row // 4 % 2
    for which in range(2):
        same = slot + 2 * which == iota((rows, utts), 1)
        total = None
        for e in range(0, lanes // width, 2):
            left = jnp.concatenate([one_hot(same & (eighth == e + n)) for n in range(2)], axis=1)
            right = [ordered[:, (e + n) * width : (e + n + 1) * width] for n in range(2)]
            term = dot(left, jnp.concatenate(right, axis=0))
            total = term if total is None else total + term
        out_ref[:, which * width : (which + 1) * width] = total.astype(out_ref.dtype)


def pair_lengths(owner_ref, order_ref, len_ref):
    slot = owner_ref[0] // 2 * 4
    return [[len_ref[order_ref[slot + 2 * which + n]] // HOP for n in range(2)] for which in range(2)]


def place_kernel(total, half, owner_ref, order_ref, len_ref, rows_ref, shifted_ref, packed_ref, placed):
    lengths = pair_lengths(owner_ref, order_ref, len_ref)
    _, spots, group = placed.shape
    columns = rows_ref.shape[0]
    column = iota((1, columns), 1)
    is_first = (column // 4) % 2 == 0
    spot = iota((spots, columns), 0)
    for which in range(2):
        first_len, second_len = lengths[which]
        acc = None
        for odd in range(2):
            frame = (column // 8) * 8 + (column % 4) * 2 + odd
            target = jnp.where(is_first, frame, frame + first_len + GAP) + half
            valid = frame < jnp.where(is_first, first_len, second_len)
            target = jnp.where(valid, target, -1)
            lane = (2 * which + odd) * group
            term = dot(one_hot(spot == target), rows_ref[:, lane : lane + group])
            acc = term if acc is None else acc + term
        placed[which] = acc

    length = shifted_ref.shape[1]
    for which in range(2):
        for third in range(3):
            pairs = [k for k in range(3 * third, 3 * third + 3) if k < 8]
            pieces = [placed[which, 2 * k : 2 * k + length, :].astype(jnp.bfloat16) for k in pairs]
            pieces.append(jnp.zeros((length, 256 - group * len(pairs)), jnp.bfloat16))
            shifted_ref[which, :, third * 256 : (third + 1) * 256] = jnp.concatenate(pieces, axis=1)
        packed_ref[which] = jnp.where(
            iota((total, 1), 0) < lengths[which][0],
            placed[which, half : half + total, :],
            placed[which, half + GAP : half + GAP + total, :],
        )


def positional_kernel(
    owner_ref, order_ref, len_ref, shifted_ref, packed_ref, taps_ref, own_ref, other_ref, sums, both
):
    blocks = taps_ref.shape[0] // 8
    lengths = pair_lengths(owner_ref, order_ref, len_ref)
    parity = owner_ref[0] % 2
    group, total = own_ref.shape
    reach = sums.shape[0] // 2

    for block in range(blocks):
        start = block * STEP
        left, right = [], []
        for slot in range(9):
            piece = block * 8 + min(slot, 7)
            size = 96 if slot % 3 == 2 else 80
            left.append(taps_ref[piece, 0:size, :])
            fold = taps_ref[piece, 80:96, :]
            right += [fold] + [jnp.roll(fold, -32 * r, axis=1) for r in range(1, 4)]
            right.append(taps_ref[piece, 96:112, :])
            if size == 96:
                right.append(fold)
        matrix = jnp.concatenate([jnp.concatenate(left, axis=0), jnp.concatenate(right, axis=0)], axis=1)
        for which in range(2):
            rows = slice(which * reach, (which + 1) * reach)
            term = dot(shifted_ref[which, start : start + reach, :], matrix)
            sums[rows, :] = term if block == 0 else sums[rows, :] + term

    spot = iota((total, 1), 0)
    for which in range(2):
        first_len, second_len = lengths[which]
        base = which * reach
        near = sums[base : base + total, 0:group] + sums[base + 1 : base + total + 1, group : 2 * group]
        base += GAP
        far = sums[base : base + total, 0:group] + sums[base + 1 : base + total + 1, group : 2 * group]
        conv_sum = jnp.where(spot < first_len + second_len, jnp.where(spot < first_len, near, far), 0.0)
        hidden = packed_ref[which] + gelu(conv_sum)
        hidden = jnp.concatenate([hidden, jnp.zeros((total, -group % LANES), jnp.float32)], axis=1)
        both[which] = hidden.T[:group].astype(both.dtype)
    own_ref[...] = both[parity]
    other_ref[...] = both[1 - parity]


def join_kernel(owner_ref, own_ref, received_ref, out_ref):
    group = own_ref.shape[0]
    parity = owner_ref[0] % 2
    out_ref[pl.ds(pl.multiple_of(parity * group, 16), group), :] = own_ref[...]
    out_ref[pl.ds(pl.multiple_of((1 - parity) * group, 16), group), :] = received_ref[...]


VMEM = pl.BlockSpec(memory_space=pltpu.VMEM)
SMEM = pl.BlockSpec(memory_space=pltpu.SMEM)
ANY = pl.BlockSpec(memory_space=pl.ANY)


def shards(features, conv_weight, proj_weight, pos_weight, utt_len, pack_order):
    owners = lax.axis_size("dp")
    parts = lax.axis_size("mp")
    utts, slice_rows, channels = features.shape
    frames = slice_rows // 2
    model_width = proj_weight.shape[1]
    width = model_width // parts
    total = frames * owners
    half = pos_weight.shape[0] * owners // 2
    params = pltpu.CompilerParams(vmem_limit_bytes=48 * 1024 * 1024)
    large = pltpu.CompilerParams(vmem_limit_bytes=62 * 1024 * 1024)

    owner = lax.axis_index("dp").reshape(1)
    ring = round(owners**0.5)
    near = [[o for o in range(owners) if o // (2 * ring) == pair] for pair in range(ring // 2)]
    far = [list(range(first, owners, 2 * ring)) for first in range(2 * ring)]
    tap_copies = pl.pallas_call(
        pack_taps_kernel,
        out_shape=jax.ShapeDtypeStruct((2 * ring, TAP_ROWS, LANES), jnp.bfloat16),
        in_specs=[VMEM],
        out_specs=VMEM,
        compiler_params=params,
    )(pos_weight)
    taps = lax.all_to_all(tap_copies, "dp", 0, 0, axis_index_groups=near, tiled=True)

    sent = pl.pallas_call(
        functools.partial(front_kernel, utts, frames, parts),
        out_shape=jax.ShapeDtypeStruct((parts, utts, frames * width), jnp.bfloat16),
        in_specs=[ANY] * 3,
        out_specs=VMEM,
        scratch_shapes=[
            pltpu.VMEM((utts * slice_rows, channels), jnp.bfloat16),
            pltpu.VMEM(conv_weight.shape, jnp.bfloat16),
            pltpu.VMEM(proj_weight.shape, jnp.bfloat16),
            pltpu.SemaphoreType.DMA((3,)),
        ],
        compiler_params=large,
    )(features.reshape(utts * slice_rows, channels), conv_weight, proj_weight)
    taps, sent = lax.optimization_barrier((taps, sent))
    taps = lax.all_gather(taps, "dp", axis=0, tiled=True, axis_index_groups=far)
    spread = lax.all_to_all(sent, "mp", split_axis=0, concat_axis=0, tiled=True)

    ordered = pl.pallas_call(
        order_kernel,
        out_shape=jax.ShapeDtypeStruct((owners * 8, 2 * width), jnp.bfloat16),
        in_specs=[VMEM] * 2,
        out_specs=VMEM,
        compiler_params=params,
    )(pack_order.reshape(1, -1), spread.reshape(parts * utts, frames * width))
    pair_rows = lax.all_to_all(
        ordered.reshape(owners, 8, 2 * width), "dp", split_axis=0, concat_axis=0, tiled=True
    )

    reach = total + GAP + 16
    length = reach + 2 * half - STEP
    group = width // 2
    scalars = (owner, pack_order, utt_len)
    shifted, packed = pl.pallas_call(
        functools.partial(place_kernel, total, half),
        out_shape=[
            jax.ShapeDtypeStruct((2, length, 768), jnp.bfloat16),
            jax.ShapeDtypeStruct((2, total, group), jnp.float32),
        ],
        in_specs=[SMEM, SMEM, SMEM, VMEM],
        out_specs=[VMEM] * 2,
        scratch_shapes=[pltpu.VMEM((2, length + STEP, group), jnp.float32)],
        compiler_params=params,
    )(*scalars, pair_rows.reshape(owners * 8, 2 * width))
    own, other = pl.pallas_call(
        positional_kernel,
        out_shape=[jax.ShapeDtypeStruct((group, total), jnp.bfloat16)] * 2,
        in_specs=[SMEM, SMEM, SMEM, VMEM, VMEM, VMEM],
        out_specs=[VMEM] * 2,
        scratch_shapes=[
            pltpu.VMEM((2 * reach, 256), jnp.float32),
            pltpu.VMEM((2, group, total), jnp.bfloat16),
        ],
        compiler_params=params,
    )(*scalars, shifted, packed, taps)
    received = lax.ppermute(other, "dp", [(o, o ^ 1) for o in range(owners)])
    hidden = pl.pallas_call(
        join_kernel,
        out_shape=jax.ShapeDtypeStruct((width, total), jnp.bfloat16),
        in_specs=[SMEM, VMEM, VMEM],
        out_specs=VMEM,
        compiler_params=params,
    )(owner, own, received)
    return hidden.T


def solution(mesh):
    in_specs = (P("mp", "dp", None), P(), P(), P("dp", "mp", None, None), P(), P())
    out_specs = P("dp", "mp")
    return jax.shard_map(shards, mesh=mesh, in_specs=in_specs, out_specs=out_specs, check_vma=False)
```

```python
import functools

import jax
import jax.numpy as jnp
from jax import lax
from jax.experimental import pallas as pl
from jax.experimental.pallas import tpu as pltpu
from jax.sharding import PartitionSpec as P

HOP = 320
EPS = 1e-05
LANES = 128
TAP_ROWS = 112
GAP = 64
STEP = 16


def iota(shape, dim):
    return lax.broadcasted_iota(jnp.int32, shape, dim)


def one_hot(condition):
    return jnp.where(condition, 1.0, 0.0).astype(jnp.bfloat16)


def dot(a, b, contract=((1,), (0,))):
    return lax.dot_general(a, b, (contract, ((), ())), preferred_element_type=jnp.float32)


def layer_norm(values):
    average = jnp.mean(values, axis=-1, keepdims=True)
    centred = values - average
    variance = jnp.mean(centred * centred, axis=-1, keepdims=True)
    return centred * lax.rsqrt(variance + EPS)


def gelu(values):
    return 0.5 * values * (1.0 + lax.erf(values * (0.5**0.5)))


def pack_taps_kernel(taps_ref, out_ref):
    packed = []
    for g in range(2):
        rest = taps_ref[1, g, :, 48:80]
        packed.append(
            jnp.concatenate(
                [
                    jnp.concatenate([taps_ref[0, g], taps_ref[1, g, :, 0:48]], axis=1),
                    jnp.concatenate([rest[16 * r : 16 * r + 16] for r in range(4)], axis=1),
                    jnp.concatenate([rest[64:80], jnp.zeros((16, 96), rest.dtype)], axis=1),
                ],
                axis=0,
            )
        )
    for device in range(out_ref.shape[0]):
        out_ref[device] = packed[device % 2]


def front_kernel(utts, frames, parts, features_hbm, conv_hbm, proj_hbm, out_ref, features_ref, conv_ref, proj_ref, sems):
    copies = [
        pltpu.make_async_copy(source, target, sems.at[n])
        for n, (source, target) in enumerate(
            [(features_hbm, features_ref), (conv_hbm, conv_ref), (proj_hbm, proj_ref)]
        )
    ]
    for copy in copies:
        copy.start()
    rows = utts * frames
    copies[0].wait()
    features = features_ref[...]
    row = iota((rows, 2 * rows), 0)
    column = iota((rows, 2 * rows), 1)
    source = (row % utts) * (2 * frames) + 2 * (row // utts)
    first = dot(one_hot(column == source), features).astype(jnp.bfloat16)
    second = dot(one_hot(column == source + 1), features).astype(jnp.bfloat16)
    copies[1].wait()
    conv_out = dot(first, conv_ref[0]) + dot(second, conv_ref[1])
    hidden = gelu(layer_norm(conv_out)).astype(jnp.bfloat16)
    normed = layer_norm(hidden.astype(jnp.float32)).astype(jnp.bfloat16)
    copies[2].wait()
    projected = dot(normed, proj_ref[...]).astype(jnp.bfloat16)
    group = projected.shape[1] // (2 * parts)
    for part in range(parts):
        pieces = [
            projected[f * utts : (f + 1) * utts, (2 * part + g) * group : (2 * part + g + 1) * group]
            for g in range(2)
            for f in range(frames)
        ]
        out_ref[part] = jnp.concatenate(pieces, axis=1)


def order_kernel(order_ref, spread_ref, out_ref):
    utts, lanes = spread_ref.shape
    rows, width = out_ref.shape
    width //= 2
    chosen = one_hot(iota((utts, utts), 0) == order_ref[...])
    ordered = dot(chosen, spread_ref[...], ((0,), (0,))).astype(jnp.bfloat16)
    row = iota((rows, utts), 0)
    eighth = (row // 8) % 2 * 4 + row % 4
    slot = row // 16 * 4 + row // 4 % 2
    for which in range(2):
        same = slot + 2 * which == iota((rows, utts), 1)
        total = None
        for e in range(0, lanes // width, 2):
            left = jnp.concatenate([one_hot(same & (eighth == e + n)) for n in range(2)], axis=1)
            right = [ordered[:, (e + n) * width : (e + n + 1) * width] for n in range(2)]
            term = dot(left, jnp.concatenate(right, axis=0))
            total = term if total is None else total + term
        out_ref[:, which * width : (which + 1) * width] = total.astype(out_ref.dtype)


def pair_lengths(owner_ref, order_ref, len_ref):
    slot = owner_ref[0] // 2 * 4
    return [[len_ref[order_ref[slot + 2 * which + n]] // HOP for n in range(2)] for which in range(2)]


def place_kernel(total, half, owner_ref, order_ref, len_ref, rows_ref, shifted_ref, packed_ref, placed):
    lengths = pair_lengths(owner_ref, order_ref, len_ref)
    _, spots, group = placed.shape
    columns = rows_ref.shape[0]
    column = iota((1, columns), 1)
    is_first = (column // 4) % 2 == 0
    spot = iota((spots, columns), 0)
    for which in range(2):
        first_len, second_len = lengths[which]
        acc = None
        for odd in range(2):
            frame = (column // 8) * 8 + (column % 4) * 2 + odd
            target = jnp.where(is_first, frame, frame + first_len + GAP) + half
            valid = frame < jnp.where(is_first, first_len, second_len)
            target = jnp.where(valid, target, -1)
            lane = (2 * which + odd) * group
            term = dot(one_hot(spot == target), rows_ref[:, lane : lane + group])
            acc = term if acc is None else acc + term
        placed[which] = acc

    length = shifted_ref.shape[1]
    for which in range(2):
        for third in range(3):
            pairs = [k for k in range(3 * third, 3 * third + 3) if k < 8]
            pieces = [placed[which, 2 * k : 2 * k + length, :].astype(jnp.bfloat16) for k in pairs]
            pieces.append(jnp.zeros((length, 256 - group * len(pairs)), jnp.bfloat16))
            shifted_ref[which, :, third * 256 : (third + 1) * 256] = jnp.concatenate(pieces, axis=1)
        packed_ref[which] = jnp.where(
            iota((total, 1), 0) < lengths[which][0],
            placed[which, half : half + total, :],
            placed[which, half + GAP : half + GAP + total, :],
        )


def positional_kernel(
    swap, owner_ref, order_ref, len_ref, shifted_hbm, packed_hbm, taps_hbm, out_ref, shifted, packed, taps, sums, sems
):
    parity = owner_ref[0] % 2
    which = 1 - parity if swap else parity
    blocks = sems.shape[0] - 2
    copies = []
    for block in range(blocks):
        rows = pl.ds(8 * block, 8)
        copies.append(pltpu.make_async_copy(taps_hbm.at[rows], taps.at[rows], sems.at[block]))
    rows_copy = pltpu.make_async_copy(shifted_hbm.at[which], shifted, sems.at[blocks])
    packed_copy = pltpu.make_async_copy(packed_hbm.at[which], packed, sems.at[blocks + 1])
    for copy in [rows_copy] + copies + [packed_copy]:
        copy.start()
    slot = 2 * (owner_ref[0] - parity + which)
    first_len = len_ref[order_ref[slot]] // HOP
    second_len = len_ref[order_ref[slot + 1]] // HOP
    total, group = packed.shape
    reach = sums.shape[0]

    rows_copy.wait()
    for block in range(blocks):
        copies[block].wait()
        start = block * STEP
        left, right = [], []
        for slot in range(9):
            piece = block * 8 + min(slot, 7)
            size = 96 if slot % 3 == 2 else 80
            left.append(taps[piece, 0:size, :])
            fold = taps[piece, 80:96, :]
            right += [fold] + [jnp.roll(fold, -32 * r, axis=1) for r in range(1, 4)]
            right.append(taps[piece, 96:112, :])
            if size == 96:
                right.append(fold)
        matrix = jnp.concatenate([jnp.concatenate(left, axis=0), jnp.concatenate(right, axis=0)], axis=1)
        term = dot(shifted[start : start + reach, :], matrix)
        sums[...] = term if block == 0 else sums[...] + term

    packed_copy.wait()
    spot = iota((total, 1), 0)
    near = sums[0:total, 0:group] + sums[1 : total + 1, group : 2 * group]
    far = sums[GAP : GAP + total, 0:group] + sums[GAP + 1 : GAP + total + 1, group : 2 * group]
    conv_sum = jnp.where(spot < first_len + second_len, jnp.where(spot < first_len, near, far), 0.0)
    hidden = packed[...] + gelu(conv_sum)
    hidden = jnp.concatenate([hidden, jnp.zeros((total, -group % LANES), jnp.float32)], axis=1)
    start = 0 if swap else pl.multiple_of(parity * group, 16)
    out_ref[pl.ds(start, group), :] = hidden.T[:group].astype(out_ref.dtype)


def join_kernel(owner_ref, received_hbm, own_hbm, out_hbm, sem):
    group = received_hbm.shape[0]
    start = pl.multiple_of((1 - owner_ref[0] % 2) * group, 16)
    copy = pltpu.make_async_copy(received_hbm, out_hbm.at[pl.ds(start, group), :], sem)
    copy.start()
    copy.wait()


VMEM = pl.BlockSpec(memory_space=pltpu.VMEM)
SMEM = pl.BlockSpec(memory_space=pltpu.SMEM)
ANY = pl.BlockSpec(memory_space=pl.ANY)


def shards(features, conv_weight, proj_weight, pos_weight, utt_len, pack_order):
    owners = lax.axis_size("dp")
    parts = lax.axis_size("mp")
    utts, slice_rows, channels = features.shape
    frames = slice_rows // 2
    model_width = proj_weight.shape[1]
    width = model_width // parts
    total = frames * owners
    half = pos_weight.shape[0] * owners // 2
    params = pltpu.CompilerParams(vmem_limit_bytes=48 * 1024 * 1024)
    large = pltpu.CompilerParams(vmem_limit_bytes=62 * 1024 * 1024)

    owner = lax.axis_index("dp").reshape(1)
    ring = round(owners**0.5)
    along_z = [[y * ring + z for z in range(ring)] for y in range(ring)]
    along_y = [[y * ring + z for y in range(ring)] for z in range(ring)]
    tap_copies = pl.pallas_call(
        pack_taps_kernel,
        out_shape=jax.ShapeDtypeStruct((ring, TAP_ROWS, LANES), jnp.bfloat16),
        in_specs=[VMEM],
        out_specs=VMEM,
        compiler_params=params,
    )(pos_weight)
    taps = lax.all_to_all(tap_copies, "dp", 0, 0, axis_index_groups=along_z, tiled=True)

    sent = pl.pallas_call(
        functools.partial(front_kernel, utts, frames, parts),
        out_shape=jax.ShapeDtypeStruct((parts, utts, frames * width), jnp.bfloat16),
        in_specs=[ANY] * 3,
        out_specs=VMEM,
        scratch_shapes=[
            pltpu.VMEM((utts * slice_rows, channels), jnp.bfloat16),
            pltpu.VMEM(conv_weight.shape, jnp.bfloat16),
            pltpu.VMEM(proj_weight.shape, jnp.bfloat16),
            pltpu.SemaphoreType.DMA((3,)),
        ],
        compiler_params=pltpu.CompilerParams(vmem_limit_bytes=66900000),
    )(features.reshape(utts * slice_rows, channels), conv_weight, proj_weight)
    taps, sent = lax.optimization_barrier((taps, sent))
    taps = lax.all_gather(taps, "dp", axis=0, tiled=True, axis_index_groups=along_y)
    spread = lax.all_to_all(sent, "mp", split_axis=0, concat_axis=0, tiled=True)

    ordered = pl.pallas_call(
        order_kernel,
        out_shape=jax.ShapeDtypeStruct((owners * 8, 2 * width), jnp.bfloat16),
        in_specs=[VMEM] * 2,
        out_specs=VMEM,
        compiler_params=params,
    )(pack_order.reshape(1, -1), spread.reshape(parts * utts, frames * width))
    pair_rows = lax.all_to_all(
        ordered.reshape(owners, 8, 2 * width), "dp", split_axis=0, concat_axis=0, tiled=True
    )

    reach = total + GAP + 16
    length = reach + 2 * half - STEP
    group = width // 2
    scalars = (owner, pack_order, utt_len)
    shifted, packed = pl.pallas_call(
        functools.partial(place_kernel, total, half),
        out_shape=[
            jax.ShapeDtypeStruct((2, length, 768), jnp.bfloat16),
            jax.ShapeDtypeStruct((2, total, group), jnp.float32),
        ],
        in_specs=[SMEM, SMEM, SMEM, VMEM],
        out_specs=[VMEM] * 2,
        scratch_shapes=[pltpu.VMEM((2, length + STEP, group), jnp.float32)],
        compiler_params=large,
    )(*scalars, pair_rows.reshape(owners * 8, 2 * width))
    convolve = lambda swap: pl.pallas_call(
        functools.partial(positional_kernel, swap),
        out_shape=jax.ShapeDtypeStruct((group if swap else width, total), jnp.bfloat16),
        in_specs=[SMEM, SMEM, SMEM, ANY, ANY, ANY],
        out_specs=VMEM,
        scratch_shapes=[
            pltpu.VMEM((length, 768), jnp.bfloat16),
            pltpu.VMEM((total, group), jnp.float32),
            pltpu.VMEM((owners, TAP_ROWS, LANES), jnp.bfloat16),
            pltpu.VMEM((reach, 256), jnp.float32),
            pltpu.SemaphoreType.DMA((2 * half // STEP + 2,)),
        ],
        compiler_params=large,
    )
    other = convolve(True)(*scalars, shifted, packed, taps)
    packed, other = lax.optimization_barrier((packed, other))
    received = lax.ppermute(other, "dp", [(o, o ^ 1) for o in range(owners)])
    own = convolve(False)(*scalars, shifted, packed, taps)
    hidden = pl.pallas_call(
        join_kernel,
        out_shape=jax.ShapeDtypeStruct((width, total), jnp.bfloat16),
        in_specs=[SMEM, ANY, ANY],
        out_specs=ANY,
        scratch_shapes=[pltpu.SemaphoreType.DMA],
        input_output_aliases={2: 0},
        compiler_params=params,
    )(owner, received, own)
    return hidden.T


def solution(mesh):
    in_specs = (P("mp", "dp", None), P(), P(), P("dp", "mp", None, None), P(), P())
    out_specs = P("dp", "mp")
    return jax.shard_map(shards, mesh=mesh, in_specs=in_specs, out_specs=out_specs, check_vma=False)
```

```python
import functools

import jax
import jax.numpy as jnp
from jax import lax
from jax.experimental import pallas as pl
from jax.experimental.pallas import tpu as pltpu
from jax.sharding import PartitionSpec as P

HOP = 320
EPS = 1e-05
LANES = 128
TAP_ROWS = 112
GAP = 64
STEP = 16


def iota(shape, dim):
    return lax.broadcasted_iota(jnp.int32, shape, dim)


def one_hot(condition):
    return jnp.where(condition, 1.0, 0.0).astype(jnp.bfloat16)


def dot(a, b, contract=((1,), (0,))):
    return lax.dot_general(a, b, (contract, ((), ())), preferred_element_type=jnp.float32)


def layer_norm(values):
    average = jnp.mean(values, axis=-1, keepdims=True)
    centred = values - average
    variance = jnp.mean(centred * centred, axis=-1, keepdims=True)
    return centred * lax.rsqrt(variance + EPS)


def gelu(values):
    return 0.5 * values * (1.0 + lax.erf(values * (0.5**0.5)))


def pack_taps_kernel(taps_ref, out_ref):
    packed = []
    for g in range(2):
        rest = taps_ref[1, g, :, 48:80]
        packed.append(
            jnp.concatenate(
                [
                    jnp.concatenate([taps_ref[0, g], taps_ref[1, g, :, 0:48]], axis=1),
                    jnp.concatenate([rest[16 * r : 16 * r + 16] for r in range(4)], axis=1),
                    jnp.concatenate([rest[64:80], jnp.zeros((16, 96), rest.dtype)], axis=1),
                ],
                axis=0,
            )
        )
    for device in range(out_ref.shape[0]):
        out_ref[device] = packed[device % 2]


def front_kernel(utts, frames, parts, features_hbm, conv_hbm, proj_hbm, out_ref, features_ref, conv_ref, proj_ref, sems):
    copies = [
        pltpu.make_async_copy(source, target, sems.at[n])
        for n, (source, target) in enumerate(
            [(features_hbm, features_ref), (conv_hbm, conv_ref), (proj_hbm, proj_ref)]
        )
    ]
    for copy in copies:
        copy.start()
    rows = utts * frames
    copies[0].wait()
    features = features_ref[...]
    row = iota((rows, 2 * rows), 0)
    column = iota((rows, 2 * rows), 1)
    source = (row % utts) * (2 * frames) + 2 * (row // utts)
    first = dot(one_hot(column == source), features).astype(jnp.bfloat16)
    second = dot(one_hot(column == source + 1), features).astype(jnp.bfloat16)
    copies[1].wait()
    conv_out = dot(first, conv_ref[0]) + dot(second, conv_ref[1])
    hidden = gelu(layer_norm(conv_out)).astype(jnp.bfloat16)
    normed = layer_norm(hidden.astype(jnp.float32)).astype(jnp.bfloat16)
    copies[2].wait()
    projected = dot(normed, proj_ref[...]).astype(jnp.bfloat16)
    group = projected.shape[1] // (2 * parts)
    for part in range(parts):
        pieces = [
            projected[f * utts : (f + 1) * utts, (2 * part + g) * group : (2 * part + g + 1) * group]
            for g in range(2)
            for f in range(frames)
        ]
        out_ref[part] = jnp.concatenate(pieces, axis=1)


def order_kernel(order_ref, spread_ref, out_ref):
    utts, lanes = spread_ref.shape
    rows, width = out_ref.shape
    width //= 2
    chosen = one_hot(iota((utts, utts), 0) == order_ref[...])
    ordered = dot(chosen, spread_ref[...], ((0,), (0,))).astype(jnp.bfloat16)
    row = iota((rows, utts), 0)
    eighth = (row // 8) % 2 * 4 + row % 4
    slot = row // 16 * 4 + row // 4 % 2
    for which in range(2):
        same = slot + 2 * which == iota((rows, utts), 1)
        total = None
        for e in range(0, lanes // width, 2):
            left = jnp.concatenate([one_hot(same & (eighth == e + n)) for n in range(2)], axis=1)
            right = [ordered[:, (e + n) * width : (e + n + 1) * width] for n in range(2)]
            term = dot(left, jnp.concatenate(right, axis=0))
            total = term if total is None else total + term
        out_ref[:, which * width : (which + 1) * width] = total.astype(out_ref.dtype)


def pair_lengths(owner_ref, order_ref, len_ref):
    slot = owner_ref[0] // 2 * 4
    return [[len_ref[order_ref[slot + 2 * which + n]] // HOP for n in range(2)] for which in range(2)]


def place_kernel(total, half, owner_ref, order_ref, len_ref, rows_ref, shifted_ref, packed_ref, placed):
    lengths = pair_lengths(owner_ref, order_ref, len_ref)
    _, spots, group = placed.shape
    columns = rows_ref.shape[0]
    column = iota((1, columns), 1)
    is_first = (column // 4) % 2 == 0
    spot = iota((spots, columns), 0)
    for which in range(2):
        first_len, second_len = lengths[which]
        acc = None
        for odd in range(2):
            frame = (column // 8) * 8 + (column % 4) * 2 + odd
            target = jnp.where(is_first, frame, frame + first_len + GAP) + half
            valid = frame < jnp.where(is_first, first_len, second_len)
            target = jnp.where(valid, target, -1)
            lane = (2 * which + odd) * group
            term = dot(one_hot(spot == target), rows_ref[:, lane : lane + group])
            acc = term if acc is None else acc + term
        placed[which] = acc

    length = shifted_ref.shape[1]
    for which in range(2):
        for third in range(3):
            pairs = [k for k in range(3 * third, 3 * third + 3) if k < 8]
            pieces = [placed[which, 2 * k : 2 * k + length, :].astype(jnp.bfloat16) for k in pairs]
            pieces.append(jnp.zeros((length, 256 - group * len(pairs)), jnp.bfloat16))
            shifted_ref[which, :, third * 256 : (third + 1) * 256] = jnp.concatenate(pieces, axis=1)
        packed_ref[which] = jnp.where(
            iota((total, 1), 0) < lengths[which][0],
            placed[which, half : half + total, :],
            placed[which, half + GAP : half + GAP + total, :],
        )


def positional_kernel(
    swap, owner_ref, order_ref, len_ref, shifted_ref, packed_ref, taps_ref, out_ref, sums
):
    parity = owner_ref[0] % 2
    which = 1 - parity if swap else parity
    blocks = taps_ref.shape[0] // 8
    slot = 2 * (owner_ref[0] - parity + which)
    first_len = len_ref[order_ref[slot]] // HOP
    second_len = len_ref[order_ref[slot + 1]] // HOP
    _, total, group = packed_ref.shape
    reach = sums.shape[0]

    for block in range(blocks):
        start = block * STEP
        left, right = [], []
        for slot in range(9):
            piece = block * 8 + min(slot, 7)
            size = 96 if slot % 3 == 2 else 80
            left.append(taps_ref[piece, 0:size, :])
            fold = taps_ref[piece, 80:96, :]
            right += [fold] + [jnp.roll(fold, -32 * r, axis=1) for r in range(1, 4)]
            right.append(taps_ref[piece, 96:112, :])
            if size == 96:
                right.append(fold)
        matrix = jnp.concatenate([jnp.concatenate(left, axis=0), jnp.concatenate(right, axis=0)], axis=1)
        term = dot(shifted_ref[which, start : start + reach, :], matrix)
        sums[...] = term if block == 0 else sums[...] + term

    spot = iota((total, 1), 0)
    near = sums[0:total, 0:group] + sums[1 : total + 1, group : 2 * group]
    far = sums[GAP : GAP + total, 0:group] + sums[GAP + 1 : GAP + total + 1, group : 2 * group]
    conv_sum = jnp.where(spot < first_len + second_len, jnp.where(spot < first_len, near, far), 0.0)
    hidden = packed_ref[which] + gelu(conv_sum)
    hidden = jnp.concatenate([hidden, jnp.zeros((total, -group % LANES), jnp.float32)], axis=1)
    start = 0 if swap else pl.multiple_of(parity * group, 16)
    out_ref[pl.ds(start, group), :] = hidden.T[:group].astype(out_ref.dtype)


def join_kernel(owner_ref, received_hbm, own_hbm, out_hbm, sem):
    group = received_hbm.shape[0]
    start = pl.multiple_of((1 - owner_ref[0] % 2) * group, 16)
    copy = pltpu.make_async_copy(received_hbm, out_hbm.at[pl.ds(start, group), :], sem)
    copy.start()
    copy.wait()


VMEM = pl.BlockSpec(memory_space=pltpu.VMEM)
SMEM = pl.BlockSpec(memory_space=pltpu.SMEM)
ANY = pl.BlockSpec(memory_space=pl.ANY)


def shards(features, conv_weight, proj_weight, pos_weight, utt_len, pack_order):
    owners = lax.axis_size("dp")
    parts = lax.axis_size("mp")
    utts, slice_rows, channels = features.shape
    frames = slice_rows // 2
    model_width = proj_weight.shape[1]
    width = model_width // parts
    total = frames * owners
    half = pos_weight.shape[0] * owners // 2
    params = pltpu.CompilerParams(vmem_limit_bytes=48 * 1024 * 1024)
    large = pltpu.CompilerParams(vmem_limit_bytes=62 * 1024 * 1024)

    owner = lax.axis_index("dp").reshape(1)
    ring = round(owners**0.5)
    along_z = [[y * ring + z for z in range(ring)] for y in range(ring)]
    along_y = [[y * ring + z for y in range(ring)] for z in range(ring)]
    tap_copies = pl.pallas_call(
        pack_taps_kernel,
        out_shape=jax.ShapeDtypeStruct((ring, TAP_ROWS, LANES), jnp.bfloat16),
        in_specs=[VMEM],
        out_specs=VMEM,
        compiler_params=params,
    )(pos_weight)
    taps = lax.all_to_all(tap_copies, "dp", 0, 0, axis_index_groups=along_z, tiled=True)

    sent = pl.pallas_call(
        functools.partial(front_kernel, utts, frames, parts),
        out_shape=jax.ShapeDtypeStruct((parts, utts, frames * width), jnp.bfloat16),
        in_specs=[ANY] * 3,
        out_specs=VMEM,
        scratch_shapes=[
            pltpu.VMEM((utts * slice_rows, channels), jnp.bfloat16),
            pltpu.VMEM(conv_weight.shape, jnp.bfloat16),
            pltpu.VMEM(proj_weight.shape, jnp.bfloat16),
            pltpu.SemaphoreType.DMA((3,)),
        ],
        compiler_params=pltpu.CompilerParams(vmem_limit_bytes=66900000),
    )(features.reshape(utts * slice_rows, channels), conv_weight, proj_weight)
    taps, sent = lax.optimization_barrier((taps, sent))
    taps = lax.all_gather(taps, "dp", axis=0, tiled=True, axis_index_groups=along_y)
    spread = lax.all_to_all(sent, "mp", split_axis=0, concat_axis=0, tiled=True)

    ordered = pl.pallas_call(
        order_kernel,
        out_shape=jax.ShapeDtypeStruct((owners * 8, 2 * width), jnp.bfloat16),
        in_specs=[VMEM] * 2,
        out_specs=VMEM,
        compiler_params=params,
    )(pack_order.reshape(1, -1), spread.reshape(parts * utts, frames * width))
    pair_rows = lax.all_to_all(
        ordered.reshape(owners, 8, 2 * width), "dp", split_axis=0, concat_axis=0, tiled=True
    )

    reach = total + GAP + 16
    length = reach + 2 * half - STEP
    group = width // 2
    scalars = (owner, pack_order, utt_len)
    shifted, packed = pl.pallas_call(
        functools.partial(place_kernel, total, half),
        out_shape=[
            jax.ShapeDtypeStruct((2, length, 768), jnp.bfloat16),
            jax.ShapeDtypeStruct((2, total, group), jnp.float32),
        ],
        in_specs=[SMEM, SMEM, SMEM, VMEM],
        out_specs=[VMEM] * 2,
        scratch_shapes=[pltpu.VMEM((2, length + STEP, group), jnp.float32)],
        compiler_params=params,
    )(*scalars, pair_rows.reshape(owners * 8, 2 * width))
    convolve = lambda swap: pl.pallas_call(
        functools.partial(positional_kernel, swap),
        out_shape=jax.ShapeDtypeStruct((group if swap else width, total), jnp.bfloat16),
        in_specs=[SMEM, SMEM, SMEM, VMEM, VMEM, VMEM],
        out_specs=VMEM,
        scratch_shapes=[pltpu.VMEM((reach, 256), jnp.float32)],
        compiler_params=params,
    )
    other = convolve(True)(*scalars, shifted, packed, taps)
    packed, other = lax.optimization_barrier((packed, other))
    received = lax.ppermute(other, "dp", [(o, o ^ 1) for o in range(owners)])
    own = convolve(False)(*scalars, shifted, packed, taps)
    hidden = pl.pallas_call(
        join_kernel,
        out_shape=jax.ShapeDtypeStruct((width, total), jnp.bfloat16),
        in_specs=[SMEM, ANY, ANY],
        out_specs=ANY,
        scratch_shapes=[pltpu.SemaphoreType.DMA],
        input_output_aliases={2: 0},
        compiler_params=params,
    )(owner, received, own)
    return hidden.T


def solution(mesh):
    in_specs = (P("mp", "dp", None), P(), P(), P("dp", "mp", None, None), P(), P())
    out_specs = P("dp", "mp")
    return jax.shard_map(shards, mesh=mesh, in_specs=in_specs, out_specs=out_specs, check_vma=False)
```

```python
import functools

import jax
import jax.numpy as jnp
from jax import lax
from jax.experimental import pallas as pl
from jax.experimental.pallas import tpu as pltpu
from jax.sharding import PartitionSpec as P

HOP = 320
EPS = 1e-05
LANES = 128
TAP_ROWS = 112
GAP = 64
STEP = 16


def iota(shape, dim):
    return lax.broadcasted_iota(jnp.int32, shape, dim)


def one_hot(condition):
    return jnp.where(condition, 1.0, 0.0).astype(jnp.bfloat16)


def dot(a, b, contract=((1,), (0,))):
    return lax.dot_general(a, b, (contract, ((), ())), preferred_element_type=jnp.float32)


def layer_norm(values):
    average = jnp.mean(values, axis=-1, keepdims=True)
    centred = values - average
    variance = jnp.mean(centred * centred, axis=-1, keepdims=True)
    return centred * lax.rsqrt(variance + EPS)


def gelu(values):
    return 0.5 * values * (1.0 + lax.erf(values * (0.5**0.5)))


def pack_taps_kernel(taps_ref, out_ref):
    packed = []
    for g in range(2):
        rest = taps_ref[1, g, :, 48:80]
        packed.append(
            jnp.concatenate(
                [
                    jnp.concatenate([taps_ref[0, g], taps_ref[1, g, :, 0:48]], axis=1),
                    jnp.concatenate([rest[16 * r : 16 * r + 16] for r in range(4)], axis=1),
                    jnp.concatenate([rest[64:80], jnp.zeros((16, 96), rest.dtype)], axis=1),
                ],
                axis=0,
            )
        )
    for device in range(out_ref.shape[0]):
        out_ref[device] = packed[device % 2]


def front_kernel(utts, frames, parts, features_hbm, conv_hbm, proj_hbm, out_ref, features_ref, conv_ref, proj_ref, sems):
    copies = [
        pltpu.make_async_copy(source, target, sems.at[n])
        for n, (source, target) in enumerate(
            [(features_hbm, features_ref), (conv_hbm, conv_ref), (proj_hbm, proj_ref)]
        )
    ]
    for copy in copies:
        copy.start()
    rows = utts * frames
    copies[0].wait()
    features = features_ref[...]
    row = iota((rows, 2 * rows), 0)
    column = iota((rows, 2 * rows), 1)
    source = (row % utts) * (2 * frames) + 2 * (row // utts)
    first = dot(one_hot(column == source), features).astype(jnp.bfloat16)
    second = dot(one_hot(column == source + 1), features).astype(jnp.bfloat16)
    copies[1].wait()
    conv_out = dot(first, conv_ref[0]) + dot(second, conv_ref[1])
    hidden = gelu(layer_norm(conv_out)).astype(jnp.bfloat16)
    normed = layer_norm(hidden.astype(jnp.float32)).astype(jnp.bfloat16)
    copies[2].wait()
    projected = dot(normed, proj_ref[...]).astype(jnp.bfloat16)
    group = projected.shape[1] // (2 * parts)
    for part in range(parts):
        pieces = [
            projected[f * utts : (f + 1) * utts, (2 * part + g) * group : (2 * part + g + 1) * group]
            for g in range(2)
            for f in range(frames)
        ]
        out_ref[part] = jnp.concatenate(pieces, axis=1)


def order_kernel(order_ref, spread_ref, out_ref):
    utts, lanes = spread_ref.shape
    rows, width = out_ref.shape
    width //= 2
    chosen = one_hot(iota((utts, utts), 0) == order_ref[...])
    ordered = dot(chosen, spread_ref[...], ((0,), (0,))).astype(jnp.bfloat16)
    row = iota((rows, utts), 0)
    eighth = (row // 8) % 2 * 4 + row % 4
    slot = row // 16 * 4 + row // 4 % 2
    for which in range(2):
        same = slot + 2 * which == iota((rows, utts), 1)
        total = None
        for e in range(0, lanes // width, 2):
            left = jnp.concatenate([one_hot(same & (eighth == e + n)) for n in range(2)], axis=1)
            right = [ordered[:, (e + n) * width : (e + n + 1) * width] for n in range(2)]
            term = dot(left, jnp.concatenate(right, axis=0))
            total = term if total is None else total + term
        out_ref[:, which * width : (which + 1) * width] = total.astype(out_ref.dtype)


def pair_lengths(owner_ref, order_ref, len_ref):
    slot = owner_ref[0] // 2 * 4
    return [[len_ref[order_ref[slot + 2 * which + n]] // HOP for n in range(2)] for which in range(2)]


def place_kernel(total, half, owner_ref, order_ref, len_ref, rows_ref, shifted_ref, packed_ref, placed):
    lengths = pair_lengths(owner_ref, order_ref, len_ref)
    _, spots, group = placed.shape
    columns = rows_ref.shape[0]
    column = iota((1, columns), 1)
    is_first = (column // 4) % 2 == 0
    spot = iota((spots, columns), 0)
    for which in range(2):
        first_len, second_len = lengths[which]
        acc = None
        for odd in range(2):
            frame = (column // 8) * 8 + (column % 4) * 2 + odd
            target = jnp.where(is_first, frame, frame + first_len + GAP) + half
            valid = frame < jnp.where(is_first, first_len, second_len)
            target = jnp.where(valid, target, -1)
            lane = (2 * which + odd) * group
            term = dot(one_hot(spot == target), rows_ref[:, lane : lane + group])
            acc = term if acc is None else acc + term
        placed[which] = acc

    length = shifted_ref.shape[1]
    for which in range(2):
        for third in range(3):
            pairs = [k for k in range(3 * third, 3 * third + 3) if k < 8]
            pieces = [placed[which, 2 * k : 2 * k + length, :].astype(jnp.bfloat16) for k in pairs]
            pieces.append(jnp.zeros((length, 256 - group * len(pairs)), jnp.bfloat16))
            shifted_ref[which, :, third * 256 : (third + 1) * 256] = jnp.concatenate(pieces, axis=1)
        packed_ref[which] = jnp.where(
            iota((total, 1), 0) < lengths[which][0],
            placed[which, half : half + total, :],
            placed[which, half + GAP : half + GAP + total, :],
        )


def positional_kernel(
    swap, owner_ref, order_ref, len_ref, shifted_ref, packed_ref, *refs
):
    taps_refs, (out_ref, sums) = refs[:-2], refs[-2:]
    parity = owner_ref[0] % 2
    which = 1 - parity if swap else parity
    ring = taps_refs[0].shape[0]
    blocks = [[(ref, n) for n in range(ring)] for ref in taps_refs[:4] + taps_refs[6:]]
    blocks.insert(4, [(ref, n) for ref in taps_refs[4:6] for n in range(ring // 2)])
    slot = 2 * (owner_ref[0] - parity + which)
    first_len = len_ref[order_ref[slot]] // HOP
    second_len = len_ref[order_ref[slot + 1]] // HOP
    _, total, group = packed_ref.shape
    reach = sums.shape[0]

    for away, pieces in enumerate(blocks):
        start = pl.multiple_of(lax.rem(owner_ref[0] // ring + ring - away, ring) * STEP, STEP)
        left, right = [], []
        for slot in range(9):
            taps_ref, piece = pieces[min(slot, 7)]
            size = 96 if slot % 3 == 2 else 80
            left.append(taps_ref[piece, 0:size, :])
            fold = taps_ref[piece, 80:96, :]
            right += [fold] + [jnp.roll(fold, -32 * r, axis=1) for r in range(1, 4)]
            right.append(taps_ref[piece, 96:112, :])
            if size == 96:
                right.append(fold)
        matrix = jnp.concatenate([jnp.concatenate(left, axis=0), jnp.concatenate(right, axis=0)], axis=1)
        term = dot(shifted_ref[which, pl.ds(start, reach), :], matrix)
        sums[...] = term if away == 0 else sums[...] + term

    spot = iota((total, 1), 0)
    near = sums[0:total, 0:group] + sums[1 : total + 1, group : 2 * group]
    far = sums[GAP : GAP + total, 0:group] + sums[GAP + 1 : GAP + total + 1, group : 2 * group]
    conv_sum = jnp.where(spot < first_len + second_len, jnp.where(spot < first_len, near, far), 0.0)
    hidden = packed_ref[which] + gelu(conv_sum)
    hidden = jnp.concatenate([hidden, jnp.zeros((total, -group % LANES), jnp.float32)], axis=1)
    start = 0 if swap else pl.multiple_of(parity * group, 16)
    out_ref[pl.ds(start, group), :] = hidden.T[:group].astype(out_ref.dtype)


def join_kernel(owner_ref, received_hbm, own_hbm, out_hbm, sem):
    group = received_hbm.shape[0]
    start = pl.multiple_of((1 - owner_ref[0] % 2) * group, 16)
    copy = pltpu.make_async_copy(received_hbm, out_hbm.at[pl.ds(start, group), :], sem)
    copy.start()
    copy.wait()


VMEM = pl.BlockSpec(memory_space=pltpu.VMEM)
SMEM = pl.BlockSpec(memory_space=pltpu.SMEM)
ANY = pl.BlockSpec(memory_space=pl.ANY)


def send(values, ring, step):
    return lax.ppermute(values, "dp", [(o, (o + step * ring) % (ring * ring)) for o in range(ring * ring)])


def shards(features, conv_weight, proj_weight, pos_weight, utt_len, pack_order):
    owners = lax.axis_size("dp")
    parts = lax.axis_size("mp")
    utts, slice_rows, channels = features.shape
    frames = slice_rows // 2
    model_width = proj_weight.shape[1]
    width = model_width // parts
    total = frames * owners
    half = pos_weight.shape[0] * owners // 2
    params = pltpu.CompilerParams(vmem_limit_bytes=48 * 1024 * 1024)
    large = pltpu.CompilerParams(vmem_limit_bytes=62 * 1024 * 1024)

    owner = lax.axis_index("dp").reshape(1)
    ring = round(owners**0.5)
    along_z = [[y * ring + z for z in range(ring)] for y in range(ring)]
    tap_copies = pl.pallas_call(
        pack_taps_kernel,
        out_shape=jax.ShapeDtypeStruct((ring, TAP_ROWS, LANES), jnp.bfloat16),
        in_specs=[VMEM],
        out_specs=VMEM,
        compiler_params=params,
    )(pos_weight)
    taps = lax.all_to_all(tap_copies, "dp", 0, 0, axis_index_groups=along_z, tiled=True)

    sent = pl.pallas_call(
        functools.partial(front_kernel, utts, frames, parts),
        out_shape=jax.ShapeDtypeStruct((parts, utts, frames * width), jnp.bfloat16),
        in_specs=[ANY] * 3,
        out_specs=VMEM,
        scratch_shapes=[
            pltpu.VMEM((utts * slice_rows, channels), jnp.bfloat16),
            pltpu.VMEM(conv_weight.shape, jnp.bfloat16),
            pltpu.VMEM(proj_weight.shape, jnp.bfloat16),
            pltpu.SemaphoreType.DMA((3,)),
        ],
        compiler_params=pltpu.CompilerParams(vmem_limit_bytes=66900000),
    )(features.reshape(utts * slice_rows, channels), conv_weight, proj_weight)
    taps, sent = lax.optimization_barrier((taps, sent))
    one, minus_one = send(taps, ring, 1), send(taps, ring, -1)
    spread = lax.all_to_all(sent, "mp", split_axis=0, concat_axis=0, tiled=True)
    one, minus_one, spread = lax.optimization_barrier((one, minus_one, spread))
    two, minus_two = send(one, ring, 1), send(minus_one, ring, -1)

    ordered = pl.pallas_call(
        order_kernel,
        out_shape=jax.ShapeDtypeStruct((owners * 8, 2 * width), jnp.bfloat16),
        in_specs=[VMEM] * 2,
        out_specs=VMEM,
        compiler_params=params,
    )(pack_order.reshape(1, -1), spread.reshape(parts * utts, frames * width))
    two, minus_two, _ = lax.optimization_barrier((two, minus_two, ordered))
    three, minus_three = send(two, ring, 1), send(minus_two, ring, -1)
    low, high = send(two[: ring // 2], ring, 2), send(minus_two[ring // 2 :], ring, -2)
    taps = (taps, one, two, three, low, high, minus_three, minus_two, minus_one)
    pair_rows = lax.all_to_all(
        ordered.reshape(owners, 8, 2 * width), "dp", split_axis=0, concat_axis=0, tiled=True
    )

    reach = total + GAP + 16
    length = reach + 2 * half - STEP
    group = width // 2
    scalars = (owner, pack_order, utt_len)
    shifted, packed = pl.pallas_call(
        functools.partial(place_kernel, total, half),
        out_shape=[
            jax.ShapeDtypeStruct((2, length, 768), jnp.bfloat16),
            jax.ShapeDtypeStruct((2, total, group), jnp.float32),
        ],
        in_specs=[SMEM, SMEM, SMEM, VMEM],
        out_specs=[VMEM] * 2,
        scratch_shapes=[pltpu.VMEM((2, length + STEP, group), jnp.float32)],
        compiler_params=params,
    )(*scalars, pair_rows.reshape(owners * 8, 2 * width))
    convolve = lambda swap: pl.pallas_call(
        functools.partial(positional_kernel, swap),
        out_shape=jax.ShapeDtypeStruct((group if swap else width, total), jnp.bfloat16),
        in_specs=[SMEM, SMEM, SMEM, VMEM, VMEM] + [VMEM] * len(taps),
        out_specs=VMEM,
        scratch_shapes=[pltpu.VMEM((reach, 256), jnp.float32)],
        compiler_params=params,
    )
    other = convolve(True)(*scalars, shifted, packed, *taps)
    packed, other = lax.optimization_barrier((packed, other))
    received = lax.ppermute(other, "dp", [(o, o ^ 1) for o in range(owners)])
    own = convolve(False)(*scalars, shifted, packed, *taps)
    hidden = pl.pallas_call(
        join_kernel,
        out_shape=jax.ShapeDtypeStruct((width, total), jnp.bfloat16),
        in_specs=[SMEM, ANY, ANY],
        out_specs=ANY,
        scratch_shapes=[pltpu.SemaphoreType.DMA],
        input_output_aliases={2: 0},
        compiler_params=params,
    )(owner, received, own)
    return hidden.T


def solution(mesh):
    in_specs = (P("mp", "dp", None), P(), P(), P("dp", "mp", None, None), P(), P())
    out_specs = P("dp", "mp")
    return jax.shard_map(shards, mesh=mesh, in_specs=in_specs, out_specs=out_specs, check_vma=False)
```

```python
import functools

import jax
import jax.numpy as jnp
from jax import lax
from jax.experimental import pallas as pl
from jax.experimental.pallas import tpu as pltpu
from jax.sharding import PartitionSpec as P

HOP = 320
EPS = 1e-05
LANES = 128
TAP_ROWS = 112
GAP = 64
STEP = 16


def iota(shape, dim):
    return lax.broadcasted_iota(jnp.int32, shape, dim)


def one_hot(condition):
    return jnp.where(condition, 1.0, 0.0).astype(jnp.bfloat16)


def dot(a, b, contract=((1,), (0,))):
    return lax.dot_general(a, b, (contract, ((), ())), preferred_element_type=jnp.float32)


def layer_norm(values):
    average = jnp.mean(values, axis=-1, keepdims=True)
    centred = values - average
    variance = jnp.mean(centred * centred, axis=-1, keepdims=True)
    return centred * lax.rsqrt(variance + EPS)


def gelu(values):
    return 0.5 * values * (1.0 + lax.erf(values * (0.5**0.5)))


def pack_taps_kernel(taps_ref, out_ref):
    packed = []
    for g in range(2):
        rest = taps_ref[1, g, :, 48:80]
        packed.append(
            jnp.concatenate(
                [
                    jnp.concatenate([taps_ref[0, g], taps_ref[1, g, :, 0:48]], axis=1),
                    jnp.concatenate([rest[16 * r : 16 * r + 16] for r in range(4)], axis=1),
                    jnp.concatenate([rest[64:80], jnp.zeros((16, 96), rest.dtype)], axis=1),
                ],
                axis=0,
            )
        )
    for device in range(out_ref.shape[0]):
        out_ref[device] = packed[device % 2]


def front_kernel(utts, frames, parts, features_hbm, conv_hbm, proj_hbm, out_ref, features_ref, conv_ref, proj_ref, sems):
    copies = [
        pltpu.make_async_copy(source, target, sems.at[n])
        for n, (source, target) in enumerate(
            [(features_hbm, features_ref), (conv_hbm, conv_ref), (proj_hbm, proj_ref)]
        )
    ]
    for copy in copies:
        copy.start()
    rows = utts * frames
    copies[0].wait()
    features = features_ref[...]
    row = iota((rows, 2 * rows), 0)
    column = iota((rows, 2 * rows), 1)
    source = (row % utts) * (2 * frames) + 2 * (row // utts)
    first = dot(one_hot(column == source), features).astype(jnp.bfloat16)
    second = dot(one_hot(column == source + 1), features).astype(jnp.bfloat16)
    copies[1].wait()
    conv_out = dot(first, conv_ref[0]) + dot(second, conv_ref[1])
    hidden = gelu(layer_norm(conv_out)).astype(jnp.bfloat16)
    normed = layer_norm(hidden.astype(jnp.float32)).astype(jnp.bfloat16)
    copies[2].wait()
    projected = dot(normed, proj_ref[...]).astype(jnp.bfloat16)
    group = projected.shape[1] // (2 * parts)
    for part in range(parts):
        pieces = [
            projected[f * utts : (f + 1) * utts, (2 * part + g) * group : (2 * part + g + 1) * group]
            for g in range(2)
            for f in range(frames)
        ]
        out_ref[part] = jnp.concatenate(pieces, axis=1)


def order_kernel(order_ref, spread_ref, out_ref):
    utts, lanes = spread_ref.shape
    rows, width = out_ref.shape
    width //= 2
    chosen = one_hot(iota((utts, utts), 0) == order_ref[...])
    ordered = dot(chosen, spread_ref[...], ((0,), (0,))).astype(jnp.bfloat16)
    row = iota((rows, utts), 0)
    eighth = (row // 8) % 2 * 4 + row % 4
    slot = row // 16 * 4 + row // 4 % 2
    for which in range(2):
        same = slot + 2 * which == iota((rows, utts), 1)
        total = None
        for e in range(0, lanes // width, 2):
            left = jnp.concatenate([one_hot(same & (eighth == e + n)) for n in range(2)], axis=1)
            right = [ordered[:, (e + n) * width : (e + n + 1) * width] for n in range(2)]
            term = dot(left, jnp.concatenate(right, axis=0))
            total = term if total is None else total + term
        out_ref[:, which * width : (which + 1) * width] = total.astype(out_ref.dtype)


def pair_lengths(owner_ref, order_ref, len_ref):
    slot = owner_ref[0] // 2 * 4
    return [[len_ref[order_ref[slot + 2 * which + n]] // HOP for n in range(2)] for which in range(2)]


def place_kernel(total, half, owner_ref, order_ref, len_ref, rows_ref, shifted_ref, packed_ref, placed):
    lengths = pair_lengths(owner_ref, order_ref, len_ref)
    _, spots, group = placed.shape
    columns = rows_ref.shape[0]
    column = iota((1, columns), 1)
    is_first = (column // 4) % 2 == 0
    spot = iota((spots, columns), 0)
    for which in range(2):
        first_len, second_len = lengths[which]
        acc = None
        for odd in range(2):
            frame = (column // 8) * 8 + (column % 4) * 2 + odd
            target = jnp.where(is_first, frame, frame + first_len + GAP) + half
            valid = frame < jnp.where(is_first, first_len, second_len)
            target = jnp.where(valid, target, -1)
            lane = (2 * which + odd) * group
            term = dot(one_hot(spot == target), rows_ref[:, lane : lane + group])
            acc = term if acc is None else acc + term
        placed[which] = acc

    length = shifted_ref.shape[1]
    for which in range(2):
        for third in range(3):
            pairs = [k for k in range(3 * third, 3 * third + 3) if k < 8]
            pieces = [placed[which, 2 * k : 2 * k + length, :].astype(jnp.bfloat16) for k in pairs]
            pieces.append(jnp.zeros((length, 256 - group * len(pairs)), jnp.bfloat16))
            shifted_ref[which, :, third * 256 : (third + 1) * 256] = jnp.concatenate(pieces, axis=1)
        packed_ref[which] = jnp.where(
            iota((total, 1), 0) < lengths[which][0],
            placed[which, half : half + total, :],
            placed[which, half + GAP : half + GAP + total, :],
        )


def positional_kernel(
    swap, owner_ref, order_ref, len_ref, shifted_ref, packed_ref, *refs
):
    taps_refs, (out_ref, sums) = refs[:-2], refs[-2:]
    parity = owner_ref[0] % 2
    which = 1 - parity if swap else parity
    ring = taps_refs[0].shape[0]
    blocks = [[(ref, n) for n in range(ring)] for ref in taps_refs[:4] + taps_refs[6:]]
    blocks.insert(4, [(ref, n) for ref in taps_refs[4:6] for n in range(ring // 2)])
    slot = 2 * (owner_ref[0] - parity + which)
    first_len = len_ref[order_ref[slot]] // HOP
    second_len = len_ref[order_ref[slot + 1]] // HOP
    _, total, group = packed_ref.shape
    reach = sums.shape[0]

    for away, pieces in enumerate(blocks):
        start = pl.multiple_of(lax.rem(owner_ref[0] // ring + ring - away, ring) * STEP, STEP)
        left, right = [], []
        for slot in range(9):
            taps_ref, piece = pieces[min(slot, 7)]
            size = 96 if slot % 3 == 2 else 80
            left.append(taps_ref[piece, 0:size, :])
            fold = taps_ref[piece, 80:96, :]
            right += [fold] + [jnp.roll(fold, -32 * r, axis=1) for r in range(1, 4)]
            right.append(taps_ref[piece, 96:112, :])
            if size == 96:
                right.append(fold)
        matrix = jnp.concatenate([jnp.concatenate(left, axis=0), jnp.concatenate(right, axis=0)], axis=1)
        term = dot(shifted_ref[which, pl.ds(start, reach), :], matrix)
        sums[...] = term if away == 0 else sums[...] + term

    spot = iota((total, 1), 0)
    near = sums[0:total, 0:group] + sums[1 : total + 1, group : 2 * group]
    far = sums[GAP : GAP + total, 0:group] + sums[GAP + 1 : GAP + total + 1, group : 2 * group]
    conv_sum = jnp.where(spot < first_len + second_len, jnp.where(spot < first_len, near, far), 0.0)
    hidden = packed_ref[which] + gelu(conv_sum)
    hidden = jnp.concatenate([hidden, jnp.zeros((total, -group % LANES), jnp.float32)], axis=1)
    start = 0 if swap else pl.multiple_of(parity * group, 16)
    out_ref[pl.ds(start, group), :] = hidden.T[:group].astype(out_ref.dtype)


def join_kernel(owner_ref, received_hbm, own_hbm, out_hbm, sem):
    group = received_hbm.shape[0]
    start = pl.multiple_of((1 - owner_ref[0] % 2) * group, 16)
    copy = pltpu.make_async_copy(received_hbm, out_hbm.at[pl.ds(start, group), :], sem)
    copy.start()
    copy.wait()


VMEM = pl.BlockSpec(memory_space=pltpu.VMEM)
SMEM = pl.BlockSpec(memory_space=pltpu.SMEM)
ANY = pl.BlockSpec(memory_space=pl.ANY)


def send(values, ring, step):
    return lax.ppermute(values, "dp", [(o, (o + step * ring) % (ring * ring)) for o in range(ring * ring)])


def shards(features, conv_weight, proj_weight, pos_weight, utt_len, pack_order):
    owners = lax.axis_size("dp")
    parts = lax.axis_size("mp")
    utts, slice_rows, channels = features.shape
    frames = slice_rows // 2
    model_width = proj_weight.shape[1]
    width = model_width // parts
    total = frames * owners
    half = pos_weight.shape[0] * owners // 2
    params = pltpu.CompilerParams(vmem_limit_bytes=48 * 1024 * 1024)
    large = pltpu.CompilerParams(vmem_limit_bytes=62 * 1024 * 1024)

    owner = lax.axis_index("dp").reshape(1)
    ring = round(owners**0.5)
    along_z = [[y * ring + z for z in range(ring)] for y in range(ring)]
    tap_copies = pl.pallas_call(
        pack_taps_kernel,
        out_shape=jax.ShapeDtypeStruct((ring, TAP_ROWS, LANES), jnp.bfloat16),
        in_specs=[VMEM],
        out_specs=VMEM,
        compiler_params=params,
    )(pos_weight)
    taps = lax.all_to_all(tap_copies, "dp", 0, 0, axis_index_groups=along_z, tiled=True)

    sent = pl.pallas_call(
        functools.partial(front_kernel, utts, frames, parts),
        out_shape=jax.ShapeDtypeStruct((parts, utts, frames * width), jnp.bfloat16),
        in_specs=[ANY] * 3,
        out_specs=VMEM,
        scratch_shapes=[
            pltpu.VMEM((utts * slice_rows, channels), jnp.bfloat16),
            pltpu.VMEM(conv_weight.shape, jnp.bfloat16),
            pltpu.VMEM(proj_weight.shape, jnp.bfloat16),
            pltpu.SemaphoreType.DMA((3,)),
        ],
        compiler_params=pltpu.CompilerParams(vmem_limit_bytes=66900000),
    )(features.reshape(utts * slice_rows, channels), conv_weight, proj_weight)
    taps, sent = lax.optimization_barrier((taps, sent))
    one, minus_one, two, minus_two = [send(taps, ring, step) for step in (1, -1, 2, -2)]
    spread = lax.all_to_all(sent, "mp", split_axis=0, concat_axis=0, tiled=True)

    ordered = pl.pallas_call(
        order_kernel,
        out_shape=jax.ShapeDtypeStruct((owners * 8, 2 * width), jnp.bfloat16),
        in_specs=[VMEM] * 2,
        out_specs=VMEM,
        compiler_params=params,
    )(pack_order.reshape(1, -1), spread.reshape(parts * utts, frames * width))
    two, minus_two, _ = lax.optimization_barrier((two, minus_two, ordered))
    three, minus_three = send(two, ring, 1), send(minus_two, ring, -1)
    low, high = send(two[: ring // 2], ring, 2), send(minus_two[ring // 2 :], ring, -2)
    taps = (taps, one, two, three, low, high, minus_three, minus_two, minus_one)
    pair_rows = lax.all_to_all(
        ordered.reshape(owners, 8, 2 * width), "dp", split_axis=0, concat_axis=0, tiled=True
    )

    reach = total + GAP + 16
    length = reach + 2 * half - STEP
    group = width // 2
    scalars = (owner, pack_order, utt_len)
    shifted, packed = pl.pallas_call(
        functools.partial(place_kernel, total, half),
        out_shape=[
            jax.ShapeDtypeStruct((2, length, 768), jnp.bfloat16),
            jax.ShapeDtypeStruct((2, total, group), jnp.float32),
        ],
        in_specs=[SMEM, SMEM, SMEM, VMEM],
        out_specs=[VMEM] * 2,
        scratch_shapes=[pltpu.VMEM((2, length + STEP, group), jnp.float32)],
        compiler_params=params,
    )(*scalars, pair_rows.reshape(owners * 8, 2 * width))
    convolve = lambda swap: pl.pallas_call(
        functools.partial(positional_kernel, swap),
        out_shape=jax.ShapeDtypeStruct((group if swap else width, total), jnp.bfloat16),
        in_specs=[SMEM, SMEM, SMEM, VMEM, VMEM] + [VMEM] * len(taps),
        out_specs=VMEM,
        scratch_shapes=[pltpu.VMEM((reach, 256), jnp.float32)],
        compiler_params=params,
    )
    other = convolve(True)(*scalars, shifted, packed, *taps)
    packed, other = lax.optimization_barrier((packed, other))
    received = lax.ppermute(other, "dp", [(o, o ^ 1) for o in range(owners)])
    own = convolve(False)(*scalars, shifted, packed, *taps)
    hidden = pl.pallas_call(
        join_kernel,
        out_shape=jax.ShapeDtypeStruct((width, total), jnp.bfloat16),
        in_specs=[SMEM, ANY, ANY],
        out_specs=ANY,
        scratch_shapes=[pltpu.SemaphoreType.DMA],
        input_output_aliases={2: 0},
        compiler_params=params,
    )(owner, received, own)
    return hidden.T


def solution(mesh):
    in_specs = (P("mp", "dp", None), P(), P(), P("dp", "mp", None, None), P(), P())
    out_specs = P("dp", "mp")
    return jax.shard_map(shards, mesh=mesh, in_specs=in_specs, out_specs=out_specs, check_vma=False)
```

```python
import functools

import jax
import jax.numpy as jnp
from jax import lax
from jax.experimental import pallas as pl
from jax.experimental.pallas import tpu as pltpu
from jax.sharding import PartitionSpec as P

HOP = 320
EPS = 1e-05
LANES = 128
TAP_ROWS = 112
GAP = 64
STEP = 16


def iota(shape, dim):
    return lax.broadcasted_iota(jnp.int32, shape, dim)


def one_hot(condition):
    return jnp.where(condition, 1.0, 0.0).astype(jnp.bfloat16)


def dot(a, b, contract=((1,), (0,))):
    return lax.dot_general(a, b, (contract, ((), ())), preferred_element_type=jnp.float32)


def layer_norm(values):
    average = jnp.mean(values, axis=-1, keepdims=True)
    centred = values - average
    variance = jnp.mean(centred * centred, axis=-1, keepdims=True)
    return centred * lax.rsqrt(variance + EPS)


def gelu(values):
    return 0.5 * values * (1.0 + lax.erf(values * (0.5**0.5)))


def pack_taps_kernel(taps_ref, out_ref):
    packed = []
    for g in range(2):
        rest = taps_ref[1, g, :, 48:80]
        packed.append(
            jnp.concatenate(
                [
                    jnp.concatenate([taps_ref[0, g], taps_ref[1, g, :, 0:48]], axis=1),
                    jnp.concatenate([rest[16 * r : 16 * r + 16] for r in range(4)], axis=1),
                    jnp.concatenate([rest[64:80], jnp.zeros((16, 96), rest.dtype)], axis=1),
                ],
                axis=0,
            )
        )
    for device in range(out_ref.shape[0]):
        out_ref[device] = packed[device % 2]


def front_kernel(utts, frames, parts, features_hbm, conv_hbm, proj_hbm, out_ref, features_ref, conv_ref, proj_ref, sems):
    copies = [
        pltpu.make_async_copy(source, target, sems.at[n])
        for n, (source, target) in enumerate(
            [(features_hbm, features_ref), (conv_hbm, conv_ref), (proj_hbm, proj_ref)]
        )
    ]
    for copy in copies:
        copy.start()
    rows = utts * frames
    copies[0].wait()
    features = features_ref[...]
    row = iota((rows, 2 * rows), 0)
    column = iota((rows, 2 * rows), 1)
    source = (row % utts) * (2 * frames) + 2 * (row // utts)
    first = dot(one_hot(column == source), features).astype(jnp.bfloat16)
    second = dot(one_hot(column == source + 1), features).astype(jnp.bfloat16)
    copies[1].wait()
    conv_out = dot(first, conv_ref[0]) + dot(second, conv_ref[1])
    hidden = gelu(layer_norm(conv_out)).astype(jnp.bfloat16)
    normed = layer_norm(hidden.astype(jnp.float32)).astype(jnp.bfloat16)
    copies[2].wait()
    projected = dot(normed, proj_ref[...]).astype(jnp.bfloat16)
    group = projected.shape[1] // (2 * parts)
    for part in range(parts):
        pieces = [
            projected[f * utts : (f + 1) * utts, (2 * part + g) * group : (2 * part + g + 1) * group]
            for g in range(2)
            for f in range(frames)
        ]
        out_ref[part] = jnp.concatenate(pieces, axis=1)


def order_kernel(order_ref, spread_ref, out_ref):
    utts, lanes = spread_ref.shape
    rows, width = out_ref.shape
    width //= 2
    chosen = one_hot(iota((utts, utts), 0) == order_ref[...])
    ordered = dot(chosen, spread_ref[...], ((0,), (0,))).astype(jnp.bfloat16)
    row = iota((rows, utts), 0)
    eighth = (row // 8) % 2 * 4 + row % 4
    slot = row // 16 * 4 + row // 4 % 2
    for which in range(2):
        same = slot + 2 * which == iota((rows, utts), 1)
        total = None
        for e in range(0, lanes // width, 2):
            left = jnp.concatenate([one_hot(same & (eighth == e + n)) for n in range(2)], axis=1)
            right = [ordered[:, (e + n) * width : (e + n + 1) * width] for n in range(2)]
            term = dot(left, jnp.concatenate(right, axis=0))
            total = term if total is None else total + term
        out_ref[:, which * width : (which + 1) * width] = total.astype(out_ref.dtype)


def pair_lengths(owner_ref, order_ref, len_ref):
    slot = owner_ref[0] // 2 * 4
    return [[len_ref[order_ref[slot + 2 * which + n]] // HOP for n in range(2)] for which in range(2)]


def place_kernel(total, half, owner_ref, order_ref, len_ref, rows_ref, shifted_ref, packed_ref, placed):
    lengths = pair_lengths(owner_ref, order_ref, len_ref)
    _, spots, group = placed.shape
    columns = rows_ref.shape[0]
    column = iota((1, columns), 1)
    is_first = (column // 4) % 2 == 0
    spot = iota((spots, columns), 0)
    for which in range(2):
        first_len, second_len = lengths[which]
        acc = None
        for odd in range(2):
            frame = (column // 8) * 8 + (column % 4) * 2 + odd
            target = jnp.where(is_first, frame, frame + first_len + GAP) + half
            valid = frame < jnp.where(is_first, first_len, second_len)
            target = jnp.where(valid, target, -1)
            lane = (2 * which + odd) * group
            term = dot(one_hot(spot == target), rows_ref[:, lane : lane + group])
            acc = term if acc is None else acc + term
        placed[which] = acc

    length = shifted_ref.shape[1]
    for which in range(2):
        for third in range(3):
            pairs = [k for k in range(3 * third, 3 * third + 3) if k < 8]
            pieces = [placed[which, 2 * k : 2 * k + length, :].astype(jnp.bfloat16) for k in pairs]
            pieces.append(jnp.zeros((length, 256 - group * len(pairs)), jnp.bfloat16))
            shifted_ref[which, :, third * 256 : (third + 1) * 256] = jnp.concatenate(pieces, axis=1)
        packed_ref[which] = jnp.where(
            iota((total, 1), 0) < lengths[which][0],
            placed[which, half : half + total, :],
            placed[which, half + GAP : half + GAP + total, :],
        )


def positional_kernel(
    swap, owner_ref, order_ref, len_ref, shifted_ref, packed_ref, *refs
):
    taps_refs, (out_ref, sums) = refs[:-2], refs[-2:]
    parity = owner_ref[0] % 2
    which = 1 - parity if swap else parity
    ring = taps_refs[0].shape[0]
    blocks = [[(ref, n) for n in range(ring)] for ref in taps_refs[:4] + taps_refs[6:]]
    blocks.insert(4, [(ref, n) for ref in taps_refs[4:6] for n in range(ring // 2)])
    slot = 2 * (owner_ref[0] - parity + which)
    first_len = len_ref[order_ref[slot]] // HOP
    second_len = len_ref[order_ref[slot + 1]] // HOP
    _, total, group = packed_ref.shape
    reach = sums.shape[0]

    for away, pieces in enumerate(blocks):
        start = pl.multiple_of(lax.rem(owner_ref[0] // ring + ring - away, ring) * STEP, STEP)
        left, right = [], []
        for slot in range(9):
            taps_ref, piece = pieces[min(slot, 7)]
            size = 96 if slot % 3 == 2 else 80
            left.append(taps_ref[piece, 0:size, :])
            fold = taps_ref[piece, 80:96, :]
            right += [fold] + [jnp.roll(fold, -32 * r, axis=1) for r in range(1, 4)]
            right.append(taps_ref[piece, 96:112, :])
            if size == 96:
                right.append(fold)
        matrix = jnp.concatenate([jnp.concatenate(left, axis=0), jnp.concatenate(right, axis=0)], axis=1)
        term = dot(shifted_ref[which, pl.ds(start, reach), :], matrix)
        sums[...] = term if away == 0 else sums[...] + term

    spot = iota((total, 1), 0)
    near = sums[0:total, 0:group] + sums[1 : total + 1, group : 2 * group]
    far = sums[GAP : GAP + total, 0:group] + sums[GAP + 1 : GAP + total + 1, group : 2 * group]
    conv_sum = jnp.where(spot < first_len + second_len, jnp.where(spot < first_len, near, far), 0.0)
    hidden = packed_ref[which] + gelu(conv_sum)
    hidden = jnp.concatenate([hidden, jnp.zeros((total, -group % LANES), jnp.float32)], axis=1)
    start = 0 if swap else pl.multiple_of(parity * group, 16)
    out_ref[pl.ds(start, group), :] = hidden.T[:group].astype(out_ref.dtype)


def join_kernel(owner_ref, received_hbm, own_hbm, out_hbm, sem):
    group = received_hbm.shape[0]
    start = pl.multiple_of((1 - owner_ref[0] % 2) * group, 16)
    copy = pltpu.make_async_copy(received_hbm, out_hbm.at[pl.ds(start, group), :], sem)
    copy.start()
    copy.wait()


VMEM = pl.BlockSpec(memory_space=pltpu.VMEM)
SMEM = pl.BlockSpec(memory_space=pltpu.SMEM)
ANY = pl.BlockSpec(memory_space=pl.ANY)


def send(values, ring, step):
    return lax.ppermute(values, "dp", [(o, (o + step * ring) % (ring * ring)) for o in range(ring * ring)])


def shards(features, conv_weight, proj_weight, pos_weight, utt_len, pack_order):
    owners = lax.axis_size("dp")
    parts = lax.axis_size("mp")
    utts, slice_rows, channels = features.shape
    frames = slice_rows // 2
    model_width = proj_weight.shape[1]
    width = model_width // parts
    total = frames * owners
    half = pos_weight.shape[0] * owners // 2
    params = pltpu.CompilerParams(vmem_limit_bytes=48 * 1024 * 1024)
    large = pltpu.CompilerParams(vmem_limit_bytes=62 * 1024 * 1024)

    owner = lax.axis_index("dp").reshape(1)
    ring = round(owners**0.5)
    along_z = [[y * ring + z for z in range(ring)] for y in range(ring)]
    tap_copies = pl.pallas_call(
        pack_taps_kernel,
        out_shape=jax.ShapeDtypeStruct((ring, TAP_ROWS, LANES), jnp.bfloat16),
        in_specs=[VMEM],
        out_specs=VMEM,
        compiler_params=params,
    )(pos_weight)
    taps = lax.all_to_all(tap_copies, "dp", 0, 0, axis_index_groups=along_z, tiled=True)

    sent = pl.pallas_call(
        functools.partial(front_kernel, utts, frames, parts),
        out_shape=jax.ShapeDtypeStruct((parts, utts, frames * width), jnp.bfloat16),
        in_specs=[ANY] * 3,
        out_specs=VMEM,
        scratch_shapes=[
            pltpu.VMEM((utts * slice_rows, channels), jnp.bfloat16),
            pltpu.VMEM(conv_weight.shape, jnp.bfloat16),
            pltpu.VMEM(proj_weight.shape, jnp.bfloat16),
            pltpu.SemaphoreType.DMA((3,)),
        ],
        compiler_params=pltpu.CompilerParams(vmem_limit_bytes=66900000),
    )(features.reshape(utts * slice_rows, channels), conv_weight, proj_weight)
    taps, sent = lax.optimization_barrier((taps, sent))
    one, minus_one, two, minus_two = [send(taps, ring, step) for step in (1, -1, 2, -2)]
    spread = lax.all_to_all(sent, "mp", split_axis=0, concat_axis=0, tiled=True)

    ordered = pl.pallas_call(
        order_kernel,
        out_shape=jax.ShapeDtypeStruct((owners * 8, 2 * width), jnp.bfloat16),
        in_specs=[VMEM] * 2,
        out_specs=VMEM,
        compiler_params=params,
    )(pack_order.reshape(1, -1), spread.reshape(parts * utts, frames * width))
    one, minus_one, two, minus_two, ordered = lax.optimization_barrier((one, minus_one, two, minus_two, ordered))
    three, minus_three = send(two, ring, 1), send(minus_two, ring, -1)
    low, high = send(two[: ring // 2], ring, 2), send(minus_two[ring // 2 :], ring, -2)
    taps = (taps, one, two, three, low, high, minus_three, minus_two, minus_one)
    pair_rows = lax.all_to_all(
        ordered.reshape(owners, 8, 2 * width), "dp", split_axis=0, concat_axis=0, tiled=True
    )

    reach = total + GAP + 16
    length = reach + 2 * half - STEP
    group = width // 2
    scalars = (owner, pack_order, utt_len)
    shifted, packed = pl.pallas_call(
        functools.partial(place_kernel, total, half),
        out_shape=[
            jax.ShapeDtypeStruct((2, length, 768), jnp.bfloat16),
            jax.ShapeDtypeStruct((2, total, group), jnp.float32),
        ],
        in_specs=[SMEM, SMEM, SMEM, VMEM],
        out_specs=[VMEM] * 2,
        scratch_shapes=[pltpu.VMEM((2, length + STEP, group), jnp.float32)],
        compiler_params=params,
    )(*scalars, pair_rows.reshape(owners * 8, 2 * width))
    convolve = lambda swap: pl.pallas_call(
        functools.partial(positional_kernel, swap),
        out_shape=jax.ShapeDtypeStruct((group if swap else width, total), jnp.bfloat16),
        in_specs=[SMEM, SMEM, SMEM, VMEM, VMEM] + [VMEM] * len(taps),
        out_specs=VMEM,
        scratch_shapes=[pltpu.VMEM((reach, 256), jnp.float32)],
        compiler_params=params,
    )
    other = convolve(True)(*scalars, shifted, packed, *taps)
    packed, other = lax.optimization_barrier((packed, other))
    received = lax.ppermute(other, "dp", [(o, o ^ 1) for o in range(owners)])
    own = convolve(False)(*scalars, shifted, packed, *taps)
    hidden = pl.pallas_call(
        join_kernel,
        out_shape=jax.ShapeDtypeStruct((width, total), jnp.bfloat16),
        in_specs=[SMEM, ANY, ANY],
        out_specs=ANY,
        scratch_shapes=[pltpu.SemaphoreType.DMA],
        input_output_aliases={2: 0},
        compiler_params=params,
    )(owner, received, own)
    return hidden.T


def solution(mesh):
    in_specs = (P("mp", "dp", None), P(), P(), P("dp", "mp", None, None), P(), P())
    out_specs = P("dp", "mp")
    return jax.shard_map(shards, mesh=mesh, in_specs=in_specs, out_specs=out_specs, check_vma=False)
```

```python
import functools

import jax
import jax.numpy as jnp
from jax import lax
from jax.experimental import pallas as pl
from jax.experimental.pallas import tpu as pltpu
from jax.sharding import PartitionSpec as P

HOP = 320
EPS = 1e-05
LANES = 128
TAP_ROWS = 112
GAP = 64
STEP = 16


def iota(shape, dim):
    return lax.broadcasted_iota(jnp.int32, shape, dim)


def one_hot(condition):
    return jnp.where(condition, 1.0, 0.0).astype(jnp.bfloat16)


def dot(a, b, contract=((1,), (0,))):
    return lax.dot_general(a, b, (contract, ((), ())), preferred_element_type=jnp.float32)


def layer_norm(values):
    average = jnp.mean(values, axis=-1, keepdims=True)
    centred = values - average
    variance = jnp.mean(centred * centred, axis=-1, keepdims=True)
    return centred * lax.rsqrt(variance + EPS)


def gelu(values):
    return 0.5 * values * (1.0 + lax.erf(values * (0.5**0.5)))


def pack_taps_kernel(taps_ref, out_ref):
    packed = []
    for g in range(2):
        rest = taps_ref[1, g, :, 48:80]
        packed.append(
            jnp.concatenate(
                [
                    jnp.concatenate([taps_ref[0, g], taps_ref[1, g, :, 0:48]], axis=1),
                    jnp.concatenate([rest[16 * r : 16 * r + 16] for r in range(4)], axis=1),
                    jnp.concatenate([rest[64:80], jnp.zeros((16, 96), rest.dtype)], axis=1),
                ],
                axis=0,
            )
        )
    for device in range(out_ref.shape[0]):
        out_ref[device] = packed[device % 2]


def front_kernel(utts, frames, parts, features_hbm, conv_hbm, proj_hbm, out_ref, features_ref, conv_ref, proj_ref, sems):
    copies = [
        pltpu.make_async_copy(source, target, sems.at[n])
        for n, (source, target) in enumerate(
            [(features_hbm, features_ref), (conv_hbm, conv_ref), (proj_hbm, proj_ref)]
        )
    ]
    for copy in copies:
        copy.start()
    rows = utts * frames
    copies[0].wait()
    features = features_ref[...]
    row = iota((rows, 2 * rows), 0)
    column = iota((rows, 2 * rows), 1)
    source = (row % utts) * (2 * frames) + 2 * (row // utts)
    first = dot(one_hot(column == source), features).astype(jnp.bfloat16)
    second = dot(one_hot(column == source + 1), features).astype(jnp.bfloat16)
    copies[1].wait()
    conv_out = dot(first, conv_ref[0]) + dot(second, conv_ref[1])
    hidden = gelu(layer_norm(conv_out)).astype(jnp.bfloat16)
    normed = layer_norm(hidden.astype(jnp.float32)).astype(jnp.bfloat16)
    copies[2].wait()
    projected = dot(normed, proj_ref[...]).astype(jnp.bfloat16)
    group = projected.shape[1] // (2 * parts)
    for part in range(parts):
        pieces = [
            projected[f * utts : (f + 1) * utts, (2 * part + g) * group : (2 * part + g + 1) * group]
            for g in range(2)
            for f in range(frames)
        ]
        out_ref[part] = jnp.concatenate(pieces, axis=1)


def order_kernel(order_ref, spread_ref, out_ref):
    utts, lanes = spread_ref.shape
    rows, width = out_ref.shape
    width //= 2
    chosen = one_hot(iota((utts, utts), 0) == order_ref[...])
    ordered = dot(chosen, spread_ref[...], ((0,), (0,))).astype(jnp.bfloat16)
    row = iota((rows, utts), 0)
    eighth = (row // 8) % 2 * 4 + row % 4
    slot = row // 16 * 4 + row // 4 % 2
    for which in range(2):
        same = slot + 2 * which == iota((rows, utts), 1)
        total = None
        for e in range(0, lanes // width, 2):
            left = jnp.concatenate([one_hot(same & (eighth == e + n)) for n in range(2)], axis=1)
            right = [ordered[:, (e + n) * width : (e + n + 1) * width] for n in range(2)]
            term = dot(left, jnp.concatenate(right, axis=0))
            total = term if total is None else total + term
        out_ref[:, which * width : (which + 1) * width] = total.astype(out_ref.dtype)


def pair_lengths(owner_ref, order_ref, len_ref):
    slot = owner_ref[0] // 2 * 4
    return [[len_ref[order_ref[slot + 2 * which + n]] // HOP for n in range(2)] for which in range(2)]


def place_kernel(total, half, owner_ref, order_ref, len_ref, rows_ref, shifted_ref, packed_ref, placed):
    lengths = pair_lengths(owner_ref, order_ref, len_ref)
    _, spots, group = placed.shape
    columns = rows_ref.shape[0]
    column = iota((1, columns), 1)
    is_first = (column // 4) % 2 == 0
    spot = iota((spots, columns), 0)
    for which in range(2):
        first_len, second_len = lengths[which]
        acc = None
        for odd in range(2):
            frame = (column // 8) * 8 + (column % 4) * 2 + odd
            target = jnp.where(is_first, frame, frame + first_len + GAP) + half
            valid = frame < jnp.where(is_first, first_len, second_len)
            target = jnp.where(valid, target, -1)
            lane = (2 * which + odd) * group
            term = dot(one_hot(spot == target), rows_ref[:, lane : lane + group])
            acc = term if acc is None else acc + term
        placed[which] = acc

    length = shifted_ref.shape[1]
    for which in range(2):
        for third in range(3):
            pairs = [k for k in range(3 * third, 3 * third + 3) if k < 8]
            pieces = [placed[which, 2 * k : 2 * k + length, :].astype(jnp.bfloat16) for k in pairs]
            pieces.append(jnp.zeros((length, 256 - group * len(pairs)), jnp.bfloat16))
            shifted_ref[which, :, third * 256 : (third + 1) * 256] = jnp.concatenate(pieces, axis=1)
        packed_ref[which] = jnp.where(
            iota((total, 1), 0) < lengths[which][0],
            placed[which, half : half + total, :],
            placed[which, half + GAP : half + GAP + total, :],
        )


def positional_kernel(
    swap, owner_ref, order_ref, len_ref, shifted_ref, packed_ref, *refs
):
    taps_refs, (out_ref, sums) = refs[:-2], refs[-2:]
    parity = owner_ref[0] % 2
    which = 1 - parity if swap else parity
    ring = taps_refs[0].shape[0]
    blocks = [[(ref, n) for n in range(ring)] for ref in taps_refs[:4] + taps_refs[6:]]
    blocks.insert(4, [(ref, n) for ref in taps_refs[4:6] for n in range(ring // 2)])
    slot = 2 * (owner_ref[0] - parity + which)
    first_len = len_ref[order_ref[slot]] // HOP
    second_len = len_ref[order_ref[slot + 1]] // HOP
    _, total, group = packed_ref.shape
    reach = sums.shape[0]

    for away, pieces in enumerate(blocks):
        start = pl.multiple_of(lax.rem(owner_ref[0] // ring + ring - away, ring) * STEP, STEP)
        left, right = [], []
        for slot in range(9):
            taps_ref, piece = pieces[min(slot, 7)]
            size = 96 if slot % 3 == 2 else 80
            left.append(taps_ref[piece, 0:size, :])
            fold = taps_ref[piece, 80:96, :]
            right += [fold] + [jnp.roll(fold, -32 * r, axis=1) for r in range(1, 4)]
            right.append(taps_ref[piece, 96:112, :])
            if size == 96:
                right.append(fold)
        matrix = jnp.concatenate([jnp.concatenate(left, axis=0), jnp.concatenate(right, axis=0)], axis=1)
        term = dot(shifted_ref[which, pl.ds(start, reach), :], matrix)
        sums[...] = term if away == 0 else sums[...] + term

    spot = iota((total, 1), 0)
    near = sums[0:total, 0:group] + sums[1 : total + 1, group : 2 * group]
    far = sums[GAP : GAP + total, 0:group] + sums[GAP + 1 : GAP + total + 1, group : 2 * group]
    conv_sum = jnp.where(spot < first_len + second_len, jnp.where(spot < first_len, near, far), 0.0)
    hidden = packed_ref[which] + gelu(conv_sum)
    hidden = jnp.concatenate([hidden, jnp.zeros((total, -group % LANES), jnp.float32)], axis=1)
    start = 0 if swap else pl.multiple_of(parity * group, 16)
    out_ref[pl.ds(start, group), :] = hidden.T[:group].astype(out_ref.dtype)


def join_kernel(owner_ref, received_hbm, own_hbm, out_hbm, sem):
    group = received_hbm.shape[0]
    start = pl.multiple_of((1 - owner_ref[0] % 2) * group, 16)
    copy = pltpu.make_async_copy(received_hbm, out_hbm.at[pl.ds(start, group), :], sem)
    copy.start()
    copy.wait()


VMEM = pl.BlockSpec(memory_space=pltpu.VMEM)
SMEM = pl.BlockSpec(memory_space=pltpu.SMEM)
ANY = pl.BlockSpec(memory_space=pl.ANY)


def send(values, ring, step):
    return lax.ppermute(values, "dp", [(o, (o + step * ring) % (ring * ring)) for o in range(ring * ring)])


def shards(features, conv_weight, proj_weight, pos_weight, utt_len, pack_order):
    owners = lax.axis_size("dp")
    parts = lax.axis_size("mp")
    utts, slice_rows, channels = features.shape
    frames = slice_rows // 2
    model_width = proj_weight.shape[1]
    width = model_width // parts
    total = frames * owners
    half = pos_weight.shape[0] * owners // 2
    params = pltpu.CompilerParams(vmem_limit_bytes=48 * 1024 * 1024)
    large = pltpu.CompilerParams(vmem_limit_bytes=62 * 1024 * 1024)

    owner = lax.axis_index("dp").reshape(1)
    ring = round(owners**0.5)
    along_z = [[y * ring + z for z in range(ring)] for y in range(ring)]
    tap_copies = pl.pallas_call(
        pack_taps_kernel,
        out_shape=jax.ShapeDtypeStruct((ring, TAP_ROWS, LANES), jnp.bfloat16),
        in_specs=[VMEM],
        out_specs=VMEM,
        compiler_params=params,
    )(pos_weight)
    taps = lax.all_to_all(tap_copies, "dp", 0, 0, axis_index_groups=along_z, tiled=True)

    sent = pl.pallas_call(
        functools.partial(front_kernel, utts, frames, parts),
        out_shape=jax.ShapeDtypeStruct((parts, utts, frames * width), jnp.bfloat16),
        in_specs=[ANY] * 3,
        out_specs=VMEM,
        scratch_shapes=[
            pltpu.VMEM((utts * slice_rows, channels), jnp.bfloat16),
            pltpu.VMEM(conv_weight.shape, jnp.bfloat16),
            pltpu.VMEM(proj_weight.shape, jnp.bfloat16),
            pltpu.SemaphoreType.DMA((3,)),
        ],
        compiler_params=pltpu.CompilerParams(vmem_limit_bytes=66900000),
    )(features.reshape(utts * slice_rows, channels), conv_weight, proj_weight)
    taps, sent = lax.optimization_barrier((taps, sent))
    two, minus_two, one, minus_one = [send(taps, ring, step) for step in (2, -2, 1, -1)]
    spread = lax.all_to_all(sent, "mp", split_axis=0, concat_axis=0, tiled=True)

    ordered = pl.pallas_call(
        order_kernel,
        out_shape=jax.ShapeDtypeStruct((owners * 8, 2 * width), jnp.bfloat16),
        in_specs=[VMEM] * 2,
        out_specs=VMEM,
        compiler_params=params,
    )(pack_order.reshape(1, -1), spread.reshape(parts * utts, frames * width))
    low, high = two[: ring // 2], minus_two[ring // 2 :]
    low, high, two, minus_two, one, minus_one, ordered = lax.optimization_barrier(
        (low, high, two, minus_two, one, minus_one, ordered)
    )
    low, high = send(low, ring, 2), send(high, ring, -2)
    three, minus_three = send(two, ring, 1), send(minus_two, ring, -1)
    taps = (taps, one, two, three, low, high, minus_three, minus_two, minus_one)
    pair_rows = lax.all_to_all(
        ordered.reshape(owners, 8, 2 * width), "dp", split_axis=0, concat_axis=0, tiled=True
    )

    reach = total + GAP + 16
    length = reach + 2 * half - STEP
    group = width // 2
    scalars = (owner, pack_order, utt_len)
    shifted, packed = pl.pallas_call(
        functools.partial(place_kernel, total, half),
        out_shape=[
            jax.ShapeDtypeStruct((2, length, 768), jnp.bfloat16),
            jax.ShapeDtypeStruct((2, total, group), jnp.float32),
        ],
        in_specs=[SMEM, SMEM, SMEM, VMEM],
        out_specs=[VMEM] * 2,
        scratch_shapes=[pltpu.VMEM((2, length + STEP, group), jnp.float32)],
        compiler_params=params,
    )(*scalars, pair_rows.reshape(owners * 8, 2 * width))
    convolve = lambda swap: pl.pallas_call(
        functools.partial(positional_kernel, swap),
        out_shape=jax.ShapeDtypeStruct((group if swap else width, total), jnp.bfloat16),
        in_specs=[SMEM, SMEM, SMEM, VMEM, VMEM] + [VMEM] * len(taps),
        out_specs=VMEM,
        scratch_shapes=[pltpu.VMEM((reach, 256), jnp.float32)],
        compiler_params=params,
    )
    other = convolve(True)(*scalars, shifted, packed, *taps)
    packed, other = lax.optimization_barrier((packed, other))
    received = lax.ppermute(other, "dp", [(o, o ^ 1) for o in range(owners)])
    own = convolve(False)(*scalars, shifted, packed, *taps)
    hidden = pl.pallas_call(
        join_kernel,
        out_shape=jax.ShapeDtypeStruct((width, total), jnp.bfloat16),
        in_specs=[SMEM, ANY, ANY],
        out_specs=ANY,
        scratch_shapes=[pltpu.SemaphoreType.DMA],
        input_output_aliases={2: 0},
        compiler_params=params,
    )(owner, received, own)
    return hidden.T


def solution(mesh):
    in_specs = (P("mp", "dp", None), P(), P(), P("dp", "mp", None, None), P(), P())
    out_specs = P("dp", "mp")
    return jax.shard_map(shards, mesh=mesh, in_specs=in_specs, out_specs=out_specs, check_vma=False)
```

```python
import functools

import jax
import jax.numpy as jnp
from jax import lax
from jax.experimental import pallas as pl
from jax.experimental.pallas import tpu as pltpu
from jax.sharding import PartitionSpec as P

HOP = 320
EPS = 1e-05
LANES = 128
TAP_ROWS = 112
GAP = 64
STEP = 16


def iota(shape, dim):
    return lax.broadcasted_iota(jnp.int32, shape, dim)


def one_hot(condition):
    return jnp.where(condition, 1.0, 0.0).astype(jnp.bfloat16)


def dot(a, b, contract=((1,), (0,))):
    return lax.dot_general(a, b, (contract, ((), ())), preferred_element_type=jnp.float32)


def layer_norm(values):
    average = jnp.mean(values, axis=-1, keepdims=True)
    centred = values - average
    variance = jnp.mean(centred * centred, axis=-1, keepdims=True)
    return centred * lax.rsqrt(variance + EPS)


def gelu(values):
    return 0.5 * values * (1.0 + lax.erf(values * (0.5**0.5)))


def pack_taps_kernel(taps_ref, out_ref):
    packed = []
    for g in range(2):
        rest = taps_ref[1, g, :, 48:80]
        packed.append(
            jnp.concatenate(
                [
                    jnp.concatenate([taps_ref[0, g], taps_ref[1, g, :, 0:48]], axis=1),
                    jnp.concatenate([rest[16 * r : 16 * r + 16] for r in range(4)], axis=1),
                    jnp.concatenate([rest[64:80], jnp.zeros((16, 96), rest.dtype)], axis=1),
                ],
                axis=0,
            )
        )
    for device in range(out_ref.shape[0]):
        out_ref[device] = packed[device % 2]


def front_kernel(utts, frames, parts, features_hbm, conv_hbm, proj_hbm, out_ref, features_ref, conv_ref, proj_ref, sems):
    copies = [
        pltpu.make_async_copy(source, target, sems.at[n])
        for n, (source, target) in enumerate(
            [(features_hbm, features_ref), (conv_hbm, conv_ref), (proj_hbm, proj_ref)]
        )
    ]
    for copy in copies:
        copy.start()
    rows = utts * frames
    copies[0].wait()
    features = features_ref[...]
    row = iota((rows, 2 * rows), 0)
    column = iota((rows, 2 * rows), 1)
    source = (row % utts) * (2 * frames) + 2 * (row // utts)
    first = dot(one_hot(column == source), features).astype(jnp.bfloat16)
    second = dot(one_hot(column == source + 1), features).astype(jnp.bfloat16)
    copies[1].wait()
    conv_out = dot(first, conv_ref[0]) + dot(second, conv_ref[1])
    hidden = gelu(layer_norm(conv_out)).astype(jnp.bfloat16)
    normed = layer_norm(hidden.astype(jnp.float32)).astype(jnp.bfloat16)
    copies[2].wait()
    projected = dot(normed, proj_ref[...]).astype(jnp.bfloat16)
    group = projected.shape[1] // (2 * parts)
    for part in range(parts):
        pieces = [
            projected[f * utts : (f + 1) * utts, (2 * part + g) * group : (2 * part + g + 1) * group]
            for g in range(2)
            for f in range(frames)
        ]
        out_ref[part] = jnp.concatenate(pieces, axis=1)


def order_kernel(order_ref, spread_ref, out_ref):
    utts, lanes = spread_ref.shape
    rows, width = out_ref.shape
    width //= 2
    chosen = one_hot(iota((utts, utts), 0) == order_ref[...])
    ordered = dot(chosen, spread_ref[...], ((0,), (0,))).astype(jnp.bfloat16)
    row = iota((rows, utts), 0)
    eighth = (row // 8) % 2 * 4 + row % 4
    slot = row // 16 * 4 + row // 4 % 2
    for which in range(2):
        same = slot + 2 * which == iota((rows, utts), 1)
        total = None
        for e in range(0, lanes // width, 2):
            left = jnp.concatenate([one_hot(same & (eighth == e + n)) for n in range(2)], axis=1)
            right = [ordered[:, (e + n) * width : (e + n + 1) * width] for n in range(2)]
            term = dot(left, jnp.concatenate(right, axis=0))
            total = term if total is None else total + term
        out_ref[:, which * width : (which + 1) * width] = total.astype(out_ref.dtype)


def pair_lengths(owner_ref, order_ref, len_ref):
    slot = owner_ref[0] // 2 * 4
    return [[len_ref[order_ref[slot + 2 * which + n]] // HOP for n in range(2)] for which in range(2)]


def place_kernel(total, half, owner_ref, order_ref, len_ref, rows_ref, shifted_ref, packed_ref, placed):
    lengths = pair_lengths(owner_ref, order_ref, len_ref)
    _, spots, group = placed.shape
    columns = rows_ref.shape[0]
    column = iota((1, columns), 1)
    is_first = (column // 4) % 2 == 0
    spot = iota((spots, columns), 0)
    for which in range(2):
        first_len, second_len = lengths[which]
        acc = None
        for odd in range(2):
            frame = (column // 8) * 8 + (column % 4) * 2 + odd
            target = jnp.where(is_first, frame, frame + first_len + GAP) + half
            valid = frame < jnp.where(is_first, first_len, second_len)
            target = jnp.where(valid, target, -1)
            lane = (2 * which + odd) * group
            term = dot(one_hot(spot == target), rows_ref[:, lane : lane + group])
            acc = term if acc is None else acc + term
        placed[which] = acc

    length = shifted_ref.shape[1]
    for which in range(2):
        for third in range(3):
            pairs = [k for k in range(3 * third, 3 * third + 3) if k < 8]
            pieces = [placed[which, 2 * k : 2 * k + length, :].astype(jnp.bfloat16) for k in pairs]
            pieces.append(jnp.zeros((length, 256 - group * len(pairs)), jnp.bfloat16))
            shifted_ref[which, :, third * 256 : (third + 1) * 256] = jnp.concatenate(pieces, axis=1)
        packed_ref[which] = jnp.where(
            iota((total, 1), 0) < lengths[which][0],
            placed[which, half : half + total, :],
            placed[which, half + GAP : half + GAP + total, :],
        )


def positional_kernel(
    swap, owner_ref, order_ref, len_ref, shifted_ref, packed_ref, *refs
):
    taps_refs, (out_ref, sums) = refs[:-2], refs[-2:]
    parity = owner_ref[0] % 2
    which = 1 - parity if swap else parity
    ring = taps_refs[0].shape[0]
    blocks = [[(ref, n) for n in range(ring)] for ref in taps_refs[:4] + taps_refs[6:]]
    blocks.insert(4, [(ref, n) for ref in taps_refs[4:6] for n in range(ring // 2)])
    slot = 2 * (owner_ref[0] - parity + which)
    first_len = len_ref[order_ref[slot]] // HOP
    second_len = len_ref[order_ref[slot + 1]] // HOP
    _, total, group = packed_ref.shape
    reach = sums.shape[0]

    for away, pieces in enumerate(blocks):
        start = pl.multiple_of(lax.rem(owner_ref[0] // ring + ring - away, ring) * STEP, STEP)
        left, right = [], []
        for slot in range(9):
            taps_ref, piece = pieces[min(slot, 7)]
            size = 96 if slot % 3 == 2 else 80
            left.append(taps_ref[piece, 0:size, :])
            fold = taps_ref[piece, 80:96, :]
            right += [fold] + [jnp.roll(fold, -32 * r, axis=1) for r in range(1, 4)]
            right.append(taps_ref[piece, 96:112, :])
            if size == 96:
                right.append(fold)
        matrix = jnp.concatenate([jnp.concatenate(left, axis=0), jnp.concatenate(right, axis=0)], axis=1)
        term = dot(shifted_ref[which, pl.ds(start, reach), :], matrix)
        sums[...] = term if away == 0 else sums[...] + term

    spot = iota((total, 1), 0)
    near = sums[0:total, 0:group] + sums[1 : total + 1, group : 2 * group]
    far = sums[GAP : GAP + total, 0:group] + sums[GAP + 1 : GAP + total + 1, group : 2 * group]
    conv_sum = jnp.where(spot < first_len + second_len, jnp.where(spot < first_len, near, far), 0.0)
    hidden = packed_ref[which] + gelu(conv_sum)
    hidden = jnp.concatenate([hidden, jnp.zeros((total, -group % LANES), jnp.float32)], axis=1)
    start = 0 if swap else pl.multiple_of(parity * group, 16)
    out_ref[pl.ds(start, group), :] = hidden.T[:group].astype(out_ref.dtype)


def join_kernel(owner_ref, received_hbm, own_hbm, out_hbm, sem):
    group = received_hbm.shape[0]
    start = pl.multiple_of((1 - owner_ref[0] % 2) * group, 16)
    copy = pltpu.make_async_copy(received_hbm, out_hbm.at[pl.ds(start, group), :], sem)
    copy.start()
    copy.wait()


VMEM = pl.BlockSpec(memory_space=pltpu.VMEM)
SMEM = pl.BlockSpec(memory_space=pltpu.SMEM)
ANY = pl.BlockSpec(memory_space=pl.ANY)


def send(values, ring, step):
    return lax.ppermute(values, "dp", [(o, (o + step * ring) % (ring * ring)) for o in range(ring * ring)])


def shards(features, conv_weight, proj_weight, pos_weight, utt_len, pack_order):
    owners = lax.axis_size("dp")
    parts = lax.axis_size("mp")
    utts, slice_rows, channels = features.shape
    frames = slice_rows // 2
    model_width = proj_weight.shape[1]
    width = model_width // parts
    total = frames * owners
    half = pos_weight.shape[0] * owners // 2
    params = pltpu.CompilerParams(vmem_limit_bytes=48 * 1024 * 1024)
    large = pltpu.CompilerParams(vmem_limit_bytes=62 * 1024 * 1024)

    owner = lax.axis_index("dp").reshape(1)
    ring = round(owners**0.5)
    along_z = [[y * ring + z for z in range(ring)] for y in range(ring)]
    tap_copies = pl.pallas_call(
        pack_taps_kernel,
        out_shape=jax.ShapeDtypeStruct((ring, TAP_ROWS, LANES), jnp.bfloat16),
        in_specs=[VMEM],
        out_specs=VMEM,
        compiler_params=params,
    )(pos_weight)
    taps = lax.all_to_all(tap_copies, "dp", 0, 0, axis_index_groups=along_z, tiled=True)

    sent = pl.pallas_call(
        functools.partial(front_kernel, utts, frames, parts),
        out_shape=jax.ShapeDtypeStruct((parts, utts, frames * width), jnp.bfloat16),
        in_specs=[ANY] * 3,
        out_specs=VMEM,
        scratch_shapes=[
            pltpu.VMEM((utts * slice_rows, channels), jnp.bfloat16),
            pltpu.VMEM(conv_weight.shape, jnp.bfloat16),
            pltpu.VMEM(proj_weight.shape, jnp.bfloat16),
            pltpu.SemaphoreType.DMA((3,)),
        ],
        compiler_params=pltpu.CompilerParams(vmem_limit_bytes=66900000),
    )(features.reshape(utts * slice_rows, channels), conv_weight, proj_weight)
    taps, sent = lax.optimization_barrier((taps, sent))
    one, minus_one = send(taps, ring, 1), send(taps, ring, -1)
    spread = lax.all_to_all(sent, "mp", split_axis=0, concat_axis=0, tiled=True)

    ordered = pl.pallas_call(
        order_kernel,
        out_shape=jax.ShapeDtypeStruct((owners * 8, 2 * width), jnp.bfloat16),
        in_specs=[VMEM] * 2,
        out_specs=VMEM,
        compiler_params=params,
    )(pack_order.reshape(1, -1), spread.reshape(parts * utts, frames * width))
    low, high = one[: ring // 2], minus_one[ring // 2 :]
    low, high, one, minus_one, ordered = lax.optimization_barrier((low, high, one, minus_one, ordered))
    low, high = send(low, ring, 3), send(high, ring, -3)
    three, minus_three = send(one, ring, 2), send(minus_one, ring, -2)
    two, minus_two = send(one, ring, 1), send(minus_one, ring, -1)
    taps = (taps, one, two, three, low, high, minus_three, minus_two, minus_one)
    pair_rows = lax.all_to_all(
        ordered.reshape(owners, 8, 2 * width), "dp", split_axis=0, concat_axis=0, tiled=True
    )

    reach = total + GAP + 16
    length = reach + 2 * half - STEP
    group = width // 2
    scalars = (owner, pack_order, utt_len)
    shifted, packed = pl.pallas_call(
        functools.partial(place_kernel, total, half),
        out_shape=[
            jax.ShapeDtypeStruct((2, length, 768), jnp.bfloat16),
            jax.ShapeDtypeStruct((2, total, group), jnp.float32),
        ],
        in_specs=[SMEM, SMEM, SMEM, VMEM],
        out_specs=[VMEM] * 2,
        scratch_shapes=[pltpu.VMEM((2, length + STEP, group), jnp.float32)],
        compiler_params=params,
    )(*scalars, pair_rows.reshape(owners * 8, 2 * width))
    convolve = lambda swap: pl.pallas_call(
        functools.partial(positional_kernel, swap),
        out_shape=jax.ShapeDtypeStruct((group if swap else width, total), jnp.bfloat16),
        in_specs=[SMEM, SMEM, SMEM, VMEM, VMEM] + [VMEM] * len(taps),
        out_specs=VMEM,
        scratch_shapes=[pltpu.VMEM((reach, 256), jnp.float32)],
        compiler_params=params,
    )
    other = convolve(True)(*scalars, shifted, packed, *taps)
    packed, other = lax.optimization_barrier((packed, other))
    received = lax.ppermute(other, "dp", [(o, o ^ 1) for o in range(owners)])
    own = convolve(False)(*scalars, shifted, packed, *taps)
    hidden = pl.pallas_call(
        join_kernel,
        out_shape=jax.ShapeDtypeStruct((width, total), jnp.bfloat16),
        in_specs=[SMEM, ANY, ANY],
        out_specs=ANY,
        scratch_shapes=[pltpu.SemaphoreType.DMA],
        input_output_aliases={2: 0},
        compiler_params=params,
    )(owner, received, own)
    return hidden.T


def solution(mesh):
    in_specs = (P("mp", "dp", None), P(), P(), P("dp", "mp", None, None), P(), P())
    out_specs = P("dp", "mp")
    return jax.shard_map(shards, mesh=mesh, in_specs=in_specs, out_specs=out_specs, check_vma=False)
```

```python
import functools

import jax
import jax.numpy as jnp
from jax import lax
from jax.experimental import pallas as pl
from jax.experimental.pallas import tpu as pltpu
from jax.sharding import PartitionSpec as P

HOP = 320
EPS = 1e-05
LANES = 128
TAP_ROWS = 104
GAP = 64
STEP = 16


def iota(shape, dim):
    return lax.broadcasted_iota(jnp.int32, shape, dim)


def one_hot(condition):
    return jnp.where(condition, 1.0, 0.0).astype(jnp.bfloat16)


def dot(a, b, contract=((1,), (0,))):
    return lax.dot_general(a, b, (contract, ((), ())), preferred_element_type=jnp.float32)


def layer_norm(values):
    average = jnp.mean(values, axis=-1, keepdims=True)
    centred = values - average
    variance = jnp.mean(centred * centred, axis=-1, keepdims=True)
    return centred * lax.rsqrt(variance + EPS)


def gelu(values):
    return 0.5 * values * (1.0 + lax.erf(values * (0.5**0.5)))


def pack_taps_kernel(taps_ref, out_ref):
    packed = []
    for g in range(2):
        first, second = taps_ref[0, g].astype(jnp.float32), taps_ref[1, g].astype(jnp.float32)
        rest = second[:, 48:80]
        blocks = [rest[8 * r : 8 * r + 8] for r in range(10)] + [jnp.zeros((8, 32), jnp.float32)] * 2
        folded = [jnp.concatenate(blocks[4 * n : 4 * n + 4], axis=1) for n in range(3)]
        wide = jnp.concatenate([first, second[:, 0:48]], axis=1)
        packed.append(jnp.concatenate([wide] + folded, axis=0).astype(out_ref.dtype))
    for device in range(out_ref.shape[0]):
        out_ref[device] = packed[device % 2]


def front_kernel(utts, frames, parts, features_hbm, conv_hbm, proj_hbm, out_ref, features_ref, conv_ref, proj_ref, sems):
    copies = [
        pltpu.make_async_copy(source, target, sems.at[n])
        for n, (source, target) in enumerate(
            [(features_hbm, features_ref), (conv_hbm, conv_ref), (proj_hbm, proj_ref)]
        )
    ]
    for copy in copies:
        copy.start()
    rows = utts * frames
    copies[0].wait()
    features = features_ref[...]
    row = iota((rows, 2 * rows), 0)
    column = iota((rows, 2 * rows), 1)
    source = (row % utts) * (2 * frames) + 2 * (row // utts)
    first = dot(one_hot(column == source), features).astype(jnp.bfloat16)
    second = dot(one_hot(column == source + 1), features).astype(jnp.bfloat16)
    copies[1].wait()
    conv_out = dot(first, conv_ref[0]) + dot(second, conv_ref[1])
    hidden = gelu(layer_norm(conv_out)).astype(jnp.bfloat16)
    normed = layer_norm(hidden.astype(jnp.float32)).astype(jnp.bfloat16)
    copies[2].wait()
    projected = dot(normed, proj_ref[...]).astype(jnp.bfloat16)
    group = projected.shape[1] // (2 * parts)
    for part in range(parts):
        pieces = [
            projected[f * utts : (f + 1) * utts, (2 * part + g) * group : (2 * part + g + 1) * group]
            for g in range(2)
            for f in range(frames)
        ]
        out_ref[part] = jnp.concatenate(pieces, axis=1)


def order_kernel(order_ref, spread_ref, out_ref):
    utts, lanes = spread_ref.shape
    rows, width = out_ref.shape
    width //= 2
    chosen = one_hot(iota((utts, utts), 0) == order_ref[...])
    ordered = dot(chosen, spread_ref[...], ((0,), (0,))).astype(jnp.bfloat16)
    row = iota((rows, utts), 0)
    eighth = (row // 8) % 2 * 4 + row % 4
    slot = row // 16 * 4 + row // 4 % 2
    for which in range(2):
        same = slot + 2 * which == iota((rows, utts), 1)
        total = None
        for e in range(0, lanes // width, 2):
            left = jnp.concatenate([one_hot(same & (eighth == e + n)) for n in range(2)], axis=1)
            right = [ordered[:, (e + n) * width : (e + n + 1) * width] for n in range(2)]
            term = dot(left, jnp.concatenate(right, axis=0))
            total = term if total is None else total + term
        out_ref[:, which * width : (which + 1) * width] = total.astype(out_ref.dtype)


def pair_lengths(owner_ref, order_ref, len_ref):
    slot = owner_ref[0] // 2 * 4
    return [[len_ref[order_ref[slot + 2 * which + n]] // HOP for n in range(2)] for which in range(2)]


def place_kernel(total, half, owner_ref, order_ref, len_ref, rows_ref, shifted_ref, packed_ref, placed):
    lengths = pair_lengths(owner_ref, order_ref, len_ref)
    _, spots, group = placed.shape
    columns = rows_ref.shape[0]
    column = iota((1, columns), 1)
    is_first = (column // 4) % 2 == 0
    spot = iota((spots, columns), 0)
    for which in range(2):
        first_len, second_len = lengths[which]
        acc = None
        for odd in range(2):
            frame = (column // 8) * 8 + (column % 4) * 2 + odd
            target = jnp.where(is_first, frame, frame + first_len + GAP) + half
            valid = frame < jnp.where(is_first, first_len, second_len)
            target = jnp.where(valid, target, -1)
            lane = (2 * which + odd) * group
            term = dot(one_hot(spot == target), rows_ref[:, lane : lane + group])
            acc = term if acc is None else acc + term
        placed[which] = acc

    length = shifted_ref.shape[1]
    for which in range(2):
        for third in range(3):
            pairs = [k for k in range(3 * third, 3 * third + 3) if k < 8]
            pieces = [placed[which, 2 * k : 2 * k + length, :].astype(jnp.bfloat16) for k in pairs]
            pieces.append(jnp.zeros((length, 256 - group * len(pairs)), jnp.bfloat16))
            shifted_ref[which, :, third * 256 : (third + 1) * 256] = jnp.concatenate(pieces, axis=1)
        packed_ref[which] = jnp.where(
            iota((total, 1), 0) < lengths[which][0],
            placed[which, half : half + total, :],
            placed[which, half + GAP : half + GAP + total, :],
        )


def positional_kernel(
    swap, owner_ref, order_ref, len_ref, shifted_ref, packed_ref, *refs
):
    taps_refs, (out_ref, sums, result, sem) = refs[:-4], refs[-4:]
    parity = owner_ref[0] % 2
    which = 1 - parity if swap else parity
    ring = taps_refs[0].shape[0]
    blocks = [[(ref, n) for n in range(ring)] for ref in taps_refs[:4] + taps_refs[6:]]
    blocks.insert(4, [(ref, n) for ref in taps_refs[4:6] for n in range(ring // 2)])
    slot = 2 * (owner_ref[0] - parity + which)
    first_len = len_ref[order_ref[slot]] // HOP
    second_len = len_ref[order_ref[slot + 1]] // HOP
    _, total, group = packed_ref.shape
    reach = sums.shape[0]

    for away, pieces in enumerate(blocks):
        start = pl.multiple_of(lax.rem(owner_ref[0] // ring + ring - away, ring) * STEP, STEP)
        left, right = [], []
        for slot in range(9):
            taps_ref, piece = pieces[min(slot, 7)]
            size = 96 if slot % 3 == 2 else 80
            left.append(taps_ref[piece, 0:size, :])
            fold = taps_ref[piece, 80:104, :].astype(jnp.float32)
            turned = [fold] + [jnp.roll(fold, -32 * r, axis=1) for r in range(1, 4)]
            right += [turned[r % 4][r // 4 * 8 : r // 4 * 8 + 8] for r in range(10)]
            if size == 96:
                right += [fold[0:16]]
        matrix = jnp.concatenate([jnp.concatenate(left, axis=0), jnp.concatenate(right, axis=0).astype(jnp.bfloat16)], axis=1)
        term = dot(shifted_ref[which, pl.ds(start, reach), :], matrix)
        sums[...] = term if away == 0 else sums[...] + term

    spot = iota((total, 1), 0)
    near = sums[0:total, 0:group] + sums[1 : total + 1, group : 2 * group]
    far = sums[GAP : GAP + total, 0:group] + sums[GAP + 1 : GAP + total + 1, group : 2 * group]
    conv_sum = jnp.where(spot < first_len + second_len, jnp.where(spot < first_len, near, far), 0.0)
    hidden = packed_ref[which] + gelu(conv_sum)
    hidden = jnp.concatenate([hidden, jnp.zeros((total, -group % LANES), jnp.float32)], axis=1)
    result[...] = hidden.T[:group].astype(result.dtype)
    start = 0 if swap else pl.multiple_of(parity * group, 16)
    copy = pltpu.make_async_copy(result, out_ref.at[pl.ds(start, group), :], sem)
    copy.start()
    copy.wait()


def join_kernel(owner_ref, received_hbm, own_hbm, out_hbm, sem):
    group = received_hbm.shape[0]
    start = pl.multiple_of((1 - owner_ref[0] % 2) * group, 16)
    copy = pltpu.make_async_copy(received_hbm, out_hbm.at[pl.ds(start, group), :], sem)
    copy.start()
    copy.wait()


VMEM = pl.BlockSpec(memory_space=pltpu.VMEM)
SMEM = pl.BlockSpec(memory_space=pltpu.SMEM)
ANY = pl.BlockSpec(memory_space=pl.ANY)


def send(values, ring, step):
    return lax.ppermute(values, "dp", [(o, (o + step * ring) % (ring * ring)) for o in range(ring * ring)])


def shards(features, conv_weight, proj_weight, pos_weight, utt_len, pack_order):
    owners = lax.axis_size("dp")
    parts = lax.axis_size("mp")
    utts, slice_rows, channels = features.shape
    frames = slice_rows // 2
    model_width = proj_weight.shape[1]
    width = model_width // parts
    total = frames * owners
    half = pos_weight.shape[0] * owners // 2
    params = pltpu.CompilerParams(vmem_limit_bytes=48 * 1024 * 1024)
    large = pltpu.CompilerParams(vmem_limit_bytes=62 * 1024 * 1024)

    owner = lax.axis_index("dp").reshape(1)
    ring = round(owners**0.5)
    along_z = [[y * ring + z for z in range(ring)] for y in range(ring)]
    tap_copies = pl.pallas_call(
        pack_taps_kernel,
        out_shape=jax.ShapeDtypeStruct((ring, TAP_ROWS, LANES), jnp.bfloat16),
        in_specs=[VMEM],
        out_specs=VMEM,
        compiler_params=params,
    )(pos_weight)
    taps = lax.all_to_all(tap_copies, "dp", 0, 0, axis_index_groups=along_z, tiled=True)

    sent = pl.pallas_call(
        functools.partial(front_kernel, utts, frames, parts),
        out_shape=jax.ShapeDtypeStruct((parts, utts, frames * width), jnp.bfloat16),
        in_specs=[ANY] * 3,
        out_specs=VMEM,
        scratch_shapes=[
            pltpu.VMEM((utts * slice_rows, channels), jnp.bfloat16),
            pltpu.VMEM(conv_weight.shape, jnp.bfloat16),
            pltpu.VMEM(proj_weight.shape, jnp.bfloat16),
            pltpu.SemaphoreType.DMA((3,)),
        ],
        compiler_params=pltpu.CompilerParams(vmem_limit_bytes=66900000),
    )(features.reshape(utts * slice_rows, channels), conv_weight, proj_weight)
    taps, sent = lax.optimization_barrier((taps, sent))
    one, minus_one, two, minus_two = [send(taps, ring, step) for step in (1, -1, 2, -2)]
    spread = lax.all_to_all(sent, "mp", split_axis=0, concat_axis=0, tiled=True)

    ordered = pl.pallas_call(
        order_kernel,
        out_shape=jax.ShapeDtypeStruct((owners * 8, 2 * width), jnp.bfloat16),
        in_specs=[VMEM] * 2,
        out_specs=VMEM,
        compiler_params=params,
    )(pack_order.reshape(1, -1), spread.reshape(parts * utts, frames * width))
    one, minus_one, two, minus_two, ordered = lax.optimization_barrier((one, minus_one, two, minus_two, ordered))
    three, minus_three = send(two, ring, 1), send(minus_two, ring, -1)
    low, high = send(two[: ring // 2], ring, 2), send(minus_two[ring // 2 :], ring, -2)
    taps = (taps, one, two, three, low, high, minus_three, minus_two, minus_one)
    pair_rows = lax.all_to_all(
        ordered.reshape(owners, 8, 2 * width), "dp", split_axis=0, concat_axis=0, tiled=True
    )

    reach = total + GAP + 16
    length = reach + 2 * half - STEP
    group = width // 2
    scalars = (owner, pack_order, utt_len)
    shifted, packed = pl.pallas_call(
        functools.partial(place_kernel, total, half),
        out_shape=[
            jax.ShapeDtypeStruct((2, length, 768), jnp.bfloat16),
            jax.ShapeDtypeStruct((2, total, group), jnp.float32),
        ],
        in_specs=[SMEM, SMEM, SMEM, VMEM],
        out_specs=[VMEM] * 2,
        scratch_shapes=[pltpu.VMEM((2, length + STEP, group), jnp.float32)],
        compiler_params=params,
    )(*scalars, pair_rows.reshape(owners * 8, 2 * width))
    convolve = lambda swap: pl.pallas_call(
        functools.partial(positional_kernel, swap),
        out_shape=jax.ShapeDtypeStruct((group if swap else width, total), jnp.bfloat16),
        in_specs=[SMEM, SMEM, SMEM, VMEM, VMEM] + [VMEM] * len(taps),
        out_specs=ANY,
        scratch_shapes=[
            pltpu.VMEM((reach, 256), jnp.float32),
            pltpu.VMEM((group, total), jnp.bfloat16),
            pltpu.SemaphoreType.DMA,
        ],
        compiler_params=params,
    )
    other = convolve(True)(*scalars, shifted, packed, *taps)
    packed, other = lax.optimization_barrier((packed, other))
    received = lax.ppermute(other, "dp", [(o, o ^ 1) for o in range(owners)])
    own = convolve(False)(*scalars, shifted, packed, *taps)
    hidden = pl.pallas_call(
        join_kernel,
        out_shape=jax.ShapeDtypeStruct((width, total), jnp.bfloat16),
        in_specs=[SMEM, ANY, ANY],
        out_specs=ANY,
        scratch_shapes=[pltpu.SemaphoreType.DMA],
        input_output_aliases={2: 0},
        compiler_params=params,
    )(owner, received, own)
    return hidden.T


def solution(mesh):
    in_specs = (P("mp", "dp", None), P(), P(), P("dp", "mp", None, None), P(), P())
    out_specs = P("dp", "mp")
    return jax.shard_map(shards, mesh=mesh, in_specs=in_specs, out_specs=out_specs, check_vma=False)
```

```python
import functools

import jax
import jax.numpy as jnp
from jax import lax
from jax.experimental import pallas as pl
from jax.experimental.pallas import tpu as pltpu
from jax.sharding import PartitionSpec as P

HOP = 320
EPS = 1e-05
LANES = 128
TAP_ROWS = 104
GAP = 64
STEP = 16


def iota(shape, dim):
    return lax.broadcasted_iota(jnp.int32, shape, dim)


def one_hot(condition):
    return jnp.where(condition, 1.0, 0.0).astype(jnp.bfloat16)


def dot(a, b, contract=((1,), (0,))):
    return lax.dot_general(a, b, (contract, ((), ())), preferred_element_type=jnp.float32)


def layer_norm(values):
    average = jnp.mean(values, axis=-1, keepdims=True)
    centred = values - average
    variance = jnp.mean(centred * centred, axis=-1, keepdims=True)
    return centred * lax.rsqrt(variance + EPS)


def gelu(values):
    return 0.5 * values * (1.0 + lax.erf(values * (0.5**0.5)))


def pack_taps_kernel(taps_ref, out_ref):
    packed = []
    for g in range(2):
        first, second = taps_ref[0, g].astype(jnp.float32), taps_ref[1, g].astype(jnp.float32)
        rest = second[:, 48:80]
        blocks = [rest[8 * r : 8 * r + 8] for r in range(10)] + [jnp.zeros((8, 32), jnp.float32)] * 2
        folded = [jnp.concatenate(blocks[4 * n : 4 * n + 4], axis=1) for n in range(3)]
        wide = jnp.concatenate([first, second[:, 0:48]], axis=1)
        packed.append(jnp.concatenate([wide] + folded, axis=0).astype(out_ref.dtype))
    for device in range(out_ref.shape[0]):
        out_ref[device] = packed[device % 2]


def front_kernel(utts, frames, parts, features_hbm, conv_hbm, proj_hbm, out_ref, features_ref, conv_ref, proj_ref, sems):
    copies = [
        pltpu.make_async_copy(source, target, sems.at[n])
        for n, (source, target) in enumerate(
            [(features_hbm, features_ref), (conv_hbm, conv_ref), (proj_hbm, proj_ref)]
        )
    ]
    for copy in copies:
        copy.start()
    rows = utts * frames
    copies[0].wait()
    features = features_ref[...]
    row = iota((rows, 2 * rows), 0)
    column = iota((rows, 2 * rows), 1)
    source = (row % utts) * (2 * frames) + 2 * (row // utts)
    first = dot(one_hot(column == source), features).astype(jnp.bfloat16)
    second = dot(one_hot(column == source + 1), features).astype(jnp.bfloat16)
    copies[1].wait()
    conv_out = dot(first, conv_ref[0]) + dot(second, conv_ref[1])
    hidden = gelu(layer_norm(conv_out)).astype(jnp.bfloat16)
    normed = layer_norm(hidden.astype(jnp.float32)).astype(jnp.bfloat16)
    copies[2].wait()
    projected = dot(normed, proj_ref[...]).astype(jnp.bfloat16)
    group = projected.shape[1] // (2 * parts)
    for part in range(parts):
        pieces = [
            projected[f * utts : (f + 1) * utts, (2 * part + g) * group : (2 * part + g + 1) * group]
            for g in range(2)
            for f in range(frames)
        ]
        out_ref[part] = jnp.concatenate(pieces, axis=1)


def order_kernel(order_ref, spread_ref, out_ref):
    utts, lanes = spread_ref.shape
    rows, width = out_ref.shape
    width //= 2
    chosen = one_hot(iota((utts, utts), 0) == order_ref[...])
    ordered = dot(chosen, spread_ref[...], ((0,), (0,))).astype(jnp.bfloat16)
    row = iota((rows, utts), 0)
    eighth = (row // 8) % 2 * 4 + row % 4
    slot = row // 16 * 4 + row // 4 % 2
    for which in range(2):
        same = slot + 2 * which == iota((rows, utts), 1)
        total = None
        for e in range(0, lanes // width, 2):
            left = jnp.concatenate([one_hot(same & (eighth == e + n)) for n in range(2)], axis=1)
            right = [ordered[:, (e + n) * width : (e + n + 1) * width] for n in range(2)]
            term = dot(left, jnp.concatenate(right, axis=0))
            total = term if total is None else total + term
        out_ref[:, which * width : (which + 1) * width] = total.astype(out_ref.dtype)


def pair_lengths(owner_ref, order_ref, len_ref):
    slot = owner_ref[0] // 2 * 4
    return [[len_ref[order_ref[slot + 2 * which + n]] // HOP for n in range(2)] for which in range(2)]


def place_kernel(total, half, owner_ref, order_ref, len_ref, rows_ref, shifted_ref, packed_ref, placed):
    lengths = pair_lengths(owner_ref, order_ref, len_ref)
    _, spots, group = placed.shape
    columns = rows_ref.shape[0]
    column = iota((1, columns), 1)
    is_first = (column // 4) % 2 == 0
    spot = iota((spots, columns), 0)
    for which in range(2):
        first_len, second_len = lengths[which]
        acc = None
        for odd in range(2):
            frame = (column // 8) * 8 + (column % 4) * 2 + odd
            target = jnp.where(is_first, frame, frame + first_len + GAP) + half
            valid = frame < jnp.where(is_first, first_len, second_len)
            target = jnp.where(valid, target, -1)
            lane = (2 * which + odd) * group
            term = dot(one_hot(spot == target), rows_ref[:, lane : lane + group])
            acc = term if acc is None else acc + term
        placed[which] = acc

    length = shifted_ref.shape[1]
    for which in range(2):
        for third in range(3):
            pairs = [k for k in range(3 * third, 3 * third + 3) if k < 8]
            pieces = [placed[which, 2 * k : 2 * k + length, :].astype(jnp.bfloat16) for k in pairs]
            pieces.append(jnp.zeros((length, 256 - group * len(pairs)), jnp.bfloat16))
            shifted_ref[which, :, third * 256 : (third + 1) * 256] = jnp.concatenate(pieces, axis=1)
        packed_ref[which] = jnp.where(
            iota((total, 1), 0) < lengths[which][0],
            placed[which, half : half + total, :],
            placed[which, half + GAP : half + GAP + total, :],
        )


def add_blocks(which, ring, distances, owner_ref, shifted_ref, refs, before, sums):
    refs = list(refs)
    for away in distances:
        count = 2 if away == ring // 2 else 1
        pieces = [(ref, n) for ref in refs[:count] for n in range(ring // count)]
        refs = refs[count:]
        start = pl.multiple_of(lax.rem(owner_ref[0] // ring + ring - away, ring) * STEP, STEP)
        left, right = [], []
        for slot in range(9):
            taps_ref, piece = pieces[min(slot, 7)]
            size = 96 if slot % 3 == 2 else 80
            left.append(taps_ref[piece, 0:size, :])
            fold = taps_ref[piece, 80:104, :].astype(jnp.float32)
            turned = [fold] + [jnp.roll(fold, -32 * r, axis=1) for r in range(1, 4)]
            right += [turned[r % 4][r // 4 * 8 : r // 4 * 8 + 8] for r in range(10)]
            if size == 96:
                right += [fold[0:16]]
        right = jnp.concatenate(right, axis=0).astype(jnp.bfloat16)
        matrix = jnp.concatenate([jnp.concatenate(left, axis=0), right], axis=1)
        term = dot(shifted_ref[which, pl.ds(start, sums.shape[0]), :], matrix)
        sums[...] = term if before is None else before[...] + term
        before = sums


def near_kernel(ring, distances, owner_ref, shifted_ref, *refs):
    add_blocks(1 - owner_ref[0] % 2, ring, distances, owner_ref, shifted_ref, refs[:-1], None, refs[-1])


def positional_kernel(swap, ring, distances, owner_ref, order_ref, len_ref, shifted_ref, packed_ref, *refs):
    taps_refs, (out_ref, sums, result, sem) = refs[:-4], refs[-4:]
    parity = owner_ref[0] % 2
    which = 1 - parity if swap else parity
    before, taps_refs = (taps_refs[0], taps_refs[1:]) if swap else (None, taps_refs)
    slot = 2 * (owner_ref[0] - parity + which)
    first_len = len_ref[order_ref[slot]] // HOP
    second_len = len_ref[order_ref[slot + 1]] // HOP
    _, total, group = packed_ref.shape
    add_blocks(which, ring, distances, owner_ref, shifted_ref, taps_refs, before, sums)

    spot = iota((total, 1), 0)
    near = sums[0:total, 0:group] + sums[1 : total + 1, group : 2 * group]
    far = sums[GAP : GAP + total, 0:group] + sums[GAP + 1 : GAP + total + 1, group : 2 * group]
    conv_sum = jnp.where(spot < first_len + second_len, jnp.where(spot < first_len, near, far), 0.0)
    hidden = packed_ref[which] + gelu(conv_sum)
    hidden = jnp.concatenate([hidden, jnp.zeros((total, -group % LANES), jnp.float32)], axis=1)
    result[...] = hidden.T[:group].astype(result.dtype)
    start = 0 if swap else pl.multiple_of(parity * group, 16)
    copy = pltpu.make_async_copy(result, out_ref.at[pl.ds(start, group), :], sem)
    copy.start()
    copy.wait()


def join_kernel(owner_ref, received_hbm, own_hbm, out_hbm, sem):
    group = received_hbm.shape[0]
    start = pl.multiple_of((1 - owner_ref[0] % 2) * group, 16)
    copy = pltpu.make_async_copy(received_hbm, out_hbm.at[pl.ds(start, group), :], sem)
    copy.start()
    copy.wait()


VMEM = pl.BlockSpec(memory_space=pltpu.VMEM)
SMEM = pl.BlockSpec(memory_space=pltpu.SMEM)
ANY = pl.BlockSpec(memory_space=pl.ANY)


def send(values, ring, step):
    return lax.ppermute(values, "dp", [(o, (o + step * ring) % (ring * ring)) for o in range(ring * ring)])


def shards(features, conv_weight, proj_weight, pos_weight, utt_len, pack_order):
    owners = lax.axis_size("dp")
    parts = lax.axis_size("mp")
    utts, slice_rows, channels = features.shape
    frames = slice_rows // 2
    model_width = proj_weight.shape[1]
    width = model_width // parts
    total = frames * owners
    half = pos_weight.shape[0] * owners // 2
    params = pltpu.CompilerParams(vmem_limit_bytes=48 * 1024 * 1024)
    large = pltpu.CompilerParams(vmem_limit_bytes=62 * 1024 * 1024)

    owner = lax.axis_index("dp").reshape(1)
    ring = round(owners**0.5)
    along_z = [[y * ring + z for z in range(ring)] for y in range(ring)]
    tap_copies = pl.pallas_call(
        pack_taps_kernel,
        out_shape=jax.ShapeDtypeStruct((ring, TAP_ROWS, LANES), jnp.bfloat16),
        in_specs=[VMEM],
        out_specs=VMEM,
        compiler_params=params,
    )(pos_weight)
    taps = lax.all_to_all(tap_copies, "dp", 0, 0, axis_index_groups=along_z, tiled=True)

    sent = pl.pallas_call(
        functools.partial(front_kernel, utts, frames, parts),
        out_shape=jax.ShapeDtypeStruct((parts, utts, frames * width), jnp.bfloat16),
        in_specs=[ANY] * 3,
        out_specs=VMEM,
        scratch_shapes=[
            pltpu.VMEM((utts * slice_rows, channels), jnp.bfloat16),
            pltpu.VMEM(conv_weight.shape, jnp.bfloat16),
            pltpu.VMEM(proj_weight.shape, jnp.bfloat16),
            pltpu.SemaphoreType.DMA((3,)),
        ],
        compiler_params=pltpu.CompilerParams(vmem_limit_bytes=66900000),
    )(features.reshape(utts * slice_rows, channels), conv_weight, proj_weight)
    taps, sent = lax.optimization_barrier((taps, sent))
    two, minus_two, one, minus_one = [send(taps, ring, step) for step in (2, -2, 1, -1)]
    spread = lax.all_to_all(sent, "mp", split_axis=0, concat_axis=0, tiled=True)

    ordered = pl.pallas_call(
        order_kernel,
        out_shape=jax.ShapeDtypeStruct((owners * 8, 2 * width), jnp.bfloat16),
        in_specs=[VMEM] * 2,
        out_specs=VMEM,
        compiler_params=params,
    )(pack_order.reshape(1, -1), spread.reshape(parts * utts, frames * width))
    one, minus_one, two, minus_two, ordered = lax.optimization_barrier((one, minus_one, two, minus_two, ordered))
    three, minus_three = send(two, ring, 1), send(minus_two, ring, -1)
    low, high = send(two[: ring // 2], ring, 2), send(minus_two[ring // 2 :], ring, -2)
    early_taps, late_taps = (taps, one, two, minus_two, minus_one), (three, low, high, minus_three)
    pair_rows = lax.all_to_all(
        ordered.reshape(owners, 8, 2 * width), "dp", split_axis=0, concat_axis=0, tiled=True
    )

    reach = total + GAP + 16
    length = reach + 2 * half - STEP
    group = width // 2
    scalars = (owner, pack_order, utt_len)
    shifted, packed = pl.pallas_call(
        functools.partial(place_kernel, total, half),
        out_shape=[
            jax.ShapeDtypeStruct((2, length, 768), jnp.bfloat16),
            jax.ShapeDtypeStruct((2, total, group), jnp.float32),
        ],
        in_specs=[SMEM, SMEM, SMEM, VMEM],
        out_specs=[VMEM] * 2,
        scratch_shapes=[pltpu.VMEM((2, length + STEP, group), jnp.float32)],
        compiler_params=params,
    )(*scalars, pair_rows.reshape(owners * 8, 2 * width))
    early, late = (0, 1, 2, 6, 7), (3, 4, 5)
    begun = pl.pallas_call(
        functools.partial(near_kernel, ring, early),
        out_shape=jax.ShapeDtypeStruct((reach, 256), jnp.float32),
        in_specs=[SMEM] + [VMEM] * 6,
        out_specs=VMEM,
        compiler_params=params,
    )(owner, shifted, *early_taps)

    def convolve(swap, distances, *taps):
        return pl.pallas_call(
            functools.partial(positional_kernel, swap, ring, distances),
            out_shape=jax.ShapeDtypeStruct((group if swap else width, total), jnp.bfloat16),
            in_specs=[SMEM, SMEM, SMEM, VMEM, VMEM] + [VMEM] * len(taps),
            out_specs=ANY,
            scratch_shapes=[
                pltpu.VMEM((reach, 256), jnp.float32),
                pltpu.VMEM((group, total), jnp.bfloat16),
                pltpu.SemaphoreType.DMA,
            ],
            compiler_params=params,
        )(*scalars, shifted, packed, *taps)

    other = convolve(True, late, begun, *late_taps)
    packed, other = lax.optimization_barrier((packed, other))
    received = lax.ppermute(other, "dp", [(o, o ^ 1) for o in range(owners)])
    own = convolve(False, early + late, *early_taps, *late_taps)
    hidden = pl.pallas_call(
        join_kernel,
        out_shape=jax.ShapeDtypeStruct((width, total), jnp.bfloat16),
        in_specs=[SMEM, ANY, ANY],
        out_specs=ANY,
        scratch_shapes=[pltpu.SemaphoreType.DMA],
        input_output_aliases={2: 0},
        compiler_params=params,
    )(owner, received, own)
    return hidden.T


def solution(mesh):
    in_specs = (P("mp", "dp", None), P(), P(), P("dp", "mp", None, None), P(), P())
    out_specs = P("dp", "mp")
    return jax.shard_map(shards, mesh=mesh, in_specs=in_specs, out_specs=out_specs, check_vma=False)
```

```python
import functools

import jax
import jax.numpy as jnp
from jax import lax
from jax.experimental import pallas as pl
from jax.experimental.pallas import tpu as pltpu
from jax.sharding import PartitionSpec as P

HOP = 320
EPS = 1e-05
LANES = 128
TAP_ROWS = 104
GAP = 64
STEP = 16


def iota(shape, dim):
    return lax.broadcasted_iota(jnp.int32, shape, dim)


def one_hot(condition):
    return jnp.where(condition, 1.0, 0.0).astype(jnp.bfloat16)


def dot(a, b, contract=((1,), (0,))):
    return lax.dot_general(a, b, (contract, ((), ())), preferred_element_type=jnp.float32)


def layer_norm(values):
    average = jnp.mean(values, axis=-1, keepdims=True)
    centred = values - average
    variance = jnp.mean(centred * centred, axis=-1, keepdims=True)
    return centred * lax.rsqrt(variance + EPS)


def gelu(values):
    return 0.5 * values * (1.0 + lax.erf(values * (0.5**0.5)))


def pack_taps_kernel(taps_ref, out_ref):
    packed = []
    for g in range(2):
        first, second = taps_ref[0, g].astype(jnp.float32), taps_ref[1, g].astype(jnp.float32)
        rest = second[:, 48:80]
        blocks = [rest[8 * r : 8 * r + 8] for r in range(10)] + [jnp.zeros((8, 32), jnp.float32)] * 2
        folded = [jnp.concatenate(blocks[4 * n : 4 * n + 4], axis=1) for n in range(3)]
        wide = jnp.concatenate([first, second[:, 0:48]], axis=1)
        packed.append(jnp.concatenate([wide] + folded, axis=0).astype(out_ref.dtype))
    for device in range(out_ref.shape[0]):
        out_ref[device] = packed[device % 2]


def front_kernel(utts, frames, parts, features_hbm, conv_hbm, proj_hbm, out_ref, features_ref, conv_ref, proj_ref, sems):
    copies = [
        pltpu.make_async_copy(source, target, sems.at[n])
        for n, (source, target) in enumerate(
            [(features_hbm, features_ref), (conv_hbm, conv_ref), (proj_hbm, proj_ref)]
        )
    ]
    for copy in copies:
        copy.start()
    rows = utts * frames
    copies[0].wait()
    features = features_ref[...]
    row = iota((rows, 2 * rows), 0)
    column = iota((rows, 2 * rows), 1)
    source = (row % utts) * (2 * frames) + 2 * (row // utts)
    first = dot(one_hot(column == source), features).astype(jnp.bfloat16)
    second = dot(one_hot(column == source + 1), features).astype(jnp.bfloat16)
    copies[1].wait()
    conv_out = dot(first, conv_ref[0]) + dot(second, conv_ref[1])
    hidden = gelu(layer_norm(conv_out)).astype(jnp.bfloat16)
    normed = layer_norm(hidden.astype(jnp.float32)).astype(jnp.bfloat16)
    copies[2].wait()
    projected = dot(normed, proj_ref[...]).astype(jnp.bfloat16)
    group = projected.shape[1] // (2 * parts)
    for part in range(parts):
        pieces = [
            projected[f * utts : (f + 1) * utts, (2 * part + g) * group : (2 * part + g + 1) * group]
            for g in range(2)
            for f in range(frames)
        ]
        out_ref[part] = jnp.concatenate(pieces, axis=1)


def order_kernel(order_ref, spread_ref, out_ref):
    utts, lanes = spread_ref.shape
    rows, width = out_ref.shape
    width //= 2
    chosen = one_hot(iota((utts, utts), 0) == order_ref[...])
    ordered = dot(chosen, spread_ref[...], ((0,), (0,))).astype(jnp.bfloat16)
    row = iota((rows, utts), 0)
    eighth = (row // 8) % 2 * 4 + row % 4
    slot = row // 16 * 4 + row // 4 % 2
    for which in range(2):
        same = slot + 2 * which == iota((rows, utts), 1)
        total = None
        for e in range(0, lanes // width, 2):
            left = jnp.concatenate([one_hot(same & (eighth == e + n)) for n in range(2)], axis=1)
            right = [ordered[:, (e + n) * width : (e + n + 1) * width] for n in range(2)]
            term = dot(left, jnp.concatenate(right, axis=0))
            total = term if total is None else total + term
        out_ref[:, which * width : (which + 1) * width] = total.astype(out_ref.dtype)


def pair_lengths(owner_ref, order_ref, len_ref):
    slot = owner_ref[0] // 2 * 4
    return [[len_ref[order_ref[slot + 2 * which + n]] // HOP for n in range(2)] for which in range(2)]


def place_kernel(total, half, owner_ref, order_ref, len_ref, rows_ref, shifted_ref, packed_ref, placed):
    lengths = pair_lengths(owner_ref, order_ref, len_ref)
    _, spots, group = placed.shape
    columns = rows_ref.shape[0]
    column = iota((1, columns), 1)
    is_first = (column // 4) % 2 == 0
    spot = iota((spots, columns), 0)
    for which in range(2):
        first_len, second_len = lengths[which]
        acc = None
        for odd in range(2):
            frame = (column // 8) * 8 + (column % 4) * 2 + odd
            target = jnp.where(is_first, frame, frame + first_len + GAP) + half
            valid = frame < jnp.where(is_first, first_len, second_len)
            target = jnp.where(valid, target, -1)
            lane = (2 * which + odd) * group
            term = dot(one_hot(spot == target), rows_ref[:, lane : lane + group])
            acc = term if acc is None else acc + term
        placed[which] = acc

    length = shifted_ref.shape[1]
    for which in range(2):
        for third in range(3):
            pairs = [k for k in range(3 * third, 3 * third + 3) if k < 8]
            pieces = [placed[which, 2 * k : 2 * k + length, :].astype(jnp.bfloat16) for k in pairs]
            pieces.append(jnp.zeros((length, 256 - group * len(pairs)), jnp.bfloat16))
            shifted_ref[which, :, third * 256 : (third + 1) * 256] = jnp.concatenate(pieces, axis=1)
        packed_ref[which] = jnp.where(
            iota((total, 1), 0) < lengths[which][0],
            placed[which, half : half + total, :],
            placed[which, half + GAP : half + GAP + total, :],
        )


def add_blocks(which, ring, distances, owner_ref, shifted_ref, refs, before, sums):
    refs = list(refs)
    for away in distances:
        count = 2 if away == ring // 2 else 1
        pieces = [(ref, n) for ref in refs[:count] for n in range(ring // count)]
        refs = refs[count:]
        start = pl.multiple_of(lax.rem(owner_ref[0] // ring + ring - away, ring) * STEP, STEP)
        left, right = [], []
        for slot in range(9):
            taps_ref, piece = pieces[min(slot, 7)]
            size = 96 if slot % 3 == 2 else 80
            left.append(taps_ref[piece, 0:size, :])
            fold = taps_ref[piece, 80:104, :].astype(jnp.float32)
            turned = [fold] + [jnp.roll(fold, -32 * r, axis=1) for r in range(1, 4)]
            right += [turned[r % 4][r // 4 * 8 : r // 4 * 8 + 8] for r in range(10)]
            if size == 96:
                right += [fold[0:16]]
        right = jnp.concatenate(right, axis=0).astype(jnp.bfloat16)
        matrix = jnp.concatenate([jnp.concatenate(left, axis=0), right], axis=1)
        term = dot(shifted_ref[which, pl.ds(start, sums.shape[0]), :], matrix)
        sums[...] = term if before is None else before[...] + term
        before = sums


def near_kernel(ring, distances, owner_ref, shifted_ref, *refs):
    add_blocks(1 - owner_ref[0] % 2, ring, distances, owner_ref, shifted_ref, refs[:-1], None, refs[-1])


def positional_kernel(swap, ring, distances, owner_ref, order_ref, len_ref, shifted_ref, packed_ref, *refs):
    taps_refs, (out_ref, sums, result, sem) = refs[:-4], refs[-4:]
    parity = owner_ref[0] % 2
    which = 1 - parity if swap else parity
    before, taps_refs = (taps_refs[0], taps_refs[1:]) if swap else (None, taps_refs)
    slot = 2 * (owner_ref[0] - parity + which)
    first_len = len_ref[order_ref[slot]] // HOP
    second_len = len_ref[order_ref[slot + 1]] // HOP
    _, total, group = packed_ref.shape
    add_blocks(which, ring, distances, owner_ref, shifted_ref, taps_refs, before, sums)

    spot = iota((total, 1), 0)
    near = sums[0:total, 0:group] + sums[1 : total + 1, group : 2 * group]
    far = sums[GAP : GAP + total, 0:group] + sums[GAP + 1 : GAP + total + 1, group : 2 * group]
    conv_sum = jnp.where(spot < first_len + second_len, jnp.where(spot < first_len, near, far), 0.0)
    hidden = packed_ref[which] + gelu(conv_sum)
    hidden = jnp.concatenate([hidden, jnp.zeros((total, -group % LANES), jnp.float32)], axis=1)
    result[...] = hidden.T[:group].astype(result.dtype)
    start = 0 if swap else pl.multiple_of(parity * group, 16)
    copy = pltpu.make_async_copy(result, out_ref.at[pl.ds(start, group), :], sem)
    copy.start()
    copy.wait()


def join_kernel(owner_ref, received_hbm, own_hbm, out_hbm, sem):
    group = received_hbm.shape[0]
    start = pl.multiple_of((1 - owner_ref[0] % 2) * group, 16)
    copy = pltpu.make_async_copy(received_hbm, out_hbm.at[pl.ds(start, group), :], sem)
    copy.start()
    copy.wait()


VMEM = pl.BlockSpec(memory_space=pltpu.VMEM)
SMEM = pl.BlockSpec(memory_space=pltpu.SMEM)
ANY = pl.BlockSpec(memory_space=pl.ANY)


def send(values, ring, step):
    return lax.ppermute(values, "dp", [(o, (o + step * ring) % (ring * ring)) for o in range(ring * ring)])


def shards(features, conv_weight, proj_weight, pos_weight, utt_len, pack_order):
    owners = lax.axis_size("dp")
    parts = lax.axis_size("mp")
    utts, slice_rows, channels = features.shape
    frames = slice_rows // 2
    model_width = proj_weight.shape[1]
    width = model_width // parts
    total = frames * owners
    half = pos_weight.shape[0] * owners // 2
    params = pltpu.CompilerParams(vmem_limit_bytes=48 * 1024 * 1024)
    large = pltpu.CompilerParams(vmem_limit_bytes=62 * 1024 * 1024)

    owner = lax.axis_index("dp").reshape(1)
    ring = round(owners**0.5)
    along_z = [[y * ring + z for z in range(ring)] for y in range(ring)]
    tap_copies = pl.pallas_call(
        pack_taps_kernel,
        out_shape=jax.ShapeDtypeStruct((ring, TAP_ROWS, LANES), jnp.bfloat16),
        in_specs=[VMEM],
        out_specs=VMEM,
        compiler_params=params,
    )(pos_weight)
    taps = lax.all_to_all(tap_copies, "dp", 0, 0, axis_index_groups=along_z, tiled=True)

    sent = pl.pallas_call(
        functools.partial(front_kernel, utts, frames, parts),
        out_shape=jax.ShapeDtypeStruct((parts, utts, frames * width), jnp.bfloat16),
        in_specs=[ANY] * 3,
        out_specs=VMEM,
        scratch_shapes=[
            pltpu.VMEM((utts * slice_rows, channels), jnp.bfloat16),
            pltpu.VMEM(conv_weight.shape, jnp.bfloat16),
            pltpu.VMEM(proj_weight.shape, jnp.bfloat16),
            pltpu.SemaphoreType.DMA((3,)),
        ],
        compiler_params=pltpu.CompilerParams(vmem_limit_bytes=66900000),
    )(features.reshape(utts * slice_rows, channels), conv_weight, proj_weight)
    taps, sent = lax.optimization_barrier((taps, sent))
    two, minus_two, one, minus_one = [send(taps, ring, step) for step in (2, -2, 1, -1)]
    spread = lax.all_to_all(sent, "mp", split_axis=0, concat_axis=0, tiled=True)

    ordered = pl.pallas_call(
        order_kernel,
        out_shape=jax.ShapeDtypeStruct((owners * 8, 2 * width), jnp.bfloat16),
        in_specs=[VMEM] * 2,
        out_specs=VMEM,
        compiler_params=params,
    )(pack_order.reshape(1, -1), spread.reshape(parts * utts, frames * width))
    two, minus_two, ordered = lax.optimization_barrier((two, minus_two, ordered))
    three, minus_three = send(two, ring, 1), send(minus_two, ring, -1)
    low, high = send(two[: ring // 2], ring, 2), send(minus_two[ring // 2 :], ring, -2)
    early_taps, late_taps = (taps, one, two, minus_two, minus_one), (three, low, high, minus_three)
    pair_rows = lax.all_to_all(
        ordered.reshape(owners, 8, 2 * width), "dp", split_axis=0, concat_axis=0, tiled=True
    )

    reach = total + GAP + 16
    length = reach + 2 * half - STEP
    group = width // 2
    scalars = (owner, pack_order, utt_len)
    shifted, packed = pl.pallas_call(
        functools.partial(place_kernel, total, half),
        out_shape=[
            jax.ShapeDtypeStruct((2, length, 768), jnp.bfloat16),
            jax.ShapeDtypeStruct((2, total, group), jnp.float32),
        ],
        in_specs=[SMEM, SMEM, SMEM, VMEM],
        out_specs=[VMEM] * 2,
        scratch_shapes=[pltpu.VMEM((2, length + STEP, group), jnp.float32)],
        compiler_params=params,
    )(*scalars, pair_rows.reshape(owners * 8, 2 * width))
    early, late = (0, 1, 2, 6, 7), (3, 4, 5)
    begun = pl.pallas_call(
        functools.partial(near_kernel, ring, early),
        out_shape=jax.ShapeDtypeStruct((reach, 256), jnp.float32),
        in_specs=[SMEM] + [VMEM] * 6,
        out_specs=VMEM,
        compiler_params=params,
    )(owner, shifted, *early_taps)

    def convolve(swap, distances, *taps):
        return pl.pallas_call(
            functools.partial(positional_kernel, swap, ring, distances),
            out_shape=jax.ShapeDtypeStruct((group if swap else width, total), jnp.bfloat16),
            in_specs=[SMEM, SMEM, SMEM, VMEM, VMEM] + [VMEM] * len(taps),
            out_specs=ANY,
            scratch_shapes=[
                pltpu.VMEM((reach, 256), jnp.float32),
                pltpu.VMEM((group, total), jnp.bfloat16),
                pltpu.SemaphoreType.DMA,
            ],
            compiler_params=params,
        )(*scalars, shifted, packed, *taps)

    other = convolve(True, late, begun, *late_taps)
    packed, other = lax.optimization_barrier((packed, other))
    received = lax.ppermute(other, "dp", [(o, o ^ 1) for o in range(owners)])
    own = convolve(False, early + late, *early_taps, *late_taps)
    hidden = pl.pallas_call(
        join_kernel,
        out_shape=jax.ShapeDtypeStruct((width, total), jnp.bfloat16),
        in_specs=[SMEM, ANY, ANY],
        out_specs=ANY,
        scratch_shapes=[pltpu.SemaphoreType.DMA],
        input_output_aliases={2: 0},
        compiler_params=params,
    )(owner, received, own)
    return hidden.T


def solution(mesh):
    in_specs = (P("mp", "dp", None), P(), P(), P("dp", "mp", None, None), P(), P())
    out_specs = P("dp", "mp")
    return jax.shard_map(shards, mesh=mesh, in_specs=in_specs, out_specs=out_specs, check_vma=False)
```

```python
import functools

import jax
import jax.numpy as jnp
from jax import lax
from jax.experimental import pallas as pl
from jax.experimental.pallas import tpu as pltpu
from jax.sharding import PartitionSpec as P

HOP = 320
EPS = 1e-05
LANES = 128
TAP_ROWS = 104
GAP = 64
STEP = 16


def iota(shape, dim):
    return lax.broadcasted_iota(jnp.int32, shape, dim)


def one_hot(condition):
    return jnp.where(condition, 1.0, 0.0).astype(jnp.bfloat16)


def dot(a, b, contract=((1,), (0,))):
    return lax.dot_general(a, b, (contract, ((), ())), preferred_element_type=jnp.float32)


def layer_norm(values):
    average = jnp.mean(values, axis=-1, keepdims=True)
    centred = values - average
    variance = jnp.mean(centred * centred, axis=-1, keepdims=True)
    return centred * lax.rsqrt(variance + EPS)


def gelu(values):
    return 0.5 * values * (1.0 + lax.erf(values * (0.5**0.5)))


def pack_taps_kernel(taps_ref, out_ref):
    packed = []
    for g in range(2):
        first, second = taps_ref[0, g].astype(jnp.float32), taps_ref[1, g].astype(jnp.float32)
        rest = second[:, 48:80]
        blocks = [rest[8 * r : 8 * r + 8] for r in range(10)] + [jnp.zeros((8, 32), jnp.float32)] * 2
        folded = [jnp.concatenate(blocks[4 * n : 4 * n + 4], axis=1) for n in range(3)]
        wide = jnp.concatenate([first, second[:, 0:48]], axis=1)
        packed.append(jnp.concatenate([wide] + folded, axis=0).astype(out_ref.dtype))
    for device in range(out_ref.shape[0]):
        out_ref[device] = packed[device % 2]


def front_kernel(utts, frames, parts, features_hbm, conv_hbm, proj_hbm, out_ref, features_ref, conv_ref, proj_ref, sems):
    copies = [
        pltpu.make_async_copy(source, target, sems.at[n])
        for n, (source, target) in enumerate(
            [(features_hbm, features_ref), (conv_hbm, conv_ref), (proj_hbm, proj_ref)]
        )
    ]
    for copy in copies:
        copy.start()
    rows = utts * frames
    copies[0].wait()
    features = features_ref[...]
    row = iota((rows, 2 * rows), 0)
    column = iota((rows, 2 * rows), 1)
    source = (row % utts) * (2 * frames) + 2 * (row // utts)
    first = dot(one_hot(column == source), features).astype(jnp.bfloat16)
    second = dot(one_hot(column == source + 1), features).astype(jnp.bfloat16)
    copies[1].wait()
    conv_out = dot(first, conv_ref[0]) + dot(second, conv_ref[1])
    hidden = gelu(layer_norm(conv_out)).astype(jnp.bfloat16)
    normed = layer_norm(hidden.astype(jnp.float32)).astype(jnp.bfloat16)
    copies[2].wait()
    projected = dot(normed, proj_ref[...]).astype(jnp.bfloat16)
    group = projected.shape[1] // (2 * parts)
    for part in range(parts):
        pieces = [
            projected[f * utts : (f + 1) * utts, (2 * part + g) * group : (2 * part + g + 1) * group]
            for g in range(2)
            for f in range(frames)
        ]
        out_ref[part] = jnp.concatenate(pieces, axis=1)


def order_kernel(order_ref, spread_ref, out_ref):
    utts, lanes = spread_ref.shape
    rows, width = out_ref.shape
    width //= 2
    chosen = one_hot(iota((utts, utts), 0) == order_ref[...])
    ordered = dot(chosen, spread_ref[...], ((0,), (0,))).astype(jnp.bfloat16)
    row = iota((rows, utts), 0)
    eighth = (row // 8) % 2 * 4 + row % 4
    slot = row // 16 * 4 + row // 4 % 2
    for which in range(2):
        same = slot + 2 * which == iota((rows, utts), 1)
        total = None
        for e in range(0, lanes // width, 2):
            left = jnp.concatenate([one_hot(same & (eighth == e + n)) for n in range(2)], axis=1)
            right = [ordered[:, (e + n) * width : (e + n + 1) * width] for n in range(2)]
            term = dot(left, jnp.concatenate(right, axis=0))
            total = term if total is None else total + term
        out_ref[:, which * width : (which + 1) * width] = total.astype(out_ref.dtype)


def pair_lengths(owner_ref, order_ref, len_ref):
    slot = owner_ref[0] // 2 * 4
    return [[len_ref[order_ref[slot + 2 * which + n]] // HOP for n in range(2)] for which in range(2)]


def place_kernel(total, half, owner_ref, order_ref, len_ref, rows_ref, shifted_ref, packed_ref, placed):
    lengths = pair_lengths(owner_ref, order_ref, len_ref)
    _, spots, group = placed.shape
    columns = rows_ref.shape[0]
    column = iota((1, columns), 1)
    is_first = (column // 4) % 2 == 0
    spot = iota((spots, columns), 0)
    for which in range(2):
        first_len, second_len = lengths[which]
        acc = None
        for odd in range(2):
            frame = (column // 8) * 8 + (column % 4) * 2 + odd
            target = jnp.where(is_first, frame, frame + first_len + GAP) + half
            valid = frame < jnp.where(is_first, first_len, second_len)
            target = jnp.where(valid, target, -1)
            lane = (2 * which + odd) * group
            term = dot(one_hot(spot == target), rows_ref[:, lane : lane + group])
            acc = term if acc is None else acc + term
        placed[which] = acc

    length = shifted_ref.shape[1]
    for which in range(2):
        for third in range(3):
            pairs = [k for k in range(3 * third, 3 * third + 3) if k < 8]
            pieces = [placed[which, 2 * k : 2 * k + length, :].astype(jnp.bfloat16) for k in pairs]
            pieces.append(jnp.zeros((length, 256 - group * len(pairs)), jnp.bfloat16))
            shifted_ref[which, :, third * 256 : (third + 1) * 256] = jnp.concatenate(pieces, axis=1)
        packed_ref[which] = jnp.where(
            iota((total, 1), 0) < lengths[which][0],
            placed[which, half : half + total, :],
            placed[which, half + GAP : half + GAP + total, :],
        )


def add_blocks(which, ring, distances, owner_ref, shifted_ref, refs, before, sums):
    refs = list(refs)
    for away in distances:
        count = 2 if away == ring // 2 else 1
        pieces = [(ref, n) for ref in refs[:count] for n in range(ring // count)]
        refs = refs[count:]
        start = pl.multiple_of(lax.rem(owner_ref[0] // ring + ring - away, ring) * STEP, STEP)
        left, right = [], []
        for slot in range(9):
            taps_ref, piece = pieces[min(slot, 7)]
            size = 96 if slot % 3 == 2 else 80
            left.append(taps_ref[piece, 0:size, :])
            fold = taps_ref[piece, 80:104, :].astype(jnp.float32)
            turned = [fold] + [jnp.roll(fold, -32 * r, axis=1) for r in range(1, 4)]
            right += [turned[r % 4][r // 4 * 8 : r // 4 * 8 + 8] for r in range(10)]
            if size == 96:
                right += [fold[0:16]]
        right = jnp.concatenate(right, axis=0).astype(jnp.bfloat16)
        matrix = jnp.concatenate([jnp.concatenate(left, axis=0), right], axis=1)
        term = dot(shifted_ref[which, pl.ds(start, sums.shape[0]), :], matrix)
        sums[...] = term if before is None else before[...] + term
        before = sums


def near_kernel(ring, distances, owner_ref, shifted_ref, *refs):
    add_blocks(1 - owner_ref[0] % 2, ring, distances, owner_ref, shifted_ref, refs[:-1], None, refs[-1])


def positional_kernel(swap, ring, distances, owner_ref, order_ref, len_ref, shifted_ref, packed_ref, *refs):
    taps_refs, (out_ref, sums, result, sem) = refs[:-4], refs[-4:]
    parity = owner_ref[0] % 2
    which = 1 - parity if swap else parity
    before, taps_refs = (taps_refs[0], taps_refs[1:]) if swap else (None, taps_refs)
    slot = 2 * (owner_ref[0] - parity + which)
    first_len = len_ref[order_ref[slot]] // HOP
    second_len = len_ref[order_ref[slot + 1]] // HOP
    _, total, group = packed_ref.shape
    add_blocks(which, ring, distances, owner_ref, shifted_ref, taps_refs, before, sums)

    spot = iota((total, 1), 0)
    near = sums[0:total, 0:group] + sums[1 : total + 1, group : 2 * group]
    far = sums[GAP : GAP + total, 0:group] + sums[GAP + 1 : GAP + total + 1, group : 2 * group]
    conv_sum = jnp.where(spot < first_len + second_len, jnp.where(spot < first_len, near, far), 0.0)
    hidden = packed_ref[which] + gelu(conv_sum)
    hidden = jnp.concatenate([hidden, jnp.zeros((total, -group % LANES), jnp.float32)], axis=1)
    result[...] = hidden.T[:group].astype(result.dtype)
    start = 0 if swap else pl.multiple_of(parity * group, 16)
    copy = pltpu.make_async_copy(result, out_ref.at[pl.ds(start, group), :], sem)
    copy.start()
    copy.wait()


def join_kernel(owner_ref, received_hbm, own_hbm, out_hbm, sem):
    group = received_hbm.shape[0]
    start = pl.multiple_of((1 - owner_ref[0] % 2) * group, 16)
    copy = pltpu.make_async_copy(received_hbm, out_hbm.at[pl.ds(start, group), :], sem)
    copy.start()
    copy.wait()


VMEM = pl.BlockSpec(memory_space=pltpu.VMEM)
SMEM = pl.BlockSpec(memory_space=pltpu.SMEM)
ANY = pl.BlockSpec(memory_space=pl.ANY)


def send(values, ring, step):
    return lax.ppermute(values, "dp", [(o, (o + step * ring) % (ring * ring)) for o in range(ring * ring)])


def shards(features, conv_weight, proj_weight, pos_weight, utt_len, pack_order):
    owners = lax.axis_size("dp")
    parts = lax.axis_size("mp")
    utts, slice_rows, channels = features.shape
    frames = slice_rows // 2
    model_width = proj_weight.shape[1]
    width = model_width // parts
    total = frames * owners
    half = pos_weight.shape[0] * owners // 2
    params = pltpu.CompilerParams(vmem_limit_bytes=48 * 1024 * 1024)
    large = pltpu.CompilerParams(vmem_limit_bytes=62 * 1024 * 1024)

    owner = lax.axis_index("dp").reshape(1)
    ring = round(owners**0.5)
    along_z = [[y * ring + z for z in range(ring)] for y in range(ring)]
    tap_copies = pl.pallas_call(
        pack_taps_kernel,
        out_shape=jax.ShapeDtypeStruct((ring, TAP_ROWS, LANES), jnp.bfloat16),
        in_specs=[VMEM],
        out_specs=VMEM,
        compiler_params=params,
    )(pos_weight)
    taps = lax.all_to_all(tap_copies, "dp", 0, 0, axis_index_groups=along_z, tiled=True)

    sent = pl.pallas_call(
        functools.partial(front_kernel, utts, frames, parts),
        out_shape=jax.ShapeDtypeStruct((parts, utts, frames * width), jnp.bfloat16),
        in_specs=[ANY] * 3,
        out_specs=VMEM,
        scratch_shapes=[
            pltpu.VMEM((utts * slice_rows, channels), jnp.bfloat16),
            pltpu.VMEM(conv_weight.shape, jnp.bfloat16),
            pltpu.VMEM(proj_weight.shape, jnp.bfloat16),
            pltpu.SemaphoreType.DMA((3,)),
        ],
        compiler_params=pltpu.CompilerParams(vmem_limit_bytes=66900000),
    )(features.reshape(utts * slice_rows, channels), conv_weight, proj_weight)
    taps, sent = lax.optimization_barrier((taps, sent))
    two, minus_two, one, minus_one = [send(taps, ring, step) for step in (2, -2, 1, -1)]
    spread = lax.all_to_all(sent, "mp", split_axis=0, concat_axis=0, tiled=True)

    ordered = pl.pallas_call(
        order_kernel,
        out_shape=jax.ShapeDtypeStruct((owners * 8, 2 * width), jnp.bfloat16),
        in_specs=[VMEM] * 2,
        out_specs=VMEM,
        compiler_params=params,
    )(pack_order.reshape(1, -1), spread.reshape(parts * utts, frames * width))
    low, high = two[: ring // 2], minus_two[ring // 2 :]
    low, high, two, minus_two, one, minus_one, ordered = lax.optimization_barrier(
        (low, high, two, minus_two, one, minus_one, ordered)
    )
    low, high = send(low, ring, 2), send(high, ring, -2)
    three, minus_three = send(two, ring, 1), send(minus_two, ring, -1)
    early_taps, late_taps = (taps, one, two, minus_two, minus_one), (three, low, high, minus_three)
    pair_rows = lax.all_to_all(
        ordered.reshape(owners, 8, 2 * width), "dp", split_axis=0, concat_axis=0, tiled=True
    )

    reach = total + GAP + 16
    length = reach + 2 * half - STEP
    group = width // 2
    scalars = (owner, pack_order, utt_len)
    shifted, packed = pl.pallas_call(
        functools.partial(place_kernel, total, half),
        out_shape=[
            jax.ShapeDtypeStruct((2, length, 768), jnp.bfloat16),
            jax.ShapeDtypeStruct((2, total, group), jnp.float32),
        ],
        in_specs=[SMEM, SMEM, SMEM, VMEM],
        out_specs=[VMEM] * 2,
        scratch_shapes=[pltpu.VMEM((2, length + STEP, group), jnp.float32)],
        compiler_params=params,
    )(*scalars, pair_rows.reshape(owners * 8, 2 * width))
    early, late = (0, 1, 2, 6, 7), (3, 4, 5)
    begun = pl.pallas_call(
        functools.partial(near_kernel, ring, early),
        out_shape=jax.ShapeDtypeStruct((reach, 256), jnp.float32),
        in_specs=[SMEM] + [VMEM] * 6,
        out_specs=VMEM,
        compiler_params=params,
    )(owner, shifted, *early_taps)

    def convolve(swap, distances, *taps):
        return pl.pallas_call(
            functools.partial(positional_kernel, swap, ring, distances),
            out_shape=jax.ShapeDtypeStruct((group if swap else width, total), jnp.bfloat16),
            in_specs=[SMEM, SMEM, SMEM, VMEM, VMEM] + [VMEM] * len(taps),
            out_specs=ANY,
            scratch_shapes=[
                pltpu.VMEM((reach, 256), jnp.float32),
                pltpu.VMEM((group, total), jnp.bfloat16),
                pltpu.SemaphoreType.DMA,
            ],
            compiler_params=params,
        )(*scalars, shifted, packed, *taps)

    other = convolve(True, late, begun, *late_taps)
    packed, other = lax.optimization_barrier((packed, other))
    received = lax.ppermute(other, "dp", [(o, o ^ 1) for o in range(owners)])
    own = convolve(False, early + late, *early_taps, *late_taps)
    hidden = pl.pallas_call(
        join_kernel,
        out_shape=jax.ShapeDtypeStruct((width, total), jnp.bfloat16),
        in_specs=[SMEM, ANY, ANY],
        out_specs=ANY,
        scratch_shapes=[pltpu.SemaphoreType.DMA],
        input_output_aliases={2: 0},
        compiler_params=params,
    )(owner, received, own)
    return hidden.T


def solution(mesh):
    in_specs = (P("mp", "dp", None), P(), P(), P("dp", "mp", None, None), P(), P())
    out_specs = P("dp", "mp")
    return jax.shard_map(shards, mesh=mesh, in_specs=in_specs, out_specs=out_specs, check_vma=False)
```

```python
import functools

import jax
import jax.numpy as jnp
from jax import lax
from jax.experimental import pallas as pl
from jax.experimental.pallas import tpu as pltpu
from jax.sharding import PartitionSpec as P

HOP = 320
EPS = 1e-05
LANES = 128
TAP_ROWS = 104
GAP = 64
STEP = 16


def iota(shape, dim):
    return lax.broadcasted_iota(jnp.int32, shape, dim)


def one_hot(condition):
    return jnp.where(condition, 1.0, 0.0).astype(jnp.bfloat16)


def dot(a, b, contract=((1,), (0,))):
    return lax.dot_general(a, b, (contract, ((), ())), preferred_element_type=jnp.float32)


def layer_norm(values):
    average = jnp.mean(values, axis=-1, keepdims=True)
    centred = values - average
    variance = jnp.mean(centred * centred, axis=-1, keepdims=True)
    return centred * lax.rsqrt(variance + EPS)


def gelu(values):
    return 0.5 * values * (1.0 + lax.erf(values * (0.5**0.5)))


def pack_taps_kernel(taps_ref, out_ref):
    packed = []
    for g in range(2):
        first, second = taps_ref[0, g].astype(jnp.float32), taps_ref[1, g].astype(jnp.float32)
        rest = second[:, 48:80]
        blocks = [rest[8 * r : 8 * r + 8] for r in range(10)] + [jnp.zeros((8, 32), jnp.float32)] * 2
        folded = [jnp.concatenate(blocks[4 * n : 4 * n + 4], axis=1) for n in range(3)]
        wide = jnp.concatenate([first, second[:, 0:48]], axis=1)
        packed.append(jnp.concatenate([wide] + folded, axis=0).astype(out_ref.dtype))
    for device in range(out_ref.shape[0]):
        out_ref[device] = packed[device % 2]


def front_kernel(utts, frames, parts, features_hbm, conv_hbm, proj_hbm, out_ref, features_ref, conv_ref, proj_ref, sems):
    copies = [
        pltpu.make_async_copy(source, target, sems.at[n])
        for n, (source, target) in enumerate(
            [(features_hbm, features_ref), (conv_hbm, conv_ref), (proj_hbm, proj_ref)]
        )
    ]
    for copy in copies:
        copy.start()
    rows = utts * frames
    copies[0].wait()
    features = features_ref[...]
    row = iota((rows, 2 * rows), 0)
    column = iota((rows, 2 * rows), 1)
    source = (row % utts) * (2 * frames) + 2 * (row // utts)
    first = dot(one_hot(column == source), features).astype(jnp.bfloat16)
    second = dot(one_hot(column == source + 1), features).astype(jnp.bfloat16)
    copies[1].wait()
    conv_out = dot(first, conv_ref[0]) + dot(second, conv_ref[1])
    hidden = gelu(layer_norm(conv_out)).astype(jnp.bfloat16)
    normed = layer_norm(hidden.astype(jnp.float32)).astype(jnp.bfloat16)
    copies[2].wait()
    projected = dot(normed, proj_ref[...]).astype(jnp.bfloat16)
    group = projected.shape[1] // (2 * parts)
    for part in range(parts):
        pieces = [
            projected[f * utts : (f + 1) * utts, (2 * part + g) * group : (2 * part + g + 1) * group]
            for g in range(2)
            for f in range(frames)
        ]
        out_ref[part] = jnp.concatenate(pieces, axis=1)


def order_kernel(order_ref, spread_ref, out_ref):
    utts, lanes = spread_ref.shape
    rows, width = out_ref.shape
    width //= 2
    chosen = one_hot(iota((utts, utts), 0) == order_ref[...])
    ordered = dot(chosen, spread_ref[...], ((0,), (0,))).astype(jnp.bfloat16)
    row = iota((rows, utts), 0)
    eighth = (row // 8) % 2 * 4 + row % 4
    slot = row // 16 * 4 + row // 4 % 2
    for which in range(2):
        same = slot + 2 * which == iota((rows, utts), 1)
        total = None
        for e in range(0, lanes // width, 2):
            left = jnp.concatenate([one_hot(same & (eighth == e + n)) for n in range(2)], axis=1)
            right = [ordered[:, (e + n) * width : (e + n + 1) * width] for n in range(2)]
            term = dot(left, jnp.concatenate(right, axis=0))
            total = term if total is None else total + term
        out_ref[:, which * width : (which + 1) * width] = total.astype(out_ref.dtype)


def pair_lengths(owner_ref, order_ref, len_ref):
    slot = owner_ref[0] // 2 * 4
    return [[len_ref[order_ref[slot + 2 * which + n]] // HOP for n in range(2)] for which in range(2)]


def place_kernel(total, half, owner_ref, order_ref, len_ref, rows_ref, shifted_ref, packed_ref, placed):
    lengths = pair_lengths(owner_ref, order_ref, len_ref)
    _, spots, group = placed.shape
    columns = rows_ref.shape[0]
    column = iota((1, columns), 1)
    is_first = (column // 4) % 2 == 0
    spot = iota((spots, columns), 0)
    for which in range(2):
        first_len, second_len = lengths[which]
        acc = None
        for odd in range(2):
            frame = (column // 8) * 8 + (column % 4) * 2 + odd
            target = jnp.where(is_first, frame, frame + first_len + GAP) + half
            valid = frame < jnp.where(is_first, first_len, second_len)
            target = jnp.where(valid, target, -1)
            lane = (2 * which + odd) * group
            term = dot(one_hot(spot == target), rows_ref[:, lane : lane + group])
            acc = term if acc is None else acc + term
        placed[which] = acc

    length = shifted_ref.shape[1]
    for which in range(2):
        for third in range(3):
            pairs = [k for k in range(3 * third, 3 * third + 3) if k < 8]
            pieces = [placed[which, 2 * k : 2 * k + length, :].astype(jnp.bfloat16) for k in pairs]
            pieces.append(jnp.zeros((length, 256 - group * len(pairs)), jnp.bfloat16))
            shifted_ref[which, :, third * 256 : (third + 1) * 256] = jnp.concatenate(pieces, axis=1)
        packed_ref[which] = jnp.where(
            iota((total, 1), 0) < lengths[which][0],
            placed[which, half : half + total, :],
            placed[which, half + GAP : half + GAP + total, :],
        )


def add_blocks(which, ring, distances, owner_ref, shifted_ref, refs, before, sums):
    refs = list(refs)
    for away in distances:
        count = 2 if away == ring // 2 else 1
        pieces = [(ref, n) for ref in refs[:count] for n in range(ring // count)]
        refs = refs[count:]
        start = pl.multiple_of(lax.rem(owner_ref[0] // ring + ring - away, ring) * STEP, STEP)
        left, right = [], []
        for slot in range(9):
            taps_ref, piece = pieces[min(slot, 7)]
            size = 96 if slot % 3 == 2 else 80
            left.append(taps_ref[piece, 0:size, :])
            fold = taps_ref[piece, 80:104, :].astype(jnp.float32)
            turned = [fold] + [jnp.roll(fold, -32 * r, axis=1) for r in range(1, 4)]
            right += [turned[r % 4][r // 4 * 8 : r // 4 * 8 + 8] for r in range(10)]
            if size == 96:
                right += [fold[0:16]]
        right = jnp.concatenate(right, axis=0).astype(jnp.bfloat16)
        matrix = jnp.concatenate([jnp.concatenate(left, axis=0), right], axis=1)
        term = dot(shifted_ref[which, pl.ds(start, sums.shape[0]), :], matrix)
        sums[...] = term if before is None else before[...] + term
        before = sums


def near_kernel(ring, distances, owner_ref, shifted_ref, *refs):
    add_blocks(1 - owner_ref[0] % 2, ring, distances, owner_ref, shifted_ref, refs[:-1], None, refs[-1])


def positional_kernel(swap, ring, distances, owner_ref, order_ref, len_ref, shifted_ref, packed_ref, *refs):
    taps_refs, (out_ref, sums, result, sem) = refs[:-4], refs[-4:]
    parity = owner_ref[0] % 2
    which = 1 - parity if swap else parity
    before, taps_refs = (taps_refs[0], taps_refs[1:]) if swap else (None, taps_refs)
    slot = 2 * (owner_ref[0] - parity + which)
    first_len = len_ref[order_ref[slot]] // HOP
    second_len = len_ref[order_ref[slot + 1]] // HOP
    _, total, group = packed_ref.shape
    add_blocks(which, ring, distances, owner_ref, shifted_ref, taps_refs, before, sums)

    spot = iota((total, 1), 0)
    near = sums[0:total, 0:group] + sums[1 : total + 1, group : 2 * group]
    far = sums[GAP : GAP + total, 0:group] + sums[GAP + 1 : GAP + total + 1, group : 2 * group]
    conv_sum = jnp.where(spot < first_len + second_len, jnp.where(spot < first_len, near, far), 0.0)
    hidden = packed_ref[which] + gelu(conv_sum)
    hidden = jnp.concatenate([hidden, jnp.zeros((total, -group % LANES), jnp.float32)], axis=1)
    result[...] = hidden.T[:group].astype(result.dtype)
    start = 0 if swap else pl.multiple_of(parity * group, 16)
    copy = pltpu.make_async_copy(result, out_ref.at[pl.ds(start, group), :], sem)
    copy.start()
    copy.wait()


def join_kernel(owner_ref, received_hbm, own_hbm, out_hbm, sem):
    group = received_hbm.shape[0]
    start = pl.multiple_of((1 - owner_ref[0] % 2) * group, 16)
    copy = pltpu.make_async_copy(received_hbm, out_hbm.at[pl.ds(start, group), :], sem)
    copy.start()
    copy.wait()


VMEM = pl.BlockSpec(memory_space=pltpu.VMEM)
SMEM = pl.BlockSpec(memory_space=pltpu.SMEM)
ANY = pl.BlockSpec(memory_space=pl.ANY)


def send(values, ring, step):
    return lax.ppermute(values, "dp", [(o, (o + step * ring) % (ring * ring)) for o in range(ring * ring)])


def shards(features, conv_weight, proj_weight, pos_weight, utt_len, pack_order):
    owners = lax.axis_size("dp")
    parts = lax.axis_size("mp")
    utts, slice_rows, channels = features.shape
    frames = slice_rows // 2
    model_width = proj_weight.shape[1]
    width = model_width // parts
    total = frames * owners
    half = pos_weight.shape[0] * owners // 2
    params = pltpu.CompilerParams(vmem_limit_bytes=48 * 1024 * 1024)
    large = pltpu.CompilerParams(vmem_limit_bytes=62 * 1024 * 1024)

    owner = lax.axis_index("dp").reshape(1)
    ring = round(owners**0.5)
    along_z = [[y * ring + z for z in range(ring)] for y in range(ring)]
    tap_copies = pl.pallas_call(
        pack_taps_kernel,
        out_shape=jax.ShapeDtypeStruct((ring, TAP_ROWS, LANES), jnp.bfloat16),
        in_specs=[VMEM],
        out_specs=VMEM,
        compiler_params=params,
    )(pos_weight)
    taps = lax.all_to_all(tap_copies, "dp", 0, 0, axis_index_groups=along_z, tiled=True)

    sent = pl.pallas_call(
        functools.partial(front_kernel, utts, frames, parts),
        out_shape=jax.ShapeDtypeStruct((parts, utts, frames * width), jnp.bfloat16),
        in_specs=[ANY] * 3,
        out_specs=VMEM,
        scratch_shapes=[
            pltpu.VMEM((utts * slice_rows, channels), jnp.bfloat16),
            pltpu.VMEM(conv_weight.shape, jnp.bfloat16),
            pltpu.VMEM(proj_weight.shape, jnp.bfloat16),
            pltpu.SemaphoreType.DMA((3,)),
        ],
        compiler_params=params,
    )(features.reshape(utts * slice_rows, channels), conv_weight, proj_weight)
    taps, sent = lax.optimization_barrier((taps, sent))
    two, minus_two, one, minus_one = [send(taps, ring, step) for step in (2, -2, 1, -1)]
    spread = lax.all_to_all(sent, "mp", split_axis=0, concat_axis=0, tiled=True)

    ordered = pl.pallas_call(
        order_kernel,
        out_shape=jax.ShapeDtypeStruct((owners * 8, 2 * width), jnp.bfloat16),
        in_specs=[VMEM] * 2,
        out_specs=VMEM,
        compiler_params=params,
    )(pack_order.reshape(1, -1), spread.reshape(parts * utts, frames * width))
    one, minus_one, two, minus_two, ordered = lax.optimization_barrier((one, minus_one, two, minus_two, ordered))
    three, minus_three = send(two, ring, 1), send(minus_two, ring, -1)
    low, high = send(two[: ring // 2], ring, 2), send(minus_two[ring // 2 :], ring, -2)
    early_taps, late_taps = (taps, one, two, minus_two, minus_one), (three, low, high, minus_three)
    pair_rows = lax.all_to_all(
        ordered.reshape(owners, 8, 2 * width), "dp", split_axis=0, concat_axis=0, tiled=True
    )

    reach = total + GAP + 16
    length = reach + 2 * half - STEP
    group = width // 2
    scalars = (owner, pack_order, utt_len)
    shifted, packed = pl.pallas_call(
        functools.partial(place_kernel, total, half),
        out_shape=[
            jax.ShapeDtypeStruct((2, length, 768), jnp.bfloat16),
            jax.ShapeDtypeStruct((2, total, group), jnp.float32),
        ],
        in_specs=[SMEM, SMEM, SMEM, VMEM],
        out_specs=[VMEM] * 2,
        scratch_shapes=[pltpu.VMEM((2, length + STEP, group), jnp.float32)],
        compiler_params=params,
    )(*scalars, pair_rows.reshape(owners * 8, 2 * width))
    early, late = (0, 1, 2, 6, 7), (3, 4, 5)
    begun = pl.pallas_call(
        functools.partial(near_kernel, ring, early),
        out_shape=jax.ShapeDtypeStruct((reach, 256), jnp.float32),
        in_specs=[SMEM] + [VMEM] * 6,
        out_specs=VMEM,
        compiler_params=params,
    )(owner, shifted, *early_taps)

    def convolve(swap, distances, *taps):
        return pl.pallas_call(
            functools.partial(positional_kernel, swap, ring, distances),
            out_shape=jax.ShapeDtypeStruct((group if swap else width, total), jnp.bfloat16),
            in_specs=[SMEM, SMEM, SMEM, VMEM, VMEM] + [VMEM] * len(taps),
            out_specs=ANY,
            scratch_shapes=[
                pltpu.VMEM((reach, 256), jnp.float32),
                pltpu.VMEM((group, total), jnp.bfloat16),
                pltpu.SemaphoreType.DMA,
            ],
            compiler_params=params,
        )(*scalars, shifted, packed, *taps)

    other = convolve(True, late, begun, *late_taps)
    packed, other = lax.optimization_barrier((packed, other))
    received = lax.ppermute(other, "dp", [(o, o ^ 1) for o in range(owners)])
    own = convolve(False, early + late, *early_taps, *late_taps)
    hidden = pl.pallas_call(
        join_kernel,
        out_shape=jax.ShapeDtypeStruct((width, total), jnp.bfloat16),
        in_specs=[SMEM, ANY, ANY],
        out_specs=ANY,
        scratch_shapes=[pltpu.SemaphoreType.DMA],
        input_output_aliases={2: 0},
        compiler_params=params,
    )(owner, received, own)
    return hidden.T


def solution(mesh):
    in_specs = (P("mp", "dp", None), P(), P(), P("dp", "mp", None, None), P(), P())
    out_specs = P("dp", "mp")
    return jax.shard_map(shards, mesh=mesh, in_specs=in_specs, out_specs=out_specs, check_vma=False)
```
